256 devices in a mesh: px: 32 (over y, z_lo, core), py: 8 (over x, z_hi).
Axes of the slice: x: 4, y: 4, z: 8 (z_hi: 2, z_lo: 4; z = z_hi * 4 + z_lo), core: 2. Of those that a mesh axis runs over, the one named last changes fastest.
Arguments:
- features: bfloat16 [32, 128, 256, 256], P(None, 'py', 'px'), may hold values from -6 to 6
- cotangent: bfloat16 [32, 128, 256, 256], P(None, 'py', 'px'), may hold values from -6 to 6
- pointwise_fine: bfloat16 [32, 32], replicated, may hold values from -1 to 1
- spectral_fine: float32 [2, 32, 32, 16, 32, 32], P(None, None, None, None, 'px', 'py'), may hold values from -16 to 16
- lift_weight: bfloat16 [32, 64], replicated, may hold values from -8 to 8
- pointwise_coarse: bfloat16 [64, 64], replicated, may hold values from -0.75 to 0.75
- spectral_coarse: float32 [2, 64, 64, 16, 32, 32], P(None, None, None, None, 'px', 'py'), may hold values from -1.5 to 1.5
- project_weight: bfloat16 [64, 32], replicated, may hold values from -0.75 to 0.75
Outputs:
- layer_out: bfloat16 [32, 128, 256, 256], P(None, 'py', 'px')
- grad_features: bfloat16 [32, 128, 256, 256], P(None, 'py', 'px')
- grad_spectral: float32 [2, 32, 32, 16, 32, 32], P(None, None, None, None, 'px', 'py')
The draws below stay inside these ranges and needn't reach their ends.
All inputs are finite; a program needn't handle non-finite values.
Results may differ from the reference program's by a relative error of at most 0.001.
Values sent between devices are 32-bit elements; how exact they have to be, the bound alone decides.
A program may use at most 128 MiB of HBM per device.

```python
import jax
import jax.numpy as jnp
from jax import lax

C = 32
CC = 64
M = 16
NX = 256
NY = 256
NZ = 128


def block_levels(rng, extent, shards, smallest, high):
    def one(position, shards_of):
        steps = jax.random.uniform(jax.random.fold_in(jax.random.fold_in(rng, 6), position), (shards_of,), jnp.float32, smallest / len(shards), high / len(shards))
        return jnp.repeat(jnp.exp(steps), extent[position] // shards_of).reshape((-1,) + (1,) * (len(extent) - position - 1))

    loudness = one(*shards[0])
    for cut in shards[1:]:
        loudness = loudness * one(*cut)
    return loudness


def scatter_about(rng, dims, width, limit, cuts=(), kind=jnp.bfloat16):
    result = jax.random.normal(rng, dims, jnp.float32) * width
    if len(cuts) > 0:
        result = block_levels(rng, dims, cuts, -0.22, 0.18) * result
    return jnp.clip(result, min=-limit, max=limit).astype(kind)


def setup_inputs(seed: int = 0) -> dict:
    key_list = jax.random.split(jax.random.key(seed), 9)
    features = scatter_about(key_list[0], (C, NZ, NY, NX), 1.0, 6.0, ((1, 8), (2, 32)))
    cotangent = scatter_about(key_list[1], (C, NZ, NY, NX), 1.0, 6.0, ((1, 8), (2, 32)))
    pointwise_fine = scatter_about(key_list[2], (C, C), C ** -0.5, 1.0)
    spectral_fine = scatter_about(key_list[3], (2, C, C, M, 2 * M, 2 * M), 2.8, 16.0, ((4, 32), (5, 8)), jnp.float32)
    lift_weight = scatter_about(key_list[4], (C, CC), (8 * C ** -0.5), 8.0)
    pointwise_coarse = scatter_about(key_list[5], (CC, CC), CC ** -0.5, 0.75)
    spectral_coarse = scatter_about(key_list[6], (2, CC, CC, M, 2 * M, 2 * M), 0.25, 1.5, ((4, 32), (5, 8)), jnp.float32)
    project_weight = scatter_about(key_list[7], (CC, C), CC ** -0.5, 0.75)
    return dict(features=features, cotangent=cotangent, pointwise_fine=pointwise_fine, spectral_fine=spectral_fine, lift_weight=lift_weight, pointwise_coarse=pointwise_coarse, spectral_coarse=spectral_coarse, project_weight=project_weight)


def kept(count):
    return jnp.concatenate([jnp.arange(M), count - M + jnp.arange(M)]).astype(jnp.int32)

def spectrum(field):
    rows_y = kept(field.shape[2])
    rows_x = kept(field.shape[3])

    def single(channel):
        full = jnp.fft.rfftn(channel, axes=(2, 1, 0))
        part = full[:M][:, rows_y][:, :, rows_x].transpose(0, 2, 1)
        return jnp.stack([jnp.real(part), jnp.imag(part)])
    return lax.map(single, field)

def synthesis(coeffs, shape):
    size_z, size_y, size_x = shape
    rows_y = kept(size_y)
    rows_x = kept(size_x)

    def single(part):
        values = lax.complex(part[0], part[1]).transpose(0, 2, 1)
        full = jnp.zeros((size_z // 2 + 1, size_y, size_x), values.dtype)
        full = full.at[:M, rows_y[:, None], rows_x[None, :]].set(values)
        return jnp.fft.irfftn(full, s=(size_x, size_y, size_z), axes=(2, 1, 0))
    return lax.map(single, coeffs)

def product(weight, values):
    return jnp.einsum('iozab,izab->ozab', weight, values, precision=lax.Precision.HIGHEST)

def mix(weight, coeffs):
    real_part = product(weight[0], coeffs[:, 0]) - product(weight[1], coeffs[:, 1])
    imag_part = product(weight[0], coeffs[:, 1]) + product(weight[1], coeffs[:, 0])
    return jnp.stack([real_part, imag_part], axis=1)

def channel_map(weight, values):
    return jnp.einsum('io,izyx->ozyx', weight.astype(jnp.float32), values, precision=lax.Precision.HIGHEST)

def reference(features, cotangent, pointwise_fine, spectral_fine, lift_weight, pointwise_coarse, spectral_coarse, project_weight):
    field = features.astype(jnp.float32)
    shape = field.shape[1:]

    def fine(values, spectral):
        local = channel_map(pointwise_fine, values)
        return jax.nn.gelu(local + synthesis(mix(spectral, spectrum(values)), shape))
    activated, pullback = jax.vjp(fine, field, spectral_fine)
    restricted = field.reshape(C, NZ // 4, 4, NY // 4, 4, NX // 4, 4).mean(axis=(2, 4, 6))
    lifted = channel_map(lift_weight, restricted)
    coarse_pre = channel_map(pointwise_coarse, lifted) + synthesis(mix(spectral_coarse, spectrum(lifted)), lifted.shape[1:])
    coarse_out = channel_map(project_weight, jax.nn.gelu(coarse_pre))
    prolonged = jnp.broadcast_to(coarse_out[:, :, None, :, None, :, None], (C, NZ // 4, 4, NY // 4, 4, NX // 4, 4)).reshape(C, NZ, NY, NX)
    layer_out = (activated + prolonged).astype(jnp.bfloat16)
    grad_field, grad_spectral = pullback(cotangent.astype(jnp.float32))
    return (layer_out, grad_field.astype(jnp.bfloat16), grad_spectral)
```

```python
import functools
import math

import jax
import jax.numpy as jnp
import numpy as np
from jax import lax
from jax.experimental import pallas as pl
from jax.experimental.pallas import tpu as pltpu
from jax.sharding import PartitionSpec as P

M = 16
F32 = jnp.float32
BF16 = jnp.bfloat16
MESH = pl.DeviceIdType.MESH
NPX, NPY = 32, 8
PAIRS = 320
ROOT = math.sqrt(2.0 / math.pi)


def single(table):
    return np.asarray(table, np.float64).astype(np.float32)


def signed(index):
    return np.where(index < M, index, index - 2 * M)


def turn(freq, cell, count):
    return (np.asarray(freq) * np.asarray(cell) % count) * (2.0 * np.pi / count)


@functools.cache
def tables():
    out = {}
    x = np.arange(256)
    rows = np.zeros((40, 256))
    for j in range(17):
        angle = turn(j, x, 256)
        if j == 0:
            rows[0] = rows[1] = 1.0
        else:
            rows[2 * j] = np.cos(angle)
            rows[2 * j + 1] = -np.sin(angle) if j < 16 else np.sin(angle)
    out["tx"] = single(rows)
    inv = rows.copy()
    inv[1] = 0.0
    out["ix"] = single(inv)

    ky = np.arange(32)
    theta = turn(signed(ky)[:, None], np.arange(256)[None, :], 256)
    cos, sin = np.cos(theta), np.sin(theta)
    zero = np.zeros_like(cos)
    plus = (((cos, sin), (-sin, cos)))
    minus = (((cos, -sin), (-sin, -cos)))
    from0 = (((cos, zero), (-sin, zero)))
    from1 = (((zero, cos), (zero, -sin)))
    none = (((zero, zero), (zero, zero)))
    kinds = [(plus, minus), (minus, plus), (from0, from1), (plus, none), (none, plus)]
    ty = np.zeros((5, 2, 2, 8, 2, 4, 32, 2, 8))
    for k, pair in enumerate(kinds):
        for q in range(2):
            for r1 in range(2):
                for r in range(2):
                    block = pair[q][r1][r].reshape(8, 4, 32, 8)
                    for dup in range(2):
                        ty[k, r1, q, :, dup, :, :, r, :] = block
    ty = ty.reshape(5, 256, 512)
    out["ty"] = single(ty)

    ti = np.zeros((5, 32, 2, 8, 2, 2, 8, 2, 4))

    def add(k, rout, q, part, sign):
        c = cos.T.reshape(32, 8, 8, 4)
        s = sin.T.reshape(32, 8, 8, 4)
        if part == 0:
            coef = {(0, 0): c, (1, 1): -c, (0, 1): -s, (1, 0): -s}
        else:
            coef = {(0, 0): s, (1, 1): -s, (0, 1): c, (1, 0): c}
        for (cs, r), value in coef.items():
            ti[k, :, rout, :, cs, q, :, r, :] += sign * value

    for k, first in ((0, 1.0), (1, -1.0)):
        add(k, 0, 0, 0, 1.0)
        add(k, 0, 1, 0, 1.0)
        add(k, 1, 0, 1, first)
        add(k, 1, 1, 1, -first)
    add(2, 0, 0, 0, 1.0)
    add(2, 1, 1, 0, 1.0)
    for k, q in ((3, 0), (4, 1)):
        add(k, 0, q, 0, 1.0)
        add(k, 1, q, 1, 1.0)
    out["ti"] = single(ti.reshape(5, 512, 256))

    kz = np.arange(16)
    zf = np.zeros((8, 2, 8, 16, 2, 8, 16))
    zi = np.zeros((8, 8, 16, 2, 8, 16))
    for b in range(8):
        phi = turn(kz[None, :], (b * 16 + np.arange(16))[:, None], 128)
        for c in range(8):
            zf[b, 0, c, :, 0, c, :] = np.cos(phi)
            zf[b, 1, c, :, 0, c, :] = np.sin(phi)
            zf[b, 0, c, :, 1, c, :] = -np.sin(phi)
            zf[b, 1, c, :, 1, c, :] = np.cos(phi)
            zi[b, c, :, 0, c, :] = np.cos(phi).T
            zi[b, c, :, 1, c, :] = np.sin(phi).T
    out["zf"] = single(zf.reshape(8, 256, 256))
    out["zi"] = single(zi.reshape(8, 128, 256))

    kx = np.arange(32)
    alpha = turn(signed(kx)[:, None], (x // 4)[None, :], 64)
    txc = np.stack([np.cos(alpha), -np.sin(alpha)], axis=1).reshape(64, 256)
    out["txc"] = single(txc)
    theta = turn(signed(ky)[:, None], np.arange(64)[None, :], 64)
    cos, sin = np.cos(theta), np.sin(theta)
    tyc = np.zeros((2, 8, 2, 4, 32, 2, 4))
    plus = ((cos, sin), (-sin, cos))
    for r1 in range(2):
        for r in range(2):
            for dup in range(2):
                tyc[r1, :, dup, :, :, r, :2] = plus[r1][r].reshape(8, 4, 32, 2)
    out["tyc"] = single(tyc.reshape(128, 256))
    tic = np.zeros((32, 2, 2, 2, 8, 2, 4))
    c = cos.T.reshape(32, 2, 8, 4)
    s = sin.T.reshape(32, 2, 8, 4)
    for (rout, cs, r), value in {
        (0, 0, 0): c, (0, 1, 1): -c, (0, 0, 1): -s, (0, 1, 0): -s,
        (1, 0, 0): s, (1, 1, 1): -s, (1, 0, 1): c, (1, 1, 0): c,
    }.items():
        tic[:, rout, :, cs, :, r, :] = value
    out["tic"] = single(tic.reshape(128, 128))
    zfc = np.zeros((8, 2, 2, 4, 2, 32, 16))
    zic = np.zeros((8, 16, 2, 64, 4))
    for b in range(8):
        phi = turn(kz[None, :], (b * 4 + np.arange(4))[:, None], 32)
        zfc[b, 0, :, :, 0] = np.cos(phi)[None, :, None, :]
        zfc[b, 1, :, :, 0] = np.sin(phi)[None, :, None, :]
        zfc[b, 0, :, :, 1] = -np.sin(phi)[None, :, None, :]
        zfc[b, 1, :, :, 1] = np.cos(phi)[None, :, None, :]
        zic[b, :, 0] = np.cos(phi).T[:, None, :]
        zic[b, :, 1] = np.sin(phi).T[:, None, :]
    out["zfc"] = single(zfc.reshape(8, 2, 8, 1024))
    out["zic"] = single(zic.reshape(8, 16, 512))
    alpha = turn(signed(kx)[:, None], np.arange(64)[None, :], 64)
    ixc = np.zeros((32, 2, 2, 2, 64))
    for big in range(2):
        ixc[:, 0, big, big] = np.cos(alpha)
        ixc[:, 1, big, big] = -np.sin(alpha)
    out["ixc"] = single(ixc.reshape(128, 128))
    return out


def split(value):
    high = value.astype(BF16)
    return high, (value - high.astype(F32)).astype(BF16)


def dot(left, right, dims=((1,), (0,))):
    return lax.dot_general(left, right, (dims, ((), ())), preferred_element_type=F32)


def dot3(left_high, left_low, right_high, right_low, dims=((1,), (0,))):
    return (
        dot(left_high, right_high, dims)
        + dot(left_high, right_low, dims)
        + dot(left_low, right_high, dims)
    )


def iota(shape, dim):
    return lax.broadcasted_iota(jnp.int32, shape, dim)


def ones_where(condition):
    return jnp.where(condition, 1.0, 0.0).astype(BF16)


def kron_eye(first, shift):
    rows, m = first.shape
    spread = ones_where(iota((m, m << shift), 0) == (iota((m, m << shift), 1) >> shift))
    full = dot(first.astype(BF16), spread)
    low = (1 << shift) - 1
    shape = (rows, m << shift)
    return jnp.where((iota(shape, 0) & low) == (iota(shape, 1) & low), full, 0.0).astype(BF16)


def rows_of(weight, n, shift, axis):
    pick = ones_where((iota((n << shift, n), 0) >> shift) == iota((n << shift, n), 1))
    return dot(pick, weight, ((1,), (axis,)))


def to_modes(packed, count):
    lanes = count * 16
    real = jnp.concatenate([packed[0:4]] * 16, axis=0)
    imag = jnp.concatenate([packed[4:8]] * 16, axis=0)
    mask = (iota((64, lanes), 0) >> 2) == (iota((64, lanes), 1) & 15)
    wide = jnp.concatenate([jnp.where(mask, real, 0.0), jnp.where(mask, imag, 0.0)], axis=0)
    pick = ones_where((iota((lanes, count), 0) >> 4) == iota((lanes, count), 1))
    high, low = split(wide)
    modes = dot(high, pick) + dot(low, pick)
    return modes[:64], modes[64:]


def from_modes(real, imag, count):
    lanes = count * 16
    high, low = split(jnp.concatenate([real, imag], axis=0))
    spread = ones_where(iota((count, lanes), 0) == (iota((count, lanes), 1) >> 4))
    wide = dot(high, spread) + dot(low, spread)
    mask = ((iota((128, lanes), 0) & 63) >> 2) == (iota((128, lanes), 1) & 15)
    high, low = split(jnp.where(mask, wide, 0.0))
    shape = (8, 128)
    total = ones_where(
        ((iota(shape, 1) >> 6) == (iota(shape, 0) >> 2)) & ((iota(shape, 1) & 3) == (iota(shape, 0) & 3))
    )
    return dot(total, high) + dot(total, low)


def column(values, index):
    return values[:, index : index + 1]


def mix_modes(weight_ref, real, imag, count):
    out_real = jnp.zeros((64, count), F32)
    out_imag = jnp.zeros((64, count), F32)
    for i in range(count):
        w0, w1 = weight_ref[0, i], weight_ref[1, i]
        a, b = column(real, i), column(imag, i)
        out_real = out_real + (w0 * a - w1 * b)
        out_imag = out_imag + (w0 * b + w1 * a)
    return out_real, out_imag


def mode_factor(cells):
    return jnp.where(iota((64, 1), 0) < 4, 1.0 / cells, 2.0 / cells).astype(F32)


def tanh_gelu(value):
    return 0.5 * value * (1.0 + jnp.tanh(ROOT * (value + 0.044715 * value * value * value)))


def kernel(
    feat, cot_hbm, w_fine, spec_hbm, lift, w_coarse, spec_c_hbm, project,
    tx_in, ix_in, ty_hbm, zf_hbm, zi_hbm, ti_hbm, txc_in, tyc_in, zfc_hbm, zic_hbm, tic_in, ixc_in,
    layer_out, grad_out, gspec,
    b0, b1, b2, fy, gph, gpl, cot, spec, spec_c,
    ty, tye, zf, zi, ti, tie, zfc, zic, zfull_h, zfull_l, zifull_h, zifull_l,
    tx, ix, ty_s, tye_s, zf_s, zi_s, ti_s, tie_s,
    wk, wkt, yc, rst, rst2, modes,
    s_buf, rx, rxe, ex, re_buf, hq, ri, sv, sve, g_buf,
    sc, rc, exc, rec, hc, ric, svc, gc,
    load_sem, px_send, px_recv, pxe_send, pxe_recv, py_send, py_recv, pye_send,
    c_send, c_recv,
):
    me = lax.axis_index("px")
    mine = lax.axis_index("py")
    partner = lax.rem(NPX - me, NPX)
    upper = lax.div(me + 15, 32)
    is0 = 1 - lax.div(me + 31, 32)
    is16 = lax.div(me, 16) * (1 - upper)
    kind = upper + 2 * is0 + 3 * is16
    regular = 1 - is0 - is16

    loads = [
        (cot_hbm, cot), (spec_hbm, spec), (spec_c_hbm, spec_c),
        (ty_hbm.at[kind], ty), (ty_hbm.at[4], tye), (zf_hbm.at[mine], zf), (zi_hbm.at[mine], zi),
        (ti_hbm.at[kind], ti), (ti_hbm.at[4], tie), (zfc_hbm.at[mine], zfc), (zic_hbm.at[mine], zic),
    ]
    loads = [pltpu.make_async_copy(a, b, load_sem.at[n]) for n, (a, b) in enumerate(loads)]
    for load in loads:
        load.start()

    barrier = pltpu.get_barrier_semaphore()

    def greet(t, carry):
        pl.semaphore_signal(
            barrier, inc=1, device_id={"px": lax.rem(me + t, NPX), "py": mine}, device_id_type=MESH
        )
        return carry

    lax.fori_loop(1, NPX, greet, 0)

    def greet_own(t, carry):
        pl.semaphore_signal(
            barrier, inc=1, device_id={"px": me, "py": lax.rem(mine + t, NPY)}, device_id_type=MESH
        )
        return carry

    lax.fori_loop(1, NPY, greet_own, 0)

    @pl.when(regular == 1)
    def _():
        def greet_partner(t, carry):
            pl.semaphore_signal(
                barrier, inc=1, device_id={"px": partner, "py": lax.rem(mine + t, NPY)},
                device_id_type=MESH,
            )
            return carry

        lax.fori_loop(1, NPY, greet_partner, 0)

    def pair_row(d):
        h = lax.div(d + 15, 32)
        return h, pl.multiple_of(16 * (d * (1 - 2 * h) + 32 * h), 16)

    def px_forward(n):
        def send(t, carry):
            d = lax.rem(me + t, NPX)
            h, row = pair_row(d)
            pltpu.make_async_remote_copy(
                s_buf.at[n, h, :, pl.ds(row, 16)], rx.at[n, :, pl.ds(pl.multiple_of(16 * me, 16), 16)],
                px_send.at[2 * n], px_recv.at[2 * n], device_id={"px": d, "py": mine}, device_id_type=MESH,
            ).start()
            return carry

        lax.fori_loop(1, NPX, send, 0)
        h, row = pair_row(me)
        pltpu.make_async_copy(
            s_buf.at[n, h, :, pl.ds(row, 16)], rx.at[n, :, pl.ds(pl.multiple_of(16 * me, 16), 16)], px_recv.at[2 * n]
        ).start()

        @pl.when(is16 == 0)
        def _():
            pltpu.make_async_remote_copy(
                s_buf.at[n, 1, :, pl.ds(256, 16)], rxe.at[n, :, pl.ds(pl.multiple_of(16 * me, 16), 16)],
                pxe_send.at[2 * n], pxe_recv.at[2 * n], device_id={"px": 16, "py": mine}, device_id_type=MESH,
            ).start()

        @pl.when(is16 == 1)
        def _():
            pltpu.make_async_copy(
                s_buf.at[n, 1, :, pl.ds(256, 16)], rxe.at[n, :, pl.ds(pl.multiple_of(16 * me, 16), 16)],
                pxe_recv.at[2 * n],
            ).start()

    def px_forward_wait(n):
        pltpu.make_async_copy(rx.at[n], rx.at[n], px_recv.at[2 * n]).wait()

        @pl.when(is16 == 1)
        def _():
            pltpu.make_async_copy(rxe.at[n], rxe.at[n], pxe_recv.at[2 * n]).wait()

    def px_inverse(n):
        h, row = pair_row(me)

        def send(t, carry):
            d = lax.rem(me + t, NPX)
            pltpu.make_async_remote_copy(
                sv.at[n, :, pl.ds(pl.multiple_of(16 * d, 16), 16)], g_buf.at[n, h, :, pl.ds(row, 16)],
                px_send.at[2 * n + 1], px_recv.at[2 * n + 1],
                device_id={"px": d, "py": mine}, device_id_type=MESH,
            ).start()
            return carry

        lax.fori_loop(1, NPX, send, 0)
        pltpu.make_async_copy(
            sv.at[n, :, pl.ds(pl.multiple_of(16 * me, 16), 16)], g_buf.at[n, h, :, pl.ds(row, 16)],
            px_recv.at[2 * n + 1],
        ).start()

        @pl.when(is16 == 1)
        def _():
            def send_extra(t, carry):
                d = lax.rem(me + t, NPX)
                pltpu.make_async_remote_copy(
                    sve.at[n, :, pl.ds(pl.multiple_of(16 * d, 16), 16)], g_buf.at[n, 1, :, pl.ds(256, 16)],
                    pxe_send.at[2 * n + 1], pxe_recv.at[2 * n + 1],
                    device_id={"px": d, "py": mine}, device_id_type=MESH,
                ).start()
                return carry

            lax.fori_loop(1, NPX, send_extra, 0)
            pltpu.make_async_copy(
                sve.at[n, :, pl.ds(pl.multiple_of(16 * me, 16), 16)], g_buf.at[n, 1, :, pl.ds(256, 16)],
                pxe_recv.at[2 * n + 1],
            ).start()

    def px_inverse_wait(n):
        pltpu.make_async_copy(rx.at[n], rx.at[n], px_recv.at[2 * n + 1]).wait()
        some = g_buf.at[n, 1, :, pl.ds(256, 16)]
        pltpu.make_async_copy(some, some, pxe_recv.at[2 * n + 1]).wait()

    def py_exchange(slot, source, target):
        def send(t, carry):
            p = lax.rem(mine + t, NPY)
            for q, to in ((0, me), (1, partner)):
                pltpu.make_async_remote_copy(
                    source(q, p), target.at[8 * q + mine], py_send.at[slot], py_recv.at[slot],
                    device_id={"px": to, "py": p}, device_id_type=MESH,
                ).start()
            return carry

        lax.fori_loop(1, NPY, send, 0)
        pltpu.make_async_copy(source(0, mine), target.at[mine], py_recv.at[slot]).start()

        @pl.when(regular == 1)
        def _():
            pltpu.make_async_remote_copy(
                source(1, mine), target.at[8 + mine], pye_send.at[slot], py_recv.at[slot],
                device_id={"px": partner, "py": mine}, device_id_type=MESH,
            ).start()

        @pl.when(regular == 0)
        def _():
            pltpu.make_async_copy(source(1, mine), target.at[8 + mine], py_recv.at[slot]).start()

    def py_wait(slot, target):
        pltpu.make_async_copy(target, target, py_recv.at[slot]).wait()

    def coarse_px(slot, source, target):
        there = target.at[pl.ds(pl.multiple_of(8 * me, 8), 8)]

        def send(t, carry):
            d = lax.rem(me + t, NPX)
            pltpu.make_async_remote_copy(
                source.at[pl.ds(pl.multiple_of(8 * d, 8), 8)], there, c_send.at[slot], c_recv.at[slot],
                device_id={"px": d, "py": mine}, device_id_type=MESH,
            ).start()
            return carry

        lax.fori_loop(1, NPX, send, 0)
        pltpu.make_async_copy(source.at[pl.ds(pl.multiple_of(8 * me, 8), 8)], there, c_recv.at[slot]).start()

    def coarse_py(slot, source, target):
        def send(t, carry):
            p = lax.rem(mine + t, NPY)
            pltpu.make_async_remote_copy(
                source(p), target.at[mine], c_send.at[slot], c_recv.at[slot],
                device_id={"px": me, "py": p}, device_id_type=MESH,
            ).start()
            return carry

        lax.fori_loop(1, NPY, send, 0)
        pltpu.make_async_copy(source(mine), target.at[mine], c_recv.at[slot]).start()

    def coarse_wait(slot, target):
        pltpu.make_async_copy(target, target, c_recv.at[slot]).wait()

    def tiles(ref, n):
        return jnp.concatenate([ref[n, 0], ref[n, 1]], axis=1)

    def put_tiles(ref, n, value):
        ref[n, 0] = value[:, :128]
        ref[n, 1] = value[:, 128:]

    def store_pairs(n, y, both):
        for h in range(2):
            for t in range(2):
                at = 256 * h + 128 * t
                s_buf[n, h, t, pl.ds(y, 40, stride=8), :] = both[:, at : at + 128]

    def fix_zero(n):
        s_buf[n, 0, :, pl.ds(8, 8), :] = s_buf[n, 1, :, pl.ds(0, 8), :]

    def forward_yz(n):
        high, low = split(tiles(rx, n))
        yc[...] = dot3(ty_s[0], ty_s[1], high, low)

        @pl.when(is16 == 1)
        def _():
            high, low = split(tiles(rxe, n))
            yc[...] += dot3(tye_s[0], tye_s[1], high, low)

        dup = ((iota((128, 128), 0) >> 2) & 1) == 0
        for t in range(2):
            lanes = pl.ds(128 * t, 128)
            both = jnp.concatenate([yc[pl.ds(0, 128), lanes], yc[pl.ds(128, 128), lanes]], axis=1)
            high, low = split(both)
            full = dot3(high, low, zf_s[0], zf_s[1])
            picked = jnp.where(dup, full[:, :128], full[:, 128:])
            ex[n, :, :, lanes] = picked.reshape(16, 8, 128)

    def gather_modes(n):
        slot0 = jnp.sum(re_buf[n, 0:8], axis=0)
        slot1 = jnp.sum(re_buf[n, 8:16], axis=0)
        swap = upper == 1
        first = jnp.where(swap, slot1, slot0)
        second = jnp.where(swap, slot0, slot1)
        return to_modes(jnp.concatenate([first, second], axis=1), 32)

    def spread_modes(n, real, imag):
        packed = from_modes(real, imag, 32)
        first, second = packed[:, :256], packed[:, 256:]
        swap = upper == 1
        hq[n, 0] = jnp.where(swap, second, first)
        hq[n, 1] = jnp.where(swap, first, second)

    def inverse_zy(n):
        value = ri[n].reshape(128, 256)
        parts = []
        for t in range(2):
            high, low = split(value[:, 128 * t : 128 * t + 128])
            parts.append(dot3(high, low, zi_s[0], zi_s[1]))
        stacked = jnp.concatenate(
            [
                jnp.concatenate([parts[0][:, :128], parts[1][:, :128]], axis=1),
                jnp.concatenate([parts[0][:, 128:], parts[1][:, 128:]], axis=1),
            ],
            axis=0,
        )
        high, low = split(stacked)
        put_tiles(sv, n, dot3(ti_s[0], ti_s[1], high, low))

        @pl.when(is16 == 1)
        def _():
            put_tiles(sve, n, dot3(tie_s[0], tie_s[1], high, low))

    def inverse_x(n, y):
        parts = [
            g_buf[n, h, t, pl.ds(y, 40, stride=8), :] for h in range(2) for t in range(2)
        ]
        value = jnp.concatenate(parts, axis=1)
        high = value.astype(BF16).astype(F32)
        stacked = jnp.concatenate([high, value - high, high, jnp.zeros((8, 512), F32)], axis=0)
        return dot(stacked.T.astype(BF16), ix[...])

    def fix_inverse_zero(n):
        g_buf[n, 1, :, pl.ds(0, 8), :] = g_buf[n, 0, :, pl.ds(8, 8), :]

    def take(ref, y):
        return jnp.concatenate(
            [ref[t, pl.ds(y, 512, stride=8), :] for t in range(2)], axis=1
        )

    def put(ref, y, value):
        for t in range(2):
            ref[t, pl.ds(y, 512, stride=8), :] = value[:, 128 * t : 128 * t + 128]

    def block(ref, y):
        rows = pl.ds(pl.multiple_of(512 * y, 512), 512)
        return jnp.concatenate([ref[0, rows, :], ref[1, rows, :]], axis=1)

    def put_block(ref, y, value):
        rows = pl.ds(pl.multiple_of(512 * y, 512), 512)
        ref[0, rows, :] = value[:, :128]
        ref[1, rows, :] = value[:, 128:]

    def unpack(ref, field):
        for t in range(2):
            ref[t] = field[:, :, pl.ds(128 * t, 128)].astype(F32).reshape(4096, 128)

    def pack(field, ref):
        for t in range(2):
            field[:, :, pl.ds(128 * t, 128)] = ref[t].reshape(512, 8, 128).astype(BF16)

    high, low = split(tx_in[...])
    tx[pl.ds(0, 40), :] = high
    tx[pl.ds(40, 40), :] = low
    high, low = split(ix_in[...])
    ix[...] = jnp.concatenate([high.astype(F32), high.astype(F32), low.astype(F32), jnp.zeros((8, 256), F32)], axis=0).astype(BF16)
    unpack(b0, feat)

    def analyse_x(y, carry):
        field = take(b0, y).astype(BF16)
        fy[y] = field
        both = dot(tx[...], field, ((1,), (1,)))
        store_pairs(0, y, both[:40] + both[40:])
        return carry

    lax.fori_loop(0, 8, analyse_x, 0)
    fix_zero(0)
    for n in range(2):
        g_buf[n, :, :, pl.ds(272, 48), :] = jnp.zeros((2, 2, 48, 128), F32)
        g_buf[n, 1, :, pl.ds(0, 16), :] = jnp.zeros((2, 16, 128), F32)
    sc[...] = jnp.zeros((256, 128), F32)

    pl.semaphore_wait(barrier, 38 + 7 * regular)
    px_forward(0)

    txc_high, txc_low = split(txc_in[...])
    pool = ones_where(iota((128, 512), 0) == (iota((128, 512), 1) >> 2))
    for big in range(2):
        total = dot(pool, fy[4 * big])
        for y in range(1, 4):
            total = total + dot(pool, fy[4 * big + y])
        total = total * (1.0 / 64.0)
        rst[big] = total
        high, low = split(total)
        part = dot3(txc_high, txc_low, high, low, ((1,), (1,)))
        sc[pl.ds(big, 64, stride=4), :] = part
    coarse_px(0, sc, rc)

    wk[...] = kron_eye(rows_of(w_fine[...], 32, 4, 1), 4)
    wkt[...] = kron_eye(rows_of(w_fine[...], 32, 4, 0), 4)

    def local(y, carry):
        put_block(b2, y, dot(wk[...], fy[y]))
        return carry

    lax.fori_loop(0, 8, local, 0)
    loads[0].wait()
    unpack(b1, cot)
    low_total = jnp.zeros((128, 128), F32)
    for big in range(2):
        gather = ones_where(iota((256, 128), 1) == 64 * big + (iota((256, 128), 0) >> 2))
        high, low = split(rst[big])
        low_total = low_total + dot(high, gather) + dot(low, gather)
    rst2[...] = low_total
    for n in range(1, 11):
        loads[n].wait()
    for whole, parts in ((ty, ty_s), (tye, tye_s), (zf, zf_s), (zi, zi_s), (ti, ti_s), (tie, tie_s)):
        high, low = split(whole[...])
        parts[0] = high
        parts[1] = low
    base_mask = (iota((128, 1024), 0) >> 2) == ((iota((128, 1024), 1) & 511) >> 4)
    for r in range(2):
        full = jnp.where(base_mask, jnp.concatenate([zfc[r]] * 16, axis=0), 0.0)
        high, low = split(full)
        zfull_h[pl.ds(128 * r, 128), :] = high
        zfull_l[pl.ds(128 * r, 128), :] = low

    def build(step, carry):
        rows = 128 * step + iota((128, 512), 0)
        keep = (rows >> 4) == ((iota((128, 512), 1) & 255) >> 2)
        high, low = split(jnp.where(keep, jnp.concatenate([zic[...]] * 8, axis=0), 0.0))
        at = pl.ds(pl.multiple_of(128 * step, 128), 128)
        zifull_h[at, :] = high
        zifull_l[at, :] = low
        return carry

    lax.fori_loop(0, 8, build, 0)

    px_forward_wait(0)
    forward_yz(0)
    py_exchange(0, lambda q, p: ex.at[0, 8 * q + p], re_buf.at[0])

    coarse_wait(0, rc)
    high, low = split(rc[...])
    along_y = dot3(*split(tyc_in[...]), high, low)
    high, low = split(jnp.concatenate([along_y[:64], along_y[64:]], axis=1))
    full = dot3(high, low, zfull_h[...], zfull_l[...])
    dup = ((iota((64, 512), 0) >> 2) & 1) == 0
    exc[...] = jnp.where(dup, full[:, :512], full[:, 512:]).reshape(8, 8, 512)
    coarse_py(1, lambda p: exc.at[p], rec)

    py_wait(0, re_buf.at[0])
    real, imag = gather_modes(0)
    modes[0] = real
    modes[1] = imag
    out_real, out_imag = mix_modes(spec, real, imag, 32)
    fine_factor = mode_factor(256.0 * 256.0 * 128.0)
    spread_modes(0, out_real * fine_factor, out_imag * fine_factor)
    py_exchange(1, lambda q, p: hq.at[0, q], ri.at[0])

    coarse_wait(1, rec)
    real, imag = to_modes(jnp.sum(rec[...], axis=0), 32)
    high, low = split(jnp.concatenate([real, imag], axis=0))
    lifted = dot(high, lift[...]) + dot(low, lift[...])
    out_real, out_imag = mix_modes(spec_c, lifted[:64], lifted[64:], 64)
    coarse_factor = mode_factor(64.0 * 64.0 * 32.0)
    hc[...] = from_modes(out_real * coarse_factor, out_imag * coarse_factor, 64)
    coarse_py(2, lambda p: hc, ric)

    py_wait(1, ri.at[0])
    inverse_zy(0)
    px_inverse(0)

    coarse_wait(2, ric)
    high, low = split(ric[...].reshape(64, 1024))
    along_z = dot3(high, low, zifull_h[...], zifull_l[...])
    high, low = split(jnp.concatenate([along_z[:, :256], along_z[:, 256:]], axis=0))
    along_y = dot3(*split(tic_in[...]), high, low)
    for hh in range(2):
        svc[pl.ds(hh, 128, stride=2), :] = along_y[:, 128 * hh : 128 * hh + 128]
    coarse_px(3, svc, gc)

    px_inverse_wait(0)
    fix_inverse_zero(0)

    def middle(y, carry):
        pre = block(b2, y) + inverse_x(0, y)
        square = pre * pre
        t = jnp.tanh(ROOT * pre * (1.0 + 0.044715 * square))
        half = 0.5 * (1.0 + t)
        put_block(b0, y, pre * half)
        slope = half + 0.5 * pre * (1.0 - t * t) * (ROOT + (3.0 * 0.044715 * ROOT) * square)
        grad = take(b1, y) * slope
        high, low = split(grad)
        gph[y] = high
        gpl[y] = low
        both = dot(tx[...], high, ((1,), (1,)))
        part = both[:40] + both[40:] + dot(tx[pl.ds(0, 40), :], low, ((1,), (1,)))
        store_pairs(1, y, part)
        return carry

    lax.fori_loop(0, 8, middle, 0)
    fix_zero(1)
    px_forward(1)

    def direct(y, carry):
        put_block(b1, y, dot(wkt[...], gph[y]) + dot(wkt[...], gpl[y]))
        return carry

    lax.fori_loop(0, 8, direct, 0)

    coarse_wait(3, gc)
    halves_out = []
    for hh in range(2):
        high, low = split(gc[pl.ds(hh, 128, stride=2), :].T)
        halves_out.append(dot3(high, low, *split(ixc_in[...])))
    spectral_part = jnp.concatenate(halves_out, axis=0)
    lift_wide = kron_eye(rows_of(lift[...], 64, 2, 1), 2)
    coarse_wide = kron_eye(rows_of(w_coarse[...], 64, 2, 1), 2)
    project_wide = kron_eye(rows_of(project[...], 32, 2, 0), 2)
    high, low = split(rst2[...])
    lifted = dot(lift_wide, high) + dot(lift_wide, low)
    high, low = split(lifted)
    coarse_pre = spectral_part + dot(coarse_wide, high) + dot(coarse_wide, low)
    high, low = split(tanh_gelu(coarse_pre))
    coarse_out = dot(project_wide, high) + dot(project_wide, low)
    out_high, out_low = split(coarse_out)
    widen = ones_where((iota((512, 128), 0) >> 2) == iota((512, 128), 1))
    for big in range(2):
        stretch = ones_where(iota((128, 256), 0) == 64 * big + (iota((128, 256), 1) >> 2))
        high, low = split(dot(out_high, stretch) + dot(out_low, stretch))
        prolonged = dot(widen, high) + dot(widen, low)
        for small in range(4):
            y = 4 * big + small
            put(b2, y, block(b0, y) + prolonged)
    pack(layer_out, b2)

    px_forward_wait(1)
    forward_yz(1)
    py_exchange(2, lambda q, p: ex.at[1, 8 * q + p], re_buf.at[1])
    py_wait(2, re_buf.at[1])
    real, imag = gather_modes(1)
    real, imag = real * fine_factor, imag * fine_factor
    lane = iota((64, 32), 1)
    pull_real = jnp.zeros((64, 32), F32)
    pull_imag = jnp.zeros((64, 32), F32)
    for i in range(32):
        w0, w1 = spec[0, i], spec[1, i]
        a = jnp.sum(w0 * real + w1 * imag, axis=1, keepdims=True)
        b = jnp.sum(w0 * imag - w1 * real, axis=1, keepdims=True)
        pull_real = jnp.where(lane == i, a, pull_real)
        pull_imag = jnp.where(lane == i, b, pull_imag)
    spread_modes(1, pull_real, pull_imag)
    py_exchange(3, lambda q, p: hq.at[1, q], ri.at[1])
    x_real, x_imag = modes[0], modes[1]
    for i in range(32):
        a, b = column(x_real, i), column(x_imag, i)
        gspec[0, i] = real * a + imag * b
        gspec[1, i] = imag * a - real * b
    py_wait(3, ri.at[1])
    inverse_zy(1)
    px_inverse(1)

    px_inverse_wait(1)
    fix_inverse_zero(1)

    def final(y, carry):
        put(b2, y, block(b1, y) + inverse_x(1, y))
        return carry

    lax.fori_loop(0, 8, final, 0)
    pack(grad_out, b2)

    for n in range(2):
        most = rx.at[n, :, pl.ds(0, 496)]
        for k in range(2):
            pltpu.make_async_copy(most, most, px_send.at[2 * n + k]).wait()

        @pl.when(is16 == 0)
        def _():
            some = rx.at[n, :, pl.ds(0, 16)]
            pltpu.make_async_copy(some, some, pxe_send.at[2 * n]).wait()

        @pl.when(is16 == 1)
        def _():
            pltpu.make_async_copy(most, most, pxe_send.at[2 * n + 1]).wait()

    for slot in range(4):
        most = ex.at[0, pl.ds(0, 14)]
        pltpu.make_async_copy(most, most, py_send.at[slot]).wait()

        @pl.when(regular == 1)
        def _():
            pltpu.make_async_copy(ex.at[0, 0], ex.at[0, 0], pye_send.at[slot]).wait()

    for slot, most in ((0, rc.at[pl.ds(0, 248)]), (1, exc.at[pl.ds(0, 7)]), (2, ric.at[pl.ds(0, 7)]), (3, gc.at[pl.ds(0, 248)])):
        pltpu.make_async_copy(most, most, c_send.at[slot]).wait()


def body(
    features, cotangent, pointwise_fine, spectral_fine, lift_weight, pointwise_coarse,
    spectral_coarse, project_weight,
):
    table = tables()
    fine = spectral_fine.transpose(0, 1, 3, 4, 5, 2).reshape(2, 32, 64, 32)
    coarse = spectral_coarse.transpose(0, 1, 3, 4, 5, 2).reshape(2, 64, 64, 64)
    vmem = pl.BlockSpec(memory_space=pltpu.VMEM)
    hbm = pl.BlockSpec(memory_space=pl.ANY)

    def f32(*shape):
        return pltpu.VMEM(shape, F32)

    def bf16(*shape):
        return pltpu.VMEM(shape, BF16)

    dma = pltpu.SemaphoreType.DMA
    layer_out, grad_out, gspec = pl.pallas_call(
        kernel,
        out_shape=[
            jax.ShapeDtypeStruct((512, 8, 256), BF16),
            jax.ShapeDtypeStruct((512, 8, 256), BF16),
            jax.ShapeDtypeStruct((2, 32, 64, 32), F32),
        ],
        in_specs=[vmem, hbm, vmem, hbm, vmem, vmem, hbm, vmem, vmem, vmem, hbm, hbm, hbm, hbm, vmem, vmem, hbm, hbm, vmem, vmem],
        out_specs=[vmem, vmem, vmem],
        scratch_shapes=[
            f32(2, 4096, 128), f32(2, 4096, 128), f32(2, 4096, 128),
            bf16(8, 512, 256), bf16(8, 512, 256), bf16(8, 512, 256),
            bf16(512, 8, 256), f32(2, 32, 64, 32), f32(2, 64, 64, 64),
            f32(256, 512), f32(256, 512), f32(256, 256), f32(128, 256),
            f32(512, 256), f32(512, 256), f32(2, 8, 1024), f32(16, 512),
            bf16(256, 1024), bf16(256, 1024), bf16(1024, 512), bf16(1024, 512),
            bf16(80, 256), bf16(128, 256), bf16(2, 256, 512), bf16(2, 256, 512), bf16(2, 256, 256), bf16(2, 128, 256),
            bf16(2, 512, 256), bf16(2, 512, 256),
            bf16(512, 512), bf16(512, 512), f32(256, 256), f32(2, 128, 256), f32(128, 128), f32(2, 64, 32),
            f32(2, 2, 2, PAIRS, 128), f32(2, 2, 512, 128), f32(2, 2, 512, 128), f32(2, 16, 8, 256), f32(2, 16, 8, 256),
            f32(2, 2, 8, 256), f32(2, 16, 8, 256), f32(2, 2, 512, 128), f32(2, 2, 512, 128), f32(2, 2, 2, PAIRS, 128),
            f32(256, 128), f32(256, 128), f32(8, 8, 512), f32(8, 8, 512), f32(8, 1024), f32(8, 8, 1024),
            f32(256, 128), f32(256, 128),
            dma((11,)), dma((4,)), dma((4,)), dma((4,)), dma((4,)), dma((4,)), dma((4,)), dma((4,)),
            dma((4,)), dma((4,)),
        ],
        compiler_params=pltpu.CompilerParams(
            collective_id=0, has_side_effects=True, vmem_limit_bytes=60 * 1024 * 1024
        ),
        name="fno_layer",
    )(
        features.reshape(512, 8, 256), cotangent.reshape(512, 8, 256), pointwise_fine, fine, lift_weight,
        pointwise_coarse, coarse, project_weight.T,
        table["tx"], table["ix"], table["ty"], table["zf"], table["zi"], table["ti"], table["txc"], table["tyc"],
        table["zfc"], table["zic"], table["tic"], table["ixc"],
    )
    shape = (32, 16, 8, 256)
    gspec = gspec.reshape(2, 32, 16, 1, 4, 32).transpose(0, 1, 5, 2, 3, 4)
    return layer_out.reshape(shape), grad_out.reshape(shape), gspec


def solution(mesh):
    placed = (
        P(None, "py", "px", None),
        P(None, "py", "px", None),
        P(),
        P(None, None, None, None, "px", "py"),
        P(),
        P(),
        P(None, None, None, None, "px", "py"),
        P(),
    )
    return jax.shard_map(
        body,
        mesh=mesh,
        in_specs=placed,
        out_specs=(
            P(None, "py", "px", None),
            P(None, "py", "px", None),
            P(None, None, None, None, "px", "py"),
        ),
        check_vma=False,
    )
```

```python
import functools
import math

import jax
import jax.numpy as jnp
import numpy as np
from jax import lax
from jax.experimental import pallas as pl
from jax.experimental.pallas import tpu as pltpu
from jax.sharding import PartitionSpec as P

M = 16
F32 = jnp.float32
BF16 = jnp.bfloat16
MESH = pl.DeviceIdType.MESH
NPX, NPY = 32, 8
PAIRS = 320
ROOT = math.sqrt(2.0 / math.pi)


def single(table):
    return np.asarray(table, np.float64).astype(np.float32)


def signed(index):
    return np.where(index < M, index, index - 2 * M)


def turn(freq, cell, count):
    return (np.asarray(freq) * np.asarray(cell) % count) * (2.0 * np.pi / count)


@functools.cache
def tables():
    out = {}
    x = np.arange(256)
    rows = np.zeros((40, 256))
    for j in range(17):
        angle = turn(j, x, 256)
        if j == 0:
            rows[0] = rows[1] = 1.0
        else:
            rows[2 * j] = np.cos(angle)
            rows[2 * j + 1] = -np.sin(angle) if j < 16 else np.sin(angle)
    out["tx"] = single(rows)
    inv = rows.copy()
    inv[1] = 0.0
    out["ix"] = single(inv)

    ky = np.arange(32)
    theta = turn(signed(ky)[:, None], np.arange(256)[None, :], 256)
    cos, sin = np.cos(theta), np.sin(theta)
    zero = np.zeros_like(cos)
    plus = (((cos, sin), (-sin, cos)))
    minus = (((cos, -sin), (-sin, -cos)))
    from0 = (((cos, zero), (-sin, zero)))
    from1 = (((zero, cos), (zero, -sin)))
    none = (((zero, zero), (zero, zero)))
    kinds = [(plus, minus), (minus, plus), (from0, from1), (plus, none), (none, plus)]
    ty = np.zeros((5, 2, 2, 8, 2, 4, 32, 2, 8))
    for k, pair in enumerate(kinds):
        for q in range(2):
            for r1 in range(2):
                for r in range(2):
                    block = pair[q][r1][r].reshape(8, 4, 32, 8)
                    for dup in range(2):
                        ty[k, r1, q, :, dup, :, :, r, :] = block
    ty = ty.reshape(5, 256, 512)
    out["ty"] = single(ty)

    ti = np.zeros((5, 32, 2, 8, 2, 2, 8, 2, 4))

    def add(k, rout, q, part, sign):
        c = cos.T.reshape(32, 8, 8, 4)
        s = sin.T.reshape(32, 8, 8, 4)
        if part == 0:
            coef = {(0, 0): c, (1, 1): -c, (0, 1): -s, (1, 0): -s}
        else:
            coef = {(0, 0): s, (1, 1): -s, (0, 1): c, (1, 0): c}
        for (cs, r), value in coef.items():
            ti[k, :, rout, :, cs, q, :, r, :] += sign * value

    for k, first in ((0, 1.0), (1, -1.0)):
        add(k, 0, 0, 0, 1.0)
        add(k, 0, 1, 0, 1.0)
        add(k, 1, 0, 1, first)
        add(k, 1, 1, 1, -first)
    add(2, 0, 0, 0, 1.0)
    add(2, 1, 1, 0, 1.0)
    for k, q in ((3, 0), (4, 1)):
        add(k, 0, q, 0, 1.0)
        add(k, 1, q, 1, 1.0)
    out["ti"] = single(ti.reshape(5, 512, 256))

    kz = np.arange(16)
    zf = np.zeros((8, 2, 8, 16, 2, 8, 16))
    zi = np.zeros((8, 8, 16, 2, 8, 16))
    for b in range(8):
        phi = turn(kz[None, :], (b * 16 + np.arange(16))[:, None], 128)
        for c in range(8):
            zf[b, 0, c, :, 0, c, :] = np.cos(phi)
            zf[b, 1, c, :, 0, c, :] = np.sin(phi)
            zf[b, 0, c, :, 1, c, :] = -np.sin(phi)
            zf[b, 1, c, :, 1, c, :] = np.cos(phi)
            zi[b, c, :, 0, c, :] = np.cos(phi).T
            zi[b, c, :, 1, c, :] = np.sin(phi).T
    out["zf"] = single(zf.reshape(8, 256, 256))
    out["zi"] = single(zi.reshape(8, 128, 256))

    kx = np.arange(32)
    alpha = turn(signed(kx)[:, None], (x // 4)[None, :], 64)
    txc = np.stack([np.cos(alpha), -np.sin(alpha)], axis=1).reshape(64, 256)
    out["txc"] = single(txc)
    theta = turn(signed(ky)[:, None], np.arange(64)[None, :], 64)
    cos, sin = np.cos(theta), np.sin(theta)
    tyc = np.zeros((2, 8, 2, 4, 32, 2, 4))
    plus = ((cos, sin), (-sin, cos))
    for r1 in range(2):
        for r in range(2):
            for dup in range(2):
                tyc[r1, :, dup, :, :, r, :2] = plus[r1][r].reshape(8, 4, 32, 2)
    out["tyc"] = single(tyc.reshape(128, 256))
    tic = np.zeros((32, 2, 2, 2, 8, 2, 4))
    c = cos.T.reshape(32, 2, 8, 4)
    s = sin.T.reshape(32, 2, 8, 4)
    for (rout, cs, r), value in {
        (0, 0, 0): c, (0, 1, 1): -c, (0, 0, 1): -s, (0, 1, 0): -s,
        (1, 0, 0): s, (1, 1, 1): -s, (1, 0, 1): c, (1, 1, 0): c,
    }.items():
        tic[:, rout, :, cs, :, r, :] = value
    out["tic"] = single(tic.reshape(128, 128))
    zfc = np.zeros((8, 2, 2, 4, 2, 32, 16))
    zic = np.zeros((8, 16, 2, 64, 4))
    for b in range(8):
        phi = turn(kz[None, :], (b * 4 + np.arange(4))[:, None], 32)
        zfc[b, 0, :, :, 0] = np.cos(phi)[None, :, None, :]
        zfc[b, 1, :, :, 0] = np.sin(phi)[None, :, None, :]
        zfc[b, 0, :, :, 1] = -np.sin(phi)[None, :, None, :]
        zfc[b, 1, :, :, 1] = np.cos(phi)[None, :, None, :]
        zic[b, :, 0] = np.cos(phi).T[:, None, :]
        zic[b, :, 1] = np.sin(phi).T[:, None, :]
    out["zfc"] = single(zfc.reshape(8, 2, 8, 1024))
    out["zic"] = single(zic.reshape(8, 16, 512))
    alpha = turn(signed(kx)[:, None], np.arange(64)[None, :], 64)
    ixc = np.zeros((32, 2, 2, 2, 64))
    for big in range(2):
        ixc[:, 0, big, big] = np.cos(alpha)
        ixc[:, 1, big, big] = -np.sin(alpha)
    out["ixc"] = single(ixc.reshape(128, 128))
    return out


def split(value):
    high = value.astype(BF16)
    return high, (value - high.astype(F32)).astype(BF16)


def dot(left, right, dims=((1,), (0,))):
    return lax.dot_general(left, right, (dims, ((), ())), preferred_element_type=F32)


def dot3(left_high, left_low, right_high, right_low, dims=((1,), (0,))):
    return (
        dot(left_high, right_high, dims)
        + dot(left_high, right_low, dims)
        + dot(left_low, right_high, dims)
    )


def iota(shape, dim):
    return lax.broadcasted_iota(jnp.int32, shape, dim)


def ones_where(condition):
    return jnp.where(condition, 1.0, 0.0).astype(BF16)


def kron_eye(first, shift):
    rows, m = first.shape
    spread = ones_where(iota((m, m << shift), 0) == (iota((m, m << shift), 1) >> shift))
    full = dot(first.astype(BF16), spread)
    low = (1 << shift) - 1
    shape = (rows, m << shift)
    return jnp.where((iota(shape, 0) & low) == (iota(shape, 1) & low), full, 0.0).astype(BF16)


def rows_of(weight, n, shift, axis):
    pick = ones_where((iota((n << shift, n), 0) >> shift) == iota((n << shift, n), 1))
    return dot(pick, weight, ((1,), (axis,)))


def to_modes(packed, count):
    lanes = count * 16
    real = jnp.concatenate([packed[0:4]] * 16, axis=0)
    imag = jnp.concatenate([packed[4:8]] * 16, axis=0)
    mask = (iota((64, lanes), 0) >> 2) == (iota((64, lanes), 1) & 15)
    wide = jnp.concatenate([jnp.where(mask, real, 0.0), jnp.where(mask, imag, 0.0)], axis=0)
    pick = ones_where((iota((lanes, count), 0) >> 4) == iota((lanes, count), 1))
    high, low = split(wide)
    modes = dot(high, pick) + dot(low, pick)
    return modes[:64], modes[64:]


def from_modes(real, imag, count):
    lanes = count * 16
    high, low = split(jnp.concatenate([real, imag], axis=0))
    spread = ones_where(iota((count, lanes), 0) == (iota((count, lanes), 1) >> 4))
    wide = dot(high, spread) + dot(low, spread)
    mask = ((iota((128, lanes), 0) & 63) >> 2) == (iota((128, lanes), 1) & 15)
    high, low = split(jnp.where(mask, wide, 0.0))
    shape = (8, 128)
    total = ones_where(
        ((iota(shape, 1) >> 6) == (iota(shape, 0) >> 2)) & ((iota(shape, 1) & 3) == (iota(shape, 0) & 3))
    )
    return dot(total, high) + dot(total, low)


def column(values, index):
    return values[:, index : index + 1]


def mix_modes(weight_ref, real, imag, count):
    out_real = jnp.zeros((64, count), F32)
    out_imag = jnp.zeros((64, count), F32)
    for i in range(count):
        w0, w1 = weight_ref[0, i], weight_ref[1, i]
        a, b = column(real, i), column(imag, i)
        out_real = out_real + (w0 * a - w1 * b)
        out_imag = out_imag + (w0 * b + w1 * a)
    return out_real, out_imag


def mode_factor(cells):
    return jnp.where(iota((64, 1), 0) < 4, 1.0 / cells, 2.0 / cells).astype(F32)


def stacked_table(table):
    high, low = split(table)
    high, low = high.astype(F32), low.astype(F32)
    return jnp.concatenate([high, high, low, jnp.zeros((8, 256), F32)], axis=0).astype(BF16)


def synthesise_x(value, table):
    high = value.astype(BF16).astype(F32)
    pad = jnp.zeros((8, value.shape[1]), F32)
    stacked = jnp.concatenate([high, value - high, high, pad], axis=0)
    return dot(stacked.T.astype(BF16), table)


def tanh_gelu(value):
    return 0.5 * value * (1.0 + jnp.tanh(ROOT * (value + 0.044715 * value * value * value)))


def kernel(
    feat_hbm, cot_hbm, w_fine, spec_hbm, lift, w_coarse, spec_c_hbm, project,
    tx_in, ix_in, ty_hbm, zf_hbm, zi_hbm, ti_hbm, txc_in, tyc_in, zfc_hbm, zic_hbm, tic_in, ixc_in,
    layer_hbm, dir_hbm, gspec_hbm, g_hbm,
    b0, b1, b2, fy, gph, gpl, feat, cot, spec, spec_c, layer_out, gspec,
    ty, tye, zf, zi, ti, tie, zfc, zic, zfull_h, zfull_l, zifull_h, zifull_l,
    tx, ix, ty_s, tye_s, zf_s, zi_s, ti_s, tie_s,
    wk, wkt, yc, rst, rst2, modes,
    s_buf, rx, rxe, ex, re_buf, hq, ri, sv, sve, g_buf,
    sc, rc, exc, rec, hc, ric, svc, gc,
    load_sem, out_sem, px_send, px_recv, pxe_send, pxe_recv, py_send, py_recv, pye_send,
    c_send, c_recv, here,
):
    me = lax.axis_index("px")
    mine = lax.axis_index("py")
    partner = lax.rem(NPX - me, NPX)
    upper = lax.div(me + 15, 32)
    is0 = 1 - lax.div(me + 31, 32)
    is16 = lax.div(me, 16) * (1 - upper)
    kind = upper + 2 * is0 + 3 * is16
    regular = 1 - is0 - is16

    loads = [
        (feat_hbm, feat), (cot_hbm, cot), (spec_hbm, spec), (spec_c_hbm, spec_c),
        (ty_hbm.at[kind], ty), (ty_hbm.at[4], tye), (zf_hbm.at[mine], zf), (zi_hbm.at[mine], zi),
        (ti_hbm.at[kind], ti), (ti_hbm.at[4], tie), (zfc_hbm.at[mine], zfc), (zic_hbm.at[mine], zic),
    ]
    loads = [pltpu.make_async_copy(a, b, load_sem.at[n]) for n, (a, b) in enumerate(loads)]
    for load in loads:
        load.start()

    barrier = pltpu.get_barrier_semaphore()
    row = 8 * lax.div(me, 8)

    def tell(semaphore, px, py):
        pl.semaphore_signal(semaphore, inc=1, device_id={"px": px, "py": py}, device_id_type=MESH)

    for t in range(1, 8):
        tell(barrier, row + lax.rem(me + t, 8), mine)
    for t in range(1, 4):
        tell(barrier, lax.rem(me + 8 * t, NPX), mine)
    for t in range(1, 4):
        tell(barrier, me, lax.rem(mine + 2 * t, NPY))
    other = 2 * lax.div(mine, 2) + 1 - lax.rem(mine, 2)
    tell(barrier, me, other)
    pl.semaphore_wait(barrier, 14)
    for t in range(1, 4):
        tell(here.at[0], lax.rem(me + 8 * t, NPX), mine)

    def pair_row(d):
        h = lax.div(d + 15, 32)
        return h, pl.multiple_of(16 * (d * (1 - 2 * h) + 32 * h), 16)

    def at16(d):
        return pl.ds(pl.multiple_of(16 * d, 16), 16)

    def px_forward(n, t):
        k = 4 * n + t

        def send(step, carry):
            d = lax.rem(me + step, NPX)
            h, row = pair_row(d)
            pltpu.make_async_remote_copy(
                s_buf.at[n, t, h, pl.ds(row, 16)], rx.at[n, t, at16(me)],
                px_send.at[k], px_recv.at[k], device_id={"px": d, "py": mine}, device_id_type=MESH,
            ).start()
            return carry

        lax.fori_loop(1, NPX, send, 0)
        h, row = pair_row(me)
        pltpu.make_async_copy(s_buf.at[n, t, h, pl.ds(row, 16)], rx.at[n, t, at16(me)], px_recv.at[k]).start()

        @pl.when(is16 == 0)
        def _():
            pltpu.make_async_remote_copy(
                s_buf.at[n, t, 1, pl.ds(256, 16)], rxe.at[n, t, at16(me)],
                pxe_send.at[k], pxe_recv.at[k], device_id={"px": 16, "py": mine}, device_id_type=MESH,
            ).start()

        @pl.when(is16 == 1)
        def _():
            pltpu.make_async_copy(
                s_buf.at[n, t, 1, pl.ds(256, 16)], rxe.at[n, t, at16(me)], pxe_recv.at[k]
            ).start()

    def px_forward_wait(n, t):
        k = 4 * n + t
        pltpu.make_async_copy(rx.at[n, t], rx.at[n, t], px_recv.at[k]).wait()

        @pl.when(is16 == 1)
        def _():
            pltpu.make_async_copy(rxe.at[n, t], rxe.at[n, t], pxe_recv.at[k]).wait()

    def px_inverse(n, t, target):
        k = 4 * n + 2 + t
        h, row = pair_row(me)

        def send(step, carry):
            d = lax.rem(me + step, NPX)
            pltpu.make_async_remote_copy(
                sv.at[n, t, at16(d)], target.at[t, h, pl.ds(row, 16)],
                px_send.at[k], px_recv.at[k], device_id={"px": d, "py": mine}, device_id_type=MESH,
            ).start()
            return carry

        lax.fori_loop(1, NPX, send, 0)
        pltpu.make_async_copy(sv.at[n, t, at16(me)], target.at[t, h, pl.ds(row, 16)], px_recv.at[k]).start()

        @pl.when(is16 == 1)
        def _():
            def send_extra(step, carry):
                d = lax.rem(me + step, NPX)
                pltpu.make_async_remote_copy(
                    sve.at[n, t, at16(d)], target.at[t, 1, pl.ds(256, 16)],
                    pxe_send.at[k], pxe_recv.at[k], device_id={"px": d, "py": mine}, device_id_type=MESH,
                ).start()
                return carry

            lax.fori_loop(1, NPX, send_extra, 0)
            pltpu.make_async_copy(sve.at[n, t, at16(me)], target.at[t, 1, pl.ds(256, 16)], pxe_recv.at[k]).start()

    def px_inverse_wait(n, t):
        k = 4 * n + 2 + t
        pltpu.make_async_copy(rx.at[n, t], rx.at[n, t], px_recv.at[k]).wait()
        some = rx.at[n, t, pl.ds(0, 16)]
        pltpu.make_async_copy(some, some, pxe_recv.at[k]).wait()

    def py_exchange(slot, source, target):
        def send(step, carry):
            p = lax.rem(mine + step, NPY)
            for q, to in ((0, me), (1, partner)):
                pltpu.make_async_remote_copy(
                    source(q, p), target.at[8 * q + mine], py_send.at[slot], py_recv.at[slot],
                    device_id={"px": to, "py": p}, device_id_type=MESH,
                ).start()
            return carry

        lax.fori_loop(1, NPY, send, 0)
        pltpu.make_async_copy(source(0, mine), target.at[mine], py_recv.at[slot]).start()

        @pl.when(regular == 1)
        def _():
            pltpu.make_async_remote_copy(
                source(1, mine), target.at[8 + mine], pye_send.at[slot], py_recv.at[slot],
                device_id={"px": partner, "py": mine}, device_id_type=MESH,
            ).start()

        @pl.when(regular == 0)
        def _():
            pltpu.make_async_copy(source(1, mine), target.at[8 + mine], py_recv.at[slot]).start()

    def py_wait(slot, target):
        pltpu.make_async_copy(target, target, py_recv.at[slot]).wait()

    def coarse_px(slot, source, target):
        there = target.at[pl.ds(pl.multiple_of(8 * me, 8), 8)]

        def send(t, carry):
            d = lax.rem(me + t, NPX)
            pltpu.make_async_remote_copy(
                source.at[pl.ds(pl.multiple_of(8 * d, 8), 8)], there, c_send.at[slot], c_recv.at[slot],
                device_id={"px": d, "py": mine}, device_id_type=MESH,
            ).start()
            return carry

        lax.fori_loop(1, NPX, send, 0)
        pltpu.make_async_copy(source.at[pl.ds(pl.multiple_of(8 * me, 8), 8)], there, c_recv.at[slot]).start()

    def coarse_py(slot, source, target):
        def send(t, carry):
            p = lax.rem(mine + t, NPY)
            pltpu.make_async_remote_copy(
                source(p), target.at[mine], c_send.at[slot], c_recv.at[slot],
                device_id={"px": me, "py": p}, device_id_type=MESH,
            ).start()
            return carry

        lax.fori_loop(1, NPY, send, 0)
        pltpu.make_async_copy(source(mine), target.at[mine], c_recv.at[slot]).start()

    def coarse_wait(slot, target):
        pltpu.make_async_copy(target, target, c_recv.at[slot]).wait()

    def fix_zero(n, t):
        s_buf[n, t, 0, pl.ds(8, 8), :] = s_buf[n, t, 1, pl.ds(0, 8), :]

    def forward_yz(n, t):
        high, low = split(rx[n, t])
        yc[...] = dot3(ty_s[0], ty_s[1], high, low)

        @pl.when(is16 == 1)
        def _():
            high, low = split(rxe[n, t])
            yc[...] += dot3(tye_s[0], tye_s[1], high, low)

        dup = ((iota((128, 128), 0) >> 2) & 1) == 0
        both = jnp.concatenate([yc[pl.ds(0, 128), :], yc[pl.ds(128, 128), :]], axis=1)
        high, low = split(both)
        full = dot3(high, low, zf_s[0], zf_s[1])
        ex[n, t] = jnp.where(dup, full[:, :128], full[:, 128:]).reshape(16, 8, 128)
        py_exchange(4 * n + t, lambda q, p: ex.at[n, t, 8 * q + p], re_buf.at[n, t])

    def gather_modes(n):
        slots = []
        for q in range(2):
            parts = []
            for t in range(2):
                if q == 0:
                    py_wait(4 * n + t, re_buf.at[n, t])
                parts.append(jnp.sum(re_buf[n, t, 8 * q : 8 * q + 8], axis=0))
            slots.append(jnp.concatenate(parts, axis=1))
        swap = upper == 1
        first = jnp.where(swap, slots[1], slots[0])
        second = jnp.where(swap, slots[0], slots[1])
        return to_modes(jnp.concatenate([first, second], axis=1), 32)

    def spread_modes(n, real, imag):
        packed = from_modes(real, imag, 32)
        swap = upper == 1
        for t in range(2):
            first, second = packed[:, 128 * t : 128 * t + 128], packed[:, 256 + 128 * t : 384 + 128 * t]
            hq[n, t, 0] = jnp.where(swap, second, first)
            hq[n, t, 1] = jnp.where(swap, first, second)
            py_exchange(4 * n + 2 + t, lambda q, p: hq.at[n, t, q], ri.at[n, t])

    def inverse_zy(n, t, target):
        py_wait(4 * n + 2 + t, ri.at[n, t])
        high, low = split(ri[n, t].reshape(128, 128))
        full = dot3(high, low, zi_s[0], zi_s[1])
        high, low = split(jnp.concatenate([full[:, :128], full[:, 128:]], axis=0))
        sv[n, t] = dot3(ti_s[0], ti_s[1], high, low)

        @pl.when(is16 == 1)
        def _():
            sve[n, t] = dot3(tie_s[0], tie_s[1], high, low)

        px_inverse(n, t, target)

    def rows_at(h, t):
        return 256 * h + 128 * t

    def take(ref, t, y):
        return jnp.concatenate(
            [
                jnp.concatenate(
                    [ref[lane, pl.ds(8 * rows_at(h, t) + y, 128, stride=8), :] for lane in range(2)], axis=1
                )
                for h in range(2)
            ],
            axis=0,
        )

    def put(ref, y, value):
        for lane in range(2):
            ref[lane, pl.ds(y, 512, stride=8), :] = value[:, 128 * lane : 128 * lane + 128]

    def block(ref, y):
        rows = pl.ds(pl.multiple_of(512 * y, 512), 512)
        return jnp.concatenate([ref[0, rows, :], ref[1, rows, :]], axis=1)

    def put_block(ref, y, value):
        rows = pl.ds(pl.multiple_of(512 * y, 512), 512)
        ref[0, rows, :] = value[:, :128]
        ref[1, rows, :] = value[:, 128:]

    def part_rows(h, t, y):
        return pl.ds(pl.multiple_of(512 * y + rows_at(h, t), 128), 128)

    def some_rows(ref, t, y):
        return jnp.concatenate(
            [
                jnp.concatenate([ref[lane, part_rows(h, t, y), :] for lane in range(2)], axis=1)
                for h in range(2)
            ],
            axis=0,
        )

    def put_part(ref, t, y, value):
        for h in range(2):
            for lane in range(2):
                ref[lane, part_rows(h, t, y), :] = value[128 * h : 128 * h + 128, 128 * lane : 128 * lane + 128]

    def put_rows(ref, t, y, value):
        for h in range(2):
            ref[y, pl.ds(rows_at(h, t), 128), :] = value[128 * h : 128 * h + 128]

    def unpack(ref, field, t):
        for h in range(2):
            for lane in range(2):
                some = field[pl.ds(rows_at(h, t), 128), :, pl.ds(128 * lane, 128)]
                ref[lane, pl.ds(8 * rows_at(h, t), 1024), :] = some.astype(F32).reshape(1024, 128)

    def pack(field, ref):
        for lane in range(2):
            field[:, :, pl.ds(128 * lane, 128)] = ref[lane].reshape(512, 8, 128).astype(BF16)

    def store_pairs(n, t, y, both):
        for h in range(2):
            s_buf[n, t, h, pl.ds(y, 40, stride=8), :] = both[:, 128 * h : 128 * h + 128]

    high, low = split(tx_in[...])
    tx[pl.ds(0, 40), :] = high
    tx[pl.ds(40, 40), :] = low
    ix[...] = stacked_table(ix_in[...])
    loads[0].wait()
    for t in range(2):
        unpack(b0, feat, t)

        def analyse_x(y, carry):
            field = take(b0, t, y).astype(BF16)
            put_rows(fy, t, y, field)
            both = dot(tx[...], field, ((1,), (1,)))
            store_pairs(0, t, y, both[:40] + both[40:])
            return carry

        lax.fori_loop(0, 8, analyse_x, 0)
        fix_zero(0, t)
        if t == 0:
            pl.semaphore_wait(here.at[0], 3)
        px_forward(0, t)
    for t in range(1, 4):
        tell(here.at[1], me, lax.rem(mine + 2 * t, NPY))
    g_buf[:, :, pl.ds(272, 48), :] = jnp.zeros((2, 2, 48, 128), F32)
    g_buf[:, 1, pl.ds(0, 16), :] = jnp.zeros((2, 16, 128), F32)
    sc[...] = jnp.zeros((256, 128), F32)

    txc_high, txc_low = split(txc_in[...])
    pool = ones_where(iota((128, 512), 0) == (iota((128, 512), 1) >> 2))
    for big in range(2):
        total = dot(pool, fy[4 * big])
        for y in range(1, 4):
            total = total + dot(pool, fy[4 * big + y])
        total = total * (1.0 / 64.0)
        rst[big] = total
        high, low = split(total)
        part = dot3(txc_high, txc_low, high, low, ((1,), (1,)))
        sc[pl.ds(big, 64, stride=4), :] = part
    coarse_px(0, sc, rc)

    pl.semaphore_wait(here.at[1], 3)
    tell(here.at[2], me, other)

    wk[...] = kron_eye(rows_of(w_fine[...], 32, 4, 1), 4)
    wkt[...] = kron_eye(rows_of(w_fine[...], 32, 4, 0), 4)

    def local(y, carry):
        put_block(b2, y, dot(wk[...], fy[y]))
        return carry

    lax.fori_loop(0, 8, local, 0)
    loads[1].wait()
    for t in range(2):
        unpack(b1, cot, t)
    low_total = jnp.zeros((128, 128), F32)
    for big in range(2):
        gather = ones_where(iota((256, 128), 1) == 64 * big + (iota((256, 128), 0) >> 2))
        high, low = split(rst[big])
        low_total = low_total + dot(high, gather) + dot(low, gather)
    rst2[...] = low_total
    for n in range(2, 12):
        loads[n].wait()
    for whole, parts in ((ty, ty_s), (tye, tye_s), (zf, zf_s), (zi, zi_s), (ti, ti_s), (tie, tie_s)):
        high, low = split(whole[...])
        parts[0] = high
        parts[1] = low
    base_mask = (iota((128, 1024), 0) >> 2) == ((iota((128, 1024), 1) & 511) >> 4)
    for r in range(2):
        full = jnp.where(base_mask, jnp.concatenate([zfc[r]] * 16, axis=0), 0.0)
        high, low = split(full)
        zfull_h[pl.ds(128 * r, 128), :] = high
        zfull_l[pl.ds(128 * r, 128), :] = low

    def build(step, carry):
        rows = 128 * step + iota((128, 512), 0)
        keep = (rows >> 4) == ((iota((128, 512), 1) & 255) >> 2)
        high, low = split(jnp.where(keep, jnp.concatenate([zic[...]] * 8, axis=0), 0.0))
        at = pl.ds(pl.multiple_of(128 * step, 128), 128)
        zifull_h[at, :] = high
        zifull_l[at, :] = low
        return carry

    lax.fori_loop(0, 8, build, 0)

    pl.semaphore_wait(here.at[2], 1)
    for t in range(2):
        px_forward_wait(0, t)
        forward_yz(0, t)

    coarse_wait(0, rc)
    high, low = split(rc[...])
    along_y = dot3(*split(tyc_in[...]), high, low)
    high, low = split(jnp.concatenate([along_y[:64], along_y[64:]], axis=1))
    full = dot3(high, low, zfull_h[...], zfull_l[...])
    dup = ((iota((64, 512), 0) >> 2) & 1) == 0
    exc[...] = jnp.where(dup, full[:, :512], full[:, 512:]).reshape(8, 8, 512)
    coarse_py(1, lambda p: exc.at[p], rec)

    real, imag = gather_modes(0)
    modes[0] = real
    modes[1] = imag
    out_real, out_imag = mix_modes(spec, real, imag, 32)
    fine_factor = mode_factor(256.0 * 256.0 * 128.0)
    spread_modes(0, out_real * fine_factor, out_imag * fine_factor)

    coarse_wait(1, rec)
    real, imag = to_modes(jnp.sum(rec[...], axis=0), 32)
    high, low = split(jnp.concatenate([real, imag], axis=0))
    lifted = dot(high, lift[...]) + dot(low, lift[...])
    out_real, out_imag = mix_modes(spec_c, lifted[:64], lifted[64:], 64)
    coarse_factor = mode_factor(64.0 * 64.0 * 32.0)
    hc[...] = from_modes(out_real * coarse_factor, out_imag * coarse_factor, 64)
    coarse_py(2, lambda p: hc, ric)

    for t in range(2):
        inverse_zy(0, t, g_buf)

    coarse_wait(2, ric)
    high, low = split(ric[...].reshape(64, 1024))
    along_z = dot3(high, low, zifull_h[...], zifull_l[...])
    high, low = split(jnp.concatenate([along_z[:, :256], along_z[:, 256:]], axis=0))
    along_y = dot3(*split(tic_in[...]), high, low)
    for hh in range(2):
        svc[pl.ds(hh, 128, stride=2), :] = along_y[:, 128 * hh : 128 * hh + 128]
    coarse_px(3, svc, gc)

    for t in range(2):
        px_inverse_wait(0, t)
        g_buf[t, 1, pl.ds(0, 8), :] = g_buf[t, 0, pl.ds(8, 8), :]

        def middle(y, carry):
            value = jnp.concatenate([g_buf[t, h, pl.ds(y, 40, stride=8), :] for h in range(2)], axis=1)
            pre = some_rows(b2, t, y) + synthesise_x(value, ix[...])
            square = pre * pre
            tanh = jnp.tanh(ROOT * pre * (1.0 + 0.044715 * square))
            half = 0.5 * (1.0 + tanh)
            put_part(b0, t, y, pre * half)
            slope = half + 0.5 * pre * (1.0 - tanh * tanh) * (ROOT + (3.0 * 0.044715 * ROOT) * square)
            high, low = split(take(b1, t, y) * slope)
            put_rows(gph, t, y, high)
            put_rows(gpl, t, y, low)
            both = dot(tx[...], high, ((1,), (1,)))
            store_pairs(1, t, y, both[:40] + both[40:] + dot(tx[pl.ds(0, 40), :], low, ((1,), (1,))))
            return carry

        lax.fori_loop(0, 8, middle, 0)
        fix_zero(1, t)
        px_forward(1, t)

    def direct(y, carry):
        put_block(b1, y, dot(wkt[...], gph[y]) + dot(wkt[...], gpl[y]))
        return carry

    lax.fori_loop(0, 8, direct, 0)
    writes = [pltpu.make_async_copy(b1, dir_hbm, out_sem.at[0])]
    writes[0].start()

    coarse_wait(3, gc)
    halves_out = []
    for hh in range(2):
        high, low = split(gc[pl.ds(hh, 128, stride=2), :].T)
        halves_out.append(dot3(high, low, *split(ixc_in[...])))
    spectral_part = jnp.concatenate(halves_out, axis=0)
    lift_wide = kron_eye(rows_of(lift[...], 64, 2, 1), 2)
    coarse_wide = kron_eye(rows_of(w_coarse[...], 64, 2, 1), 2)
    project_wide = kron_eye(rows_of(project[...], 32, 2, 0), 2)
    high, low = split(rst2[...])
    lifted = dot(lift_wide, high) + dot(lift_wide, low)
    high, low = split(lifted)
    coarse_pre = spectral_part + dot(coarse_wide, high) + dot(coarse_wide, low)
    high, low = split(tanh_gelu(coarse_pre))
    coarse_out = dot(project_wide, high) + dot(project_wide, low)
    out_high, out_low = split(coarse_out)
    widen = ones_where((iota((512, 128), 0) >> 2) == iota((512, 128), 1))
    for big in range(2):
        stretch = ones_where(iota((128, 256), 0) == 64 * big + (iota((128, 256), 1) >> 2))
        high, low = split(dot(out_high, stretch) + dot(out_low, stretch))
        prolonged = dot(widen, high) + dot(widen, low)
        for small in range(4):
            y = 4 * big + small
            put(b2, y, block(b0, y) + prolonged)
    pack(layer_out, b2)
    writes.append(pltpu.make_async_copy(layer_out, layer_hbm, out_sem.at[1]))
    writes[1].start()

    for t in range(2):
        px_forward_wait(1, t)
        forward_yz(1, t)
    real, imag = gather_modes(1)
    real, imag = real * fine_factor, imag * fine_factor
    lane = iota((64, 32), 1)
    pull_real = jnp.zeros((64, 32), F32)
    pull_imag = jnp.zeros((64, 32), F32)
    for i in range(32):
        w0, w1 = spec[0, i], spec[1, i]
        a = jnp.sum(w0 * real + w1 * imag, axis=1, keepdims=True)
        b = jnp.sum(w0 * imag - w1 * real, axis=1, keepdims=True)
        pull_real = jnp.where(lane == i, a, pull_real)
        pull_imag = jnp.where(lane == i, b, pull_imag)
    spread_modes(1, pull_real, pull_imag)
    x_real, x_imag = modes[0], modes[1]
    for i in range(32):
        a, b = column(x_real, i), column(x_imag, i)
        gspec[0, i] = real * a + imag * b
        gspec[1, i] = imag * a - real * b
    writes.append(pltpu.make_async_copy(gspec, gspec_hbm, out_sem.at[2]))
    writes[2].start()
    for t in range(2):
        inverse_zy(1, t, g_hbm)
    for t in range(2):
        px_inverse_wait(1, t)

    for write in writes:
        write.wait()
    for k in range(8):
        most = rx.at[0, 0, pl.ds(0, 496)]
        pltpu.make_async_copy(most, most, px_send.at[k]).wait()
        if k % 4 < 2:

            @pl.when(is16 == 0)
            def _():
                some = rx.at[0, 0, pl.ds(0, 16)]
                pltpu.make_async_copy(some, some, pxe_send.at[k]).wait()

        else:

            @pl.when(is16 == 1)
            def _():
                pltpu.make_async_copy(most, most, pxe_send.at[k]).wait()

    for slot in range(8):
        some = ex.at[0, 0, pl.ds(0, 14)]
        pltpu.make_async_copy(some, some, py_send.at[slot]).wait()

        @pl.when(regular == 1)
        def _():
            pltpu.make_async_copy(ex.at[0, 0, 0], ex.at[0, 0, 0], pye_send.at[slot]).wait()

    for slot, most in ((0, rc.at[pl.ds(0, 248)]), (1, exc.at[pl.ds(0, 7)]), (2, ric.at[pl.ds(0, 7)]), (3, gc.at[pl.ds(0, 248)])):
        pltpu.make_async_copy(most, most, c_send.at[slot]).wait()


def finish(g_ref, zero_ref, dir_ref, layer_ref, gspec_ref, ix_in, layer_out, grad_out, gspec_out, kept, mixed):
    second = pl.program_id(0) >= 2
    rows = iota((PAIRS, 128), 0)
    value = jnp.where(rows < 272, g_ref[0, 0], 0.0)
    zero = jnp.concatenate([zero_ref[0, 0], jnp.zeros((PAIRS - 8, 128), F32)], axis=0)
    kept[...] = jnp.where(jnp.logical_and(second, rows < 16), zero, value)
    table = stacked_table(ix_in[...])

    for y in range(8):
        some = synthesise_x(kept[pl.ds(y, 40, stride=8), :], table)
        for lane in range(2):
            at = slice(128 * lane, 128 * lane + 128)
            mixed[lane, pl.ds(y, 128, stride=8), :] = some[:, at] + dir_ref[lane, y]
    for lane in range(2):
        grad_out[:, :, pl.ds(128 * lane, 128)] = mixed[lane].reshape(128, 8, 128).astype(BF16)
    layer_out[...] = layer_ref[...]
    gspec_out[...] = gspec_ref[...]


def body(
    features, cotangent, pointwise_fine, spectral_fine, lift_weight, pointwise_coarse,
    spectral_coarse, project_weight,
):
    table = tables()
    fine = spectral_fine.transpose(0, 1, 3, 4, 5, 2).reshape(2, 32, 64, 32)
    coarse = spectral_coarse.transpose(0, 1, 3, 4, 5, 2).reshape(2, 64, 64, 64)
    vmem = pl.BlockSpec(memory_space=pltpu.VMEM)
    hbm = pl.BlockSpec(memory_space=pl.ANY)

    def f32(*shape):
        return pltpu.VMEM(shape, F32)

    def bf16(*shape):
        return pltpu.VMEM(shape, BF16)

    dma = pltpu.SemaphoreType.DMA
    layer, direct, gspec, spectrum = pl.pallas_call(
        kernel,
        out_shape=[
            jax.ShapeDtypeStruct((512, 8, 256), BF16),
            jax.ShapeDtypeStruct((2, 4096, 128), F32),
            jax.ShapeDtypeStruct((2, 32, 64, 32), F32),
            jax.ShapeDtypeStruct((2, 2, PAIRS, 128), F32),
        ],
        in_specs=[hbm, hbm, vmem, hbm, vmem, vmem, hbm, vmem, vmem, vmem, hbm, hbm, hbm, hbm, vmem, vmem, hbm, hbm, vmem, vmem],
        out_specs=[hbm] * 4,
        scratch_shapes=[
            f32(2, 4096, 128), f32(2, 4096, 128), f32(2, 4096, 128),
            bf16(8, 512, 256), bf16(8, 512, 256), bf16(8, 512, 256),
            bf16(512, 8, 256), bf16(512, 8, 256), f32(2, 32, 64, 32), f32(2, 64, 64, 64),
            bf16(512, 8, 256), f32(2, 32, 64, 32),
            f32(256, 512), f32(256, 512), f32(256, 256), f32(128, 256),
            f32(512, 256), f32(512, 256), f32(2, 8, 1024), f32(16, 512),
            bf16(256, 1024), bf16(256, 1024), bf16(1024, 512), bf16(1024, 512),
            bf16(80, 256), bf16(128, 256), bf16(2, 256, 512), bf16(2, 256, 512), bf16(2, 256, 256), bf16(2, 128, 256),
            bf16(2, 512, 256), bf16(2, 512, 256),
            bf16(512, 512), bf16(512, 512), f32(256, 128), f32(2, 128, 256), f32(128, 128), f32(2, 64, 32),
            f32(2, 2, 2, PAIRS, 128), f32(2, 2, 512, 128), f32(2, 2, 512, 128), f32(2, 2, 16, 8, 128), f32(2, 2, 16, 8, 128),
            f32(2, 2, 2, 8, 128), f32(2, 2, 16, 8, 128), f32(2, 2, 512, 128), f32(2, 2, 512, 128), f32(2, 2, PAIRS, 128),
            f32(256, 128), f32(256, 128), f32(8, 8, 512), f32(8, 8, 512), f32(8, 1024), f32(8, 8, 1024),
            f32(256, 128), f32(256, 128),
            dma((12,)), dma((3,)), dma((8,)), dma((8,)), dma((8,)), dma((8,)), dma((8,)), dma((8,)), dma((8,)),
            dma((4,)), dma((4,)), pltpu.SemaphoreType.REGULAR((3,)),
        ],
        compiler_params=pltpu.CompilerParams(
            collective_id=0, has_side_effects=True, vmem_limit_bytes=60 * 1024 * 1024
        ),
        name="fno_layer",
    )(
        features.reshape(512, 8, 256), cotangent.reshape(512, 8, 256), pointwise_fine, fine, lift_weight,
        pointwise_coarse, coarse, project_weight.T,
        table["tx"], table["ix"], table["ty"], table["zf"], table["zi"], table["ti"], table["txc"], table["tyc"],
        table["zfc"], table["zic"], table["tic"], table["ixc"],
    )
    layer_out, grad_out, gspec = pl.pallas_call(
        finish,
        grid=(4,),
        out_shape=[
            jax.ShapeDtypeStruct((512, 8, 256), BF16),
            jax.ShapeDtypeStruct((512, 8, 256), BF16),
            jax.ShapeDtypeStruct((2, 32, 64, 32), F32),
        ],
        in_specs=[
            pl.BlockSpec((1, 1, PAIRS, 128), lambda i: (i % 2, i // 2, 0, 0)),
            pl.BlockSpec((1, 1, 8, 128), lambda i: (i % 2, 0, 1, 0)),
            pl.BlockSpec((2, 8, 128, 128), lambda i: (0, 0, i, 0)),
            pl.BlockSpec((128, 8, 256), lambda i: (i, 0, 0)),
            pl.BlockSpec((2, 8, 64, 32), lambda i: (0, i, 0, 0)),
            pl.BlockSpec((40, 256), lambda i: (0, 0)),
        ],
        out_specs=[
            pl.BlockSpec((128, 8, 256), lambda i: (i, 0, 0)),
            pl.BlockSpec((128, 8, 256), lambda i: (i, 0, 0)),
            pl.BlockSpec((2, 8, 64, 32), lambda i: (0, i, 0, 0)),
        ],
        scratch_shapes=[f32(PAIRS, 128), f32(2, 1024, 128)],
        compiler_params=pltpu.CompilerParams(vmem_limit_bytes=60 * 1024 * 1024),
        name="finish",
    )(spectrum, spectrum, direct.reshape(2, 8, 512, 128), layer, gspec, table["ix"])
    shape = (32, 16, 8, 256)
    gspec = gspec.reshape(2, 32, 16, 1, 4, 32).transpose(0, 1, 5, 2, 3, 4)
    return layer_out.reshape(shape), grad_out.reshape(shape), gspec


def solution(mesh):
    placed = (
        P(None, "py", "px", None),
        P(None, "py", "px", None),
        P(),
        P(None, None, None, None, "px", "py"),
        P(),
        P(),
        P(None, None, None, None, "px", "py"),
        P(),
    )
    return jax.shard_map(
        body,
        mesh=mesh,
        in_specs=placed,
        out_specs=(
            P(None, "py", "px", None),
            P(None, "py", "px", None),
            P(None, None, None, None, "px", "py"),
        ),
        check_vma=False,
    )
```

```python
import functools
import math

import jax
import jax.numpy as jnp
import numpy as np
from jax import lax
from jax.experimental import pallas as pl
from jax.experimental.pallas import tpu as pltpu
from jax.sharding import PartitionSpec as P

M = 16
F32 = jnp.float32
BF16 = jnp.bfloat16
MESH = pl.DeviceIdType.MESH
NPX, NPY = 32, 8
PAIRS = 320
ROOT = math.sqrt(2.0 / math.pi)


def single(table):
    return np.asarray(table, np.float64).astype(np.float32)


def signed(index):
    return np.where(index < M, index, index - 2 * M)


def turn(freq, cell, count):
    return (np.asarray(freq) * np.asarray(cell) % count) * (2.0 * np.pi / count)


@functools.cache
def tables():
    out = {}
    x = np.arange(256)
    rows = np.zeros((40, 256))
    for j in range(17):
        angle = turn(j, x, 256)
        if j == 0:
            rows[0] = rows[1] = 1.0
        else:
            rows[2 * j] = np.cos(angle)
            rows[2 * j + 1] = -np.sin(angle) if j < 16 else np.sin(angle)
    out["tx"] = single(rows)
    inv = rows.copy()
    inv[1] = 0.0
    out["ix"] = single(inv)

    ky = np.arange(32)
    theta = turn(signed(ky)[:, None], np.arange(256)[None, :], 256)
    cos, sin = np.cos(theta), np.sin(theta)
    zero = np.zeros_like(cos)
    plus = (((cos, sin), (-sin, cos)))
    minus = (((cos, -sin), (-sin, -cos)))
    from0 = (((cos, zero), (-sin, zero)))
    from1 = (((zero, cos), (zero, -sin)))
    none = (((zero, zero), (zero, zero)))
    kinds = [(plus, minus), (minus, plus), (from0, from1), (plus, none), (none, plus)]
    ty = np.zeros((5, 2, 2, 8, 2, 4, 32, 2, 8))
    for k, pair in enumerate(kinds):
        for q in range(2):
            for r1 in range(2):
                for r in range(2):
                    block = pair[q][r1][r].reshape(8, 4, 32, 8)
                    for dup in range(2):
                        ty[k, r1, q, :, dup, :, :, r, :] = block
    ty = ty.reshape(5, 256, 512)
    out["ty"] = single(ty)

    ti = np.zeros((5, 32, 2, 8, 2, 2, 8, 2, 4))

    def add(k, rout, q, part, sign):
        c = cos.T.reshape(32, 8, 8, 4)
        s = sin.T.reshape(32, 8, 8, 4)
        if part == 0:
            coef = {(0, 0): c, (1, 1): -c, (0, 1): -s, (1, 0): -s}
        else:
            coef = {(0, 0): s, (1, 1): -s, (0, 1): c, (1, 0): c}
        for (cs, r), value in coef.items():
            ti[k, :, rout, :, cs, q, :, r, :] += sign * value

    for k, first in ((0, 1.0), (1, -1.0)):
        add(k, 0, 0, 0, 1.0)
        add(k, 0, 1, 0, 1.0)
        add(k, 1, 0, 1, first)
        add(k, 1, 1, 1, -first)
    add(2, 0, 0, 0, 1.0)
    add(2, 1, 1, 0, 1.0)
    for k, q in ((3, 0), (4, 1)):
        add(k, 0, q, 0, 1.0)
        add(k, 1, q, 1, 1.0)
    out["ti"] = single(ti.reshape(5, 512, 256))

    kz = np.arange(16)
    zf = np.zeros((8, 2, 8, 16, 2, 8, 16))
    zi = np.zeros((8, 8, 16, 2, 8, 16))
    for b in range(8):
        phi = turn(kz[None, :], (b * 16 + np.arange(16))[:, None], 128)
        for c in range(8):
            zf[b, 0, c, :, 0, c, :] = np.cos(phi)
            zf[b, 1, c, :, 0, c, :] = np.sin(phi)
            zf[b, 0, c, :, 1, c, :] = -np.sin(phi)
            zf[b, 1, c, :, 1, c, :] = np.cos(phi)
            zi[b, c, :, 0, c, :] = np.cos(phi).T
            zi[b, c, :, 1, c, :] = np.sin(phi).T
    out["zf"] = single(zf.reshape(8, 256, 256))
    out["zi"] = single(zi.reshape(8, 128, 256))

    kx = np.arange(32)
    alpha = turn(signed(kx)[:, None], (x // 4)[None, :], 64)
    txc = np.stack([np.cos(alpha), -np.sin(alpha)], axis=1).reshape(64, 256)
    out["txc"] = single(txc)
    theta = turn(signed(ky)[:, None], np.arange(64)[None, :], 64)
    cos, sin = np.cos(theta), np.sin(theta)
    tyc = np.zeros((2, 8, 2, 4, 32, 2, 4))
    plus = ((cos, sin), (-sin, cos))
    for r1 in range(2):
        for r in range(2):
            for dup in range(2):
                tyc[r1, :, dup, :, :, r, :2] = plus[r1][r].reshape(8, 4, 32, 2)
    out["tyc"] = single(tyc.reshape(128, 256))
    tic = np.zeros((32, 2, 2, 2, 8, 2, 4))
    c = cos.T.reshape(32, 2, 8, 4)
    s = sin.T.reshape(32, 2, 8, 4)
    for (rout, cs, r), value in {
        (0, 0, 0): c, (0, 1, 1): -c, (0, 0, 1): -s, (0, 1, 0): -s,
        (1, 0, 0): s, (1, 1, 1): -s, (1, 0, 1): c, (1, 1, 0): c,
    }.items():
        tic[:, rout, :, cs, :, r, :] = value
    out["tic"] = single(tic.reshape(128, 128))
    zfc = np.zeros((8, 2, 2, 4, 2, 32, 16))
    zic = np.zeros((8, 16, 2, 64, 4))
    for b in range(8):
        phi = turn(kz[None, :], (b * 4 + np.arange(4))[:, None], 32)
        zfc[b, 0, :, :, 0] = np.cos(phi)[None, :, None, :]
        zfc[b, 1, :, :, 0] = np.sin(phi)[None, :, None, :]
        zfc[b, 0, :, :, 1] = -np.sin(phi)[None, :, None, :]
        zfc[b, 1, :, :, 1] = np.cos(phi)[None, :, None, :]
        zic[b, :, 0] = np.cos(phi).T[:, None, :]
        zic[b, :, 1] = np.sin(phi).T[:, None, :]
    out["zfc"] = single(zfc.reshape(8, 2, 8, 1024))
    out["zic"] = single(zic.reshape(8, 16, 512))
    alpha = turn(signed(kx)[:, None], np.arange(64)[None, :], 64)
    ixc = np.zeros((32, 2, 2, 2, 64))
    for big in range(2):
        ixc[:, 0, big, big] = np.cos(alpha)
        ixc[:, 1, big, big] = -np.sin(alpha)
    out["ixc"] = single(ixc.reshape(128, 128))
    return out


def split(value):
    high = value.astype(BF16)
    return high, (value - high.astype(F32)).astype(BF16)


def dot(left, right, dims=((1,), (0,))):
    return lax.dot_general(left, right, (dims, ((), ())), preferred_element_type=F32)


def dot3(left_high, left_low, right_high, right_low, dims=((1,), (0,))):
    return (
        dot(left_high, right_high, dims)
        + dot(left_high, right_low, dims)
        + dot(left_low, right_high, dims)
    )


def iota(shape, dim):
    return lax.broadcasted_iota(jnp.int32, shape, dim)


def ones_where(condition):
    return jnp.where(condition, 1.0, 0.0).astype(BF16)


def kron_eye(first, shift):
    rows, m = first.shape
    spread = ones_where(iota((m, m << shift), 0) == (iota((m, m << shift), 1) >> shift))
    full = dot(first.astype(BF16), spread)
    low = (1 << shift) - 1
    shape = (rows, m << shift)
    return jnp.where((iota(shape, 0) & low) == (iota(shape, 1) & low), full, 0.0).astype(BF16)


def rows_of(weight, n, shift, axis):
    pick = ones_where((iota((n << shift, n), 0) >> shift) == iota((n << shift, n), 1))
    return dot(pick, weight, ((1,), (axis,)))


def to_modes(packed, count):
    lanes = count * 16
    real = jnp.concatenate([packed[0:4]] * 16, axis=0)
    imag = jnp.concatenate([packed[4:8]] * 16, axis=0)
    mask = (iota((64, lanes), 0) >> 2) == (iota((64, lanes), 1) & 15)
    wide = jnp.concatenate([jnp.where(mask, real, 0.0), jnp.where(mask, imag, 0.0)], axis=0)
    pick = ones_where((iota((lanes, count), 0) >> 4) == iota((lanes, count), 1))
    high, low = split(wide)
    modes = dot(high, pick) + dot(low, pick)
    return modes[:64], modes[64:]


def from_modes(real, imag, count):
    lanes = count * 16
    high, low = split(jnp.concatenate([real, imag], axis=0))
    spread = ones_where(iota((count, lanes), 0) == (iota((count, lanes), 1) >> 4))
    wide = dot(high, spread) + dot(low, spread)
    mask = ((iota((128, lanes), 0) & 63) >> 2) == (iota((128, lanes), 1) & 15)
    high, low = split(jnp.where(mask, wide, 0.0))
    shape = (8, 128)
    total = ones_where(
        ((iota(shape, 1) >> 6) == (iota(shape, 0) >> 2)) & ((iota(shape, 1) & 3) == (iota(shape, 0) & 3))
    )
    return dot(total, high) + dot(total, low)


def column(values, index):
    return values[:, index : index + 1]


def mix_modes(weight_ref, real, imag, count):
    out_real = jnp.zeros((64, count), F32)
    out_imag = jnp.zeros((64, count), F32)
    for i in range(count):
        w0, w1 = weight_ref[0, i], weight_ref[1, i]
        a, b = column(real, i), column(imag, i)
        out_real = out_real + (w0 * a - w1 * b)
        out_imag = out_imag + (w0 * b + w1 * a)
    return out_real, out_imag


def mode_factor(cells):
    return jnp.where(iota((64, 1), 0) < 4, 1.0 / cells, 2.0 / cells).astype(F32)


def stacked_table(table):
    high, low = split(table)
    high, low = high.astype(F32), low.astype(F32)
    return jnp.concatenate([high, high, low, jnp.zeros((8, 256), F32)], axis=0).astype(BF16)


def synthesise_x(value, table):
    high = value.astype(BF16).astype(F32)
    pad = jnp.zeros((8, value.shape[1]), F32)
    stacked = jnp.concatenate([high, value - high, high, pad], axis=0)
    return dot(stacked.T.astype(BF16), table)


def tanh_gelu(value):
    return 0.5 * value * (1.0 + jnp.tanh(ROOT * (value + 0.044715 * value * value * value)))


def kernel(
    feat_hbm, cot_hbm, w_fine_hbm, spec_hbm, lift_hbm, w_coarse_hbm, spec_c_hbm, project_hbm,
    tx_hbm, ix_hbm, ty_hbm, zf_hbm, zi_hbm, ti_hbm, txc_hbm, tyc_hbm, zfc_hbm, zic_hbm, tic_hbm, ixc_hbm,
    layer_hbm, dir_hbm, gspec_hbm, g_hbm,
    w_fine, lift, w_coarse, project, tx_in, ix_in, txc_in, tyc_in, tic_in, ixc_in,
    b0, b1, b2, fy, gph, gpl, feat, cot, spec, spec_c, layer_out, gspec,
    ty, tye, zf, zi, ti, tie, zfc, zic, zfull_h, zfull_l, zifull_h, zifull_l,
    tx, ix, ty_s, tye_s, zf_s, zi_s, ti_s, tie_s,
    wk, wkt, yc, rst, rst2, modes,
    s_buf, rx, rxe, ex, re_buf, hq, ri, sv, sve, g_buf,
    sc, rc, exc, rec, hc, ric, svc, gc,
    load_sem, out_sem, px_send, px_recv, pxe_send, pxe_recv, py_send, py_recv, pye_send,
    c_send, c_recv, here,
):
    me = lax.axis_index("px")
    mine = lax.axis_index("py")
    partner = lax.rem(NPX - me, NPX)
    upper = lax.div(me + 15, 32)
    is0 = 1 - lax.div(me + 31, 32)
    is16 = lax.div(me, 16) * (1 - upper)
    kind = upper + 2 * is0 + 3 * is16
    regular = 1 - is0 - is16

    loads = [
        (feat_hbm, feat), (tx_hbm, tx_in), (ix_hbm, ix_in), (txc_hbm, txc_in), (w_fine_hbm, w_fine),
        (lift_hbm, lift), (w_coarse_hbm, w_coarse), (project_hbm, project), (tyc_hbm, tyc_in),
        (tic_hbm, tic_in), (ixc_hbm, ixc_in),
        (cot_hbm, cot), (spec_hbm, spec), (spec_c_hbm, spec_c),
        (ty_hbm.at[kind], ty), (ty_hbm.at[4], tye), (zf_hbm.at[mine], zf), (zi_hbm.at[mine], zi),
        (ti_hbm.at[kind], ti), (ti_hbm.at[4], tie), (zfc_hbm.at[mine], zfc), (zic_hbm.at[mine], zic),
    ]
    loads = [pltpu.make_async_copy(a, b, load_sem.at[n]) for n, (a, b) in enumerate(loads)]
    for load in loads[:4]:
        load.start()

    barrier = pltpu.get_barrier_semaphore()
    row = 8 * lax.div(me, 8)

    def tell(semaphore, px, py):
        pl.semaphore_signal(semaphore, inc=1, device_id={"px": px, "py": py}, device_id_type=MESH)

    for t in range(1, 8):
        tell(barrier, row + lax.rem(me + t, 8), mine)
    for t in range(1, 4):
        tell(barrier, lax.rem(me + 8 * t, NPX), mine)
    for t in range(1, 4):
        tell(barrier, me, lax.rem(mine + 2 * t, NPY))
    other = 2 * lax.div(mine, 2) + 1 - lax.rem(mine, 2)
    tell(barrier, me, other)
    for load in loads[4:]:
        load.start()
    pl.semaphore_wait(barrier, 14)
    for t in range(1, 4):
        tell(here.at[0], lax.rem(me + 8 * t, NPX), mine)

    def pair_row(d):
        h = lax.div(d + 15, 32)
        return h, pl.multiple_of(16 * (d * (1 - 2 * h) + 32 * h), 16)

    pending = []

    def left(semaphore, ref, condition=None):
        def wait():
            pltpu.make_async_copy(ref, ref, semaphore).wait()

        pending.append(wait if condition is None else lambda: pl.when(condition)(wait))

    slab, side = lax.div(mine, 2), lax.rem(mine, 2)

    def each_px(send):
        def step(t, carry):
            send(lax.rem(me + t, NPX))
            return carry

        lax.fori_loop(1, NPX, step, 0)

    def each_py(send):
        for far, ahead in ((1, 2), (1, 1), (1, 3), (1, 0), (0, 2), (0, 1), (0, 3)):
            send(2 * lax.rem(slab + ahead, 4) + (1 - side if far else side))

    def at16(d):
        return pl.ds(pl.multiple_of(16 * d, 16), 16)

    def px_forward(n, t):
        k = 4 * n + t
        left(px_send.at[k], rx.at[0, 0, pl.ds(0, 496)])
        left(pxe_send.at[k], rx.at[0, 0, pl.ds(0, 16)], is16 == 0)

        def send(d):
            h, row = pair_row(d)
            pltpu.make_async_remote_copy(
                s_buf.at[n, t, h, pl.ds(row, 16)], rx.at[n, t, at16(me)],
                px_send.at[k], px_recv.at[k], device_id={"px": d, "py": mine}, device_id_type=MESH,
            ).start()

        each_px(send)
        h, row = pair_row(me)
        pltpu.make_async_copy(s_buf.at[n, t, h, pl.ds(row, 16)], rx.at[n, t, at16(me)], px_recv.at[k]).start()

        @pl.when(is16 == 0)
        def _():
            pltpu.make_async_remote_copy(
                s_buf.at[n, t, 1, pl.ds(256, 16)], rxe.at[n, t, at16(me)],
                pxe_send.at[k], pxe_recv.at[k], device_id={"px": 16, "py": mine}, device_id_type=MESH,
            ).start()

        @pl.when(is16 == 1)
        def _():
            pltpu.make_async_copy(
                s_buf.at[n, t, 1, pl.ds(256, 16)], rxe.at[n, t, at16(me)], pxe_recv.at[k]
            ).start()

    def px_forward_wait(n, t):
        k = 4 * n + t
        pltpu.make_async_copy(rx.at[n, t], rx.at[n, t], px_recv.at[k]).wait()

        @pl.when(is16 == 1)
        def _():
            pltpu.make_async_copy(rxe.at[n, t], rxe.at[n, t], pxe_recv.at[k]).wait()

    def px_inverse(n, t, target):
        k = 4 * n + 2 + t
        left(px_send.at[k], rx.at[0, 0, pl.ds(0, 496)])
        left(pxe_send.at[k], rx.at[0, 0, pl.ds(0, 496)], is16 == 1)
        h, row = pair_row(me)

        def send(d):
            pltpu.make_async_remote_copy(
                sv.at[n, t, at16(d)], target.at[t, h, pl.ds(row, 16)],
                px_send.at[k], px_recv.at[k], device_id={"px": d, "py": mine}, device_id_type=MESH,
            ).start()

        each_px(send)
        pltpu.make_async_copy(sv.at[n, t, at16(me)], target.at[t, h, pl.ds(row, 16)], px_recv.at[k]).start()

        @pl.when(is16 == 1)
        def _():
            def send_extra(d):
                pltpu.make_async_remote_copy(
                    sve.at[n, t, at16(d)], target.at[t, 1, pl.ds(256, 16)],
                    pxe_send.at[k], pxe_recv.at[k], device_id={"px": d, "py": mine}, device_id_type=MESH,
                ).start()

            each_px(send_extra)
            pltpu.make_async_copy(sve.at[n, t, at16(me)], target.at[t, 1, pl.ds(256, 16)], pxe_recv.at[k]).start()

    def px_inverse_wait(n, t):
        k = 4 * n + 2 + t
        pltpu.make_async_copy(rx.at[n, t], rx.at[n, t], px_recv.at[k]).wait()
        some = rx.at[n, t, pl.ds(0, 16)]
        pltpu.make_async_copy(some, some, pxe_recv.at[k]).wait()

    def py_exchange(slot, source, target):
        left(py_send.at[slot], ex.at[0, 0, pl.ds(0, 14)])
        left(pye_send.at[slot], ex.at[0, 0, 0], regular == 1)

        def send(p):
            for q, to in ((1, partner), (0, me)):
                pltpu.make_async_remote_copy(
                    source(q, p), target.at[8 * q + mine], py_send.at[slot], py_recv.at[slot],
                    device_id={"px": to, "py": p}, device_id_type=MESH,
                ).start()

        each_py(send)
        pltpu.make_async_copy(source(0, mine), target.at[mine], py_recv.at[slot]).start()

        @pl.when(regular == 1)
        def _():
            pltpu.make_async_remote_copy(
                source(1, mine), target.at[8 + mine], pye_send.at[slot], py_recv.at[slot],
                device_id={"px": partner, "py": mine}, device_id_type=MESH,
            ).start()

        @pl.when(regular == 0)
        def _():
            pltpu.make_async_copy(source(1, mine), target.at[8 + mine], py_recv.at[slot]).start()

    def py_wait(slot, target):
        pltpu.make_async_copy(target, target, py_recv.at[slot]).wait()

    def coarse_px(slot, source, target):
        left(c_send.at[slot], target.at[pl.ds(0, 248)])
        there = target.at[pl.ds(pl.multiple_of(8 * me, 8), 8)]

        def send(d):
            pltpu.make_async_remote_copy(
                source.at[pl.ds(pl.multiple_of(8 * d, 8), 8)], there, c_send.at[slot], c_recv.at[slot],
                device_id={"px": d, "py": mine}, device_id_type=MESH,
            ).start()

        each_px(send)
        pltpu.make_async_copy(source.at[pl.ds(pl.multiple_of(8 * me, 8), 8)], there, c_recv.at[slot]).start()

    def coarse_py(slot, source, target):
        left(c_send.at[slot], target.at[pl.ds(0, 7)])

        def send(p):
            pltpu.make_async_remote_copy(
                source(p), target.at[mine], c_send.at[slot], c_recv.at[slot],
                device_id={"px": me, "py": p}, device_id_type=MESH,
            ).start()

        each_py(send)
        pltpu.make_async_copy(source(mine), target.at[mine], c_recv.at[slot]).start()

    def coarse_wait(slot, target):
        pltpu.make_async_copy(target, target, c_recv.at[slot]).wait()

    def fix_zero(n, t):
        s_buf[n, t, 0, pl.ds(8, 8), :] = s_buf[n, t, 1, pl.ds(0, 8), :]

    def forward_yz(n, t):
        high, low = split(rx[n, t])
        yc[...] = dot3(ty_s[0], ty_s[1], high, low)

        @pl.when(is16 == 1)
        def _():
            high, low = split(rxe[n, t])
            yc[...] += dot3(tye_s[0], tye_s[1], high, low)

        dup = ((iota((128, 128), 0) >> 2) & 1) == 0
        both = jnp.concatenate([yc[pl.ds(0, 128), :], yc[pl.ds(128, 128), :]], axis=1)
        high, low = split(both)
        full = dot3(high, low, zf_s[0], zf_s[1])
        ex[n, t] = jnp.where(dup, full[:, :128], full[:, 128:]).reshape(16, 8, 128)
        py_exchange(4 * n + t, lambda q, p: ex.at[n, t, 8 * q + p], re_buf.at[n, t])

    def gather_modes(n):
        slots = []
        for q in range(2):
            parts = []
            for t in range(2):
                if q == 0:
                    py_wait(4 * n + t, re_buf.at[n, t])
                parts.append(jnp.sum(re_buf[n, t, 8 * q : 8 * q + 8], axis=0))
            slots.append(jnp.concatenate(parts, axis=1))
        swap = upper == 1
        first = jnp.where(swap, slots[1], slots[0])
        second = jnp.where(swap, slots[0], slots[1])
        return to_modes(jnp.concatenate([first, second], axis=1), 32)

    def spread_modes(n, real, imag):
        packed = from_modes(real, imag, 32)
        swap = upper == 1
        for t in range(2):
            first, second = packed[:, 128 * t : 128 * t + 128], packed[:, 256 + 128 * t : 384 + 128 * t]
            hq[n, t, 0] = jnp.where(swap, second, first)
            hq[n, t, 1] = jnp.where(swap, first, second)
            py_exchange(4 * n + 2 + t, lambda q, p: hq.at[n, t, q], ri.at[n, t])

    def inverse_zy(n, t, target):
        py_wait(4 * n + 2 + t, ri.at[n, t])
        high, low = split(ri[n, t].reshape(128, 128))
        full = dot3(high, low, zi_s[0], zi_s[1])
        high, low = split(jnp.concatenate([full[:, :128], full[:, 128:]], axis=0))
        sv[n, t] = dot3(ti_s[0], ti_s[1], high, low)

        @pl.when(is16 == 1)
        def _():
            sve[n, t] = dot3(tie_s[0], tie_s[1], high, low)

        px_inverse(n, t, target)

    def rows_at(h, t):
        return 256 * h + 128 * t

    def take(ref, t, y):
        return jnp.concatenate(
            [
                jnp.concatenate(
                    [ref[lane, pl.ds(8 * rows_at(h, t) + y, 128, stride=8), :] for lane in range(2)], axis=1
                )
                for h in range(2)
            ],
            axis=0,
        )

    def put(ref, y, value):
        for lane in range(2):
            ref[lane, pl.ds(y, 512, stride=8), :] = value[:, 128 * lane : 128 * lane + 128]

    def block(ref, y):
        rows = pl.ds(pl.multiple_of(512 * y, 512), 512)
        return jnp.concatenate([ref[0, rows, :], ref[1, rows, :]], axis=1)

    def put_block(ref, y, value):
        rows = pl.ds(pl.multiple_of(512 * y, 512), 512)
        ref[0, rows, :] = value[:, :128]
        ref[1, rows, :] = value[:, 128:]

    def part_rows(h, t, y):
        return pl.ds(pl.multiple_of(512 * y + rows_at(h, t), 128), 128)

    def some_rows(ref, t, y):
        return jnp.concatenate(
            [
                jnp.concatenate([ref[lane, part_rows(h, t, y), :] for lane in range(2)], axis=1)
                for h in range(2)
            ],
            axis=0,
        )

    def put_part(ref, t, y, value):
        for h in range(2):
            for lane in range(2):
                ref[lane, part_rows(h, t, y), :] = value[128 * h : 128 * h + 128, 128 * lane : 128 * lane + 128]

    def put_rows(ref, t, y, value):
        for h in range(2):
            ref[y, pl.ds(rows_at(h, t), 128), :] = value[128 * h : 128 * h + 128]

    def unpack(ref, field, t):
        for h in range(2):
            for lane in range(2):
                some = field[pl.ds(rows_at(h, t), 128), :, pl.ds(128 * lane, 128)]
                ref[lane, pl.ds(8 * rows_at(h, t), 1024), :] = some.astype(F32).reshape(1024, 128)

    def pack(field, ref):
        for lane in range(2):
            field[:, :, pl.ds(128 * lane, 128)] = ref[lane].reshape(512, 8, 128).astype(BF16)

    def store_pairs(n, t, y, both):
        for h in range(2):
            s_buf[n, t, h, pl.ds(y, 40, stride=8), :] = both[:, 128 * h : 128 * h + 128]

    for n in range(4):
        loads[n].wait()
    high, low = split(tx_in[...])
    tx[pl.ds(0, 40), :] = high
    tx[pl.ds(40, 40), :] = low
    ix[...] = stacked_table(ix_in[...])
    for t in range(2):
        unpack(b0, feat, t)

        def analyse_x(y, carry):
            field = take(b0, t, y).astype(BF16)
            put_rows(fy, t, y, field)
            both = dot(tx[...], field, ((1,), (1,)))
            store_pairs(0, t, y, both[:40] + both[40:])
            return carry

        lax.fori_loop(0, 8, analyse_x, 0)
        fix_zero(0, t)
        if t == 0:
            pl.semaphore_wait(here.at[0], 3)
        px_forward(0, t)
    for t in range(1, 4):
        tell(here.at[1], me, lax.rem(mine + 2 * t, NPY))
    g_buf[:, :, pl.ds(272, 48), :] = jnp.zeros((2, 2, 48, 128), F32)
    g_buf[:, 1, pl.ds(0, 16), :] = jnp.zeros((2, 16, 128), F32)
    sc[...] = jnp.zeros((256, 128), F32)

    for n in range(4, 11):
        loads[n].wait()

    txc_high, txc_low = split(txc_in[...])
    pool = ones_where(iota((128, 512), 0) == (iota((128, 512), 1) >> 2))
    for big in range(2):
        total = dot(pool, fy[4 * big])
        for y in range(1, 4):
            total = total + dot(pool, fy[4 * big + y])
        total = total * (1.0 / 64.0)
        rst[big] = total
        high, low = split(total)
        part = dot3(txc_high, txc_low, high, low, ((1,), (1,)))
        sc[pl.ds(big, 64, stride=4), :] = part
    pl.semaphore_wait(here.at[1], 3)
    tell(here.at[2], me, other)

    wk[...] = kron_eye(rows_of(w_fine[...], 32, 4, 1), 4)
    wkt[...] = kron_eye(rows_of(w_fine[...], 32, 4, 0), 4)

    def local(y, carry):
        put_block(b2, y, dot(wk[...], fy[y]))
        return carry

    lax.fori_loop(0, 8, local, 0)
    loads[11].wait()
    for t in range(2):
        unpack(b1, cot, t)
    low_total = jnp.zeros((128, 128), F32)
    for big in range(2):
        gather = ones_where(iota((256, 128), 1) == 64 * big + (iota((256, 128), 0) >> 2))
        high, low = split(rst[big])
        low_total = low_total + dot(high, gather) + dot(low, gather)
    rst2[...] = low_total
    for n in range(12, 22):
        loads[n].wait()
    for whole, parts in ((ty, ty_s), (tye, tye_s), (zf, zf_s), (zi, zi_s), (ti, ti_s), (tie, tie_s)):
        high, low = split(whole[...])
        parts[0] = high
        parts[1] = low
    base_mask = (iota((128, 1024), 0) >> 2) == ((iota((128, 1024), 1) & 511) >> 4)
    for r in range(2):
        full = jnp.where(base_mask, jnp.concatenate([zfc[r]] * 16, axis=0), 0.0)
        high, low = split(full)
        zfull_h[pl.ds(128 * r, 128), :] = high
        zfull_l[pl.ds(128 * r, 128), :] = low

    def build(step, carry):
        rows = 128 * step + iota((128, 512), 0)
        keep = (rows >> 4) == ((iota((128, 512), 1) & 255) >> 2)
        high, low = split(jnp.where(keep, jnp.concatenate([zic[...]] * 8, axis=0), 0.0))
        at = pl.ds(pl.multiple_of(128 * step, 128), 128)
        zifull_h[at, :] = high
        zifull_l[at, :] = low
        return carry

    lax.fori_loop(0, 8, build, 0)

    pl.semaphore_wait(here.at[2], 1)
    for t in range(2):
        px_forward_wait(0, t)
        forward_yz(0, t)

    coarse_px(0, sc, rc)

    real, imag = gather_modes(0)
    modes[0] = real
    modes[1] = imag
    out_real, out_imag = mix_modes(spec, real, imag, 32)
    fine_factor = mode_factor(256.0 * 256.0 * 128.0)
    spread_modes(0, out_real * fine_factor, out_imag * fine_factor)

    coarse_wait(0, rc)
    high, low = split(rc[...])
    along_y = dot3(*split(tyc_in[...]), high, low)
    high, low = split(jnp.concatenate([along_y[:64], along_y[64:]], axis=1))
    full = dot3(high, low, zfull_h[...], zfull_l[...])
    dup = ((iota((64, 512), 0) >> 2) & 1) == 0
    exc[...] = jnp.where(dup, full[:, :512], full[:, 512:]).reshape(8, 8, 512)
    coarse_py(1, lambda p: exc.at[p], rec)

    for t in range(2):
        inverse_zy(0, t, g_buf)

    for t in range(2):
        px_inverse_wait(0, t)
        g_buf[t, 1, pl.ds(0, 8), :] = g_buf[t, 0, pl.ds(8, 8), :]

        def middle(y, carry):
            value = jnp.concatenate([g_buf[t, h, pl.ds(y, 40, stride=8), :] for h in range(2)], axis=1)
            pre = some_rows(b2, t, y) + synthesise_x(value, ix[...])
            square = pre * pre
            tanh = jnp.tanh(ROOT * pre * (1.0 + 0.044715 * square))
            half = 0.5 * (1.0 + tanh)
            put_part(b0, t, y, pre * half)
            slope = half + 0.5 * pre * (1.0 - tanh * tanh) * (ROOT + (3.0 * 0.044715 * ROOT) * square)
            high, low = split(take(b1, t, y) * slope)
            put_rows(gph, t, y, high)
            put_rows(gpl, t, y, low)
            both = dot(tx[...], high, ((1,), (1,)))
            store_pairs(1, t, y, both[:40] + both[40:] + dot(tx[pl.ds(0, 40), :], low, ((1,), (1,))))
            return carry

        lax.fori_loop(0, 8, middle, 0)
        fix_zero(1, t)
        px_forward(1, t)

    def direct(y, carry):
        put_block(b1, y, dot(wkt[...], gph[y]) + dot(wkt[...], gpl[y]))
        return carry

    lax.fori_loop(0, 8, direct, 0)
    writes = [pltpu.make_async_copy(b1, dir_hbm, out_sem.at[0])]
    writes[0].start()

    coarse_wait(1, rec)
    real, imag = to_modes(jnp.sum(rec[...], axis=0), 32)
    high, low = split(jnp.concatenate([real, imag], axis=0))
    lifted = dot(high, lift[...]) + dot(low, lift[...])
    out_real, out_imag = mix_modes(spec_c, lifted[:64], lifted[64:], 64)
    coarse_factor = mode_factor(64.0 * 64.0 * 32.0)
    hc[...] = from_modes(out_real * coarse_factor, out_imag * coarse_factor, 64)
    for t in range(2):
        px_forward_wait(1, t)
        forward_yz(1, t)
    coarse_py(2, lambda p: hc, ric)

    real, imag = gather_modes(1)
    real, imag = real * fine_factor, imag * fine_factor
    lane = iota((64, 32), 1)
    pull_real = jnp.zeros((64, 32), F32)
    pull_imag = jnp.zeros((64, 32), F32)
    for i in range(32):
        w0, w1 = spec[0, i], spec[1, i]
        a = jnp.sum(w0 * real + w1 * imag, axis=1, keepdims=True)
        b = jnp.sum(w0 * imag - w1 * real, axis=1, keepdims=True)
        pull_real = jnp.where(lane == i, a, pull_real)
        pull_imag = jnp.where(lane == i, b, pull_imag)
    spread_modes(1, pull_real, pull_imag)
    coarse_wait(2, ric)
    high, low = split(ric[...].reshape(64, 1024))
    along_z = dot3(high, low, zifull_h[...], zifull_l[...])
    high, low = split(jnp.concatenate([along_z[:, :256], along_z[:, 256:]], axis=0))
    along_y = dot3(*split(tic_in[...]), high, low)
    for hh in range(2):
        svc[pl.ds(hh, 128, stride=2), :] = along_y[:, 128 * hh : 128 * hh + 128]
    coarse_px(3, svc, gc)

    x_real, x_imag = modes[0], modes[1]
    for i in range(32):
        a, b = column(x_real, i), column(x_imag, i)
        gspec[0, i] = real * a + imag * b
        gspec[1, i] = imag * a - real * b
    writes.append(pltpu.make_async_copy(gspec, gspec_hbm, out_sem.at[2]))
    writes[1].start()
    for t in range(2):
        inverse_zy(1, t, g_hbm)
    coarse_wait(3, gc)
    halves_out = []
    for hh in range(2):
        high, low = split(gc[pl.ds(hh, 128, stride=2), :].T)
        halves_out.append(dot3(high, low, *split(ixc_in[...])))
    spectral_part = jnp.concatenate(halves_out, axis=0)
    lift_wide = kron_eye(rows_of(lift[...], 64, 2, 1), 2)
    coarse_wide = kron_eye(rows_of(w_coarse[...], 64, 2, 1), 2)
    project_wide = kron_eye(rows_of(project[...], 32, 2, 0), 2)
    high, low = split(rst2[...])
    lifted = dot(lift_wide, high) + dot(lift_wide, low)
    high, low = split(lifted)
    coarse_pre = spectral_part + dot(coarse_wide, high) + dot(coarse_wide, low)
    high, low = split(tanh_gelu(coarse_pre))
    coarse_out = dot(project_wide, high) + dot(project_wide, low)
    out_high, out_low = split(coarse_out)
    widen = ones_where((iota((512, 128), 0) >> 2) == iota((512, 128), 1))
    for big in range(2):
        stretch = ones_where(iota((128, 256), 0) == 64 * big + (iota((128, 256), 1) >> 2))
        high, low = split(dot(out_high, stretch) + dot(out_low, stretch))
        prolonged = dot(widen, high) + dot(widen, low)
        for small in range(4):
            y = 4 * big + small
            put(b2, y, block(b0, y) + prolonged)
    pack(layer_out, b2)
    writes.append(pltpu.make_async_copy(layer_out, layer_hbm, out_sem.at[1]))
    writes[2].start()

    for t in range(2):
        px_inverse_wait(1, t)

    for write in writes:
        write.wait()
    for wait in pending:
        wait()


def finish(g_ref, zero_ref, dir_ref, layer_ref, gspec_ref, ix_in, layer_out, grad_out, gspec_out, kept, mixed):
    second = pl.program_id(0) >= 2
    rows = iota((PAIRS, 128), 0)
    value = jnp.where(rows < 272, g_ref[0, 0], 0.0)
    zero = jnp.concatenate([zero_ref[0, 0], jnp.zeros((PAIRS - 8, 128), F32)], axis=0)
    kept[...] = jnp.where(jnp.logical_and(second, rows < 16), zero, value)
    table = stacked_table(ix_in[...])

    for y in range(8):
        some = synthesise_x(kept[pl.ds(y, 40, stride=8), :], table)
        for lane in range(2):
            at = slice(128 * lane, 128 * lane + 128)
            mixed[lane, pl.ds(y, 128, stride=8), :] = some[:, at] + dir_ref[lane, y]
    for lane in range(2):
        grad_out[:, :, pl.ds(128 * lane, 128)] = mixed[lane].reshape(128, 8, 128).astype(BF16)
    layer_out[...] = layer_ref[...]
    gspec_out[...] = gspec_ref[...]


def body(
    features, cotangent, pointwise_fine, spectral_fine, lift_weight, pointwise_coarse,
    spectral_coarse, project_weight,
):
    table = tables()
    fine = spectral_fine.transpose(0, 1, 3, 4, 5, 2).reshape(2, 32, 64, 32)
    coarse = spectral_coarse.transpose(0, 1, 3, 4, 5, 2).reshape(2, 64, 64, 64)
    hbm = pl.BlockSpec(memory_space=pl.ANY)

    def f32(*shape):
        return pltpu.VMEM(shape, F32)

    def bf16(*shape):
        return pltpu.VMEM(shape, BF16)

    dma = pltpu.SemaphoreType.DMA
    layer, direct, gspec, spectrum = pl.pallas_call(
        kernel,
        out_shape=[
            jax.ShapeDtypeStruct((512, 8, 256), BF16),
            jax.ShapeDtypeStruct((2, 4096, 128), F32),
            jax.ShapeDtypeStruct((2, 32, 64, 32), F32),
            jax.ShapeDtypeStruct((2, 2, PAIRS, 128), F32),
        ],
        in_specs=[hbm] * 20,
        out_specs=[hbm] * 4,
        scratch_shapes=[
            bf16(32, 32), bf16(32, 64), bf16(64, 64), bf16(32, 64), f32(40, 256), f32(40, 256), f32(64, 256),
            f32(128, 256), f32(128, 128), f32(128, 128),
            f32(2, 4096, 128), f32(2, 4096, 128), f32(2, 4096, 128),
            bf16(8, 512, 256), bf16(8, 512, 256), bf16(8, 512, 256),
            bf16(512, 8, 256), bf16(512, 8, 256), f32(2, 32, 64, 32), f32(2, 64, 64, 64),
            bf16(512, 8, 256), f32(2, 32, 64, 32),
            f32(256, 512), f32(256, 512), f32(256, 256), f32(128, 256),
            f32(512, 256), f32(512, 256), f32(2, 8, 1024), f32(16, 512),
            bf16(256, 1024), bf16(256, 1024), bf16(1024, 512), bf16(1024, 512),
            bf16(80, 256), bf16(128, 256), bf16(2, 256, 512), bf16(2, 256, 512), bf16(2, 256, 256), bf16(2, 128, 256),
            bf16(2, 512, 256), bf16(2, 512, 256),
            bf16(512, 512), bf16(512, 512), f32(256, 128), f32(2, 128, 256), f32(128, 128), f32(2, 64, 32),
            f32(2, 2, 2, PAIRS, 128), f32(2, 2, 512, 128), f32(2, 2, 512, 128), f32(2, 2, 16, 8, 128), f32(2, 2, 16, 8, 128),
            f32(2, 2, 2, 8, 128), f32(2, 2, 16, 8, 128), f32(2, 2, 512, 128), f32(2, 2, 512, 128), f32(2, 2, PAIRS, 128),
            f32(256, 128), f32(256, 128), f32(8, 8, 512), f32(8, 8, 512), f32(8, 1024), f32(8, 8, 1024),
            f32(256, 128), f32(256, 128),
            dma((22,)), dma((3,)), dma((8,)), dma((8,)), dma((8,)), dma((8,)), dma((8,)), dma((8,)), dma((8,)),
            dma((4,)), dma((4,)), pltpu.SemaphoreType.REGULAR((3,)),
        ],
        compiler_params=pltpu.CompilerParams(
            collective_id=0, has_side_effects=True, vmem_limit_bytes=60 * 1024 * 1024
        ),
        name="fno_layer",
    )(
        features.reshape(512, 8, 256), cotangent.reshape(512, 8, 256), pointwise_fine, fine, lift_weight,
        pointwise_coarse, coarse, project_weight.T,
        table["tx"], table["ix"], table["ty"], table["zf"], table["zi"], table["ti"], table["txc"], table["tyc"],
        table["zfc"], table["zic"], table["tic"], table["ixc"],
    )
    layer_out, grad_out, gspec = pl.pallas_call(
        finish,
        grid=(4,),
        out_shape=[
            jax.ShapeDtypeStruct((512, 8, 256), BF16),
            jax.ShapeDtypeStruct((512, 8, 256), BF16),
            jax.ShapeDtypeStruct((2, 32, 64, 32), F32),
        ],
        in_specs=[
            pl.BlockSpec((1, 1, PAIRS, 128), lambda i: (i % 2, i // 2, 0, 0)),
            pl.BlockSpec((1, 1, 8, 128), lambda i: (i % 2, 0, 1, 0)),
            pl.BlockSpec((2, 8, 128, 128), lambda i: (0, 0, i, 0)),
            pl.BlockSpec((128, 8, 256), lambda i: (i, 0, 0)),
            pl.BlockSpec((2, 8, 64, 32), lambda i: (0, i, 0, 0)),
            pl.BlockSpec((40, 256), lambda i: (0, 0)),
        ],
        out_specs=[
            pl.BlockSpec((128, 8, 256), lambda i: (i, 0, 0)),
            pl.BlockSpec((128, 8, 256), lambda i: (i, 0, 0)),
            pl.BlockSpec((2, 8, 64, 32), lambda i: (0, i, 0, 0)),
        ],
        scratch_shapes=[f32(PAIRS, 128), f32(2, 1024, 128)],
        compiler_params=pltpu.CompilerParams(vmem_limit_bytes=60 * 1024 * 1024),
        name="finish",
    )(spectrum, spectrum, direct.reshape(2, 8, 512, 128), layer, gspec, table["ix"])
    shape = (32, 16, 8, 256)
    gspec = gspec.reshape(2, 32, 16, 1, 4, 32).transpose(0, 1, 5, 2, 3, 4)
    return layer_out.reshape(shape), grad_out.reshape(shape), gspec


def solution(mesh):
    placed = (
        P(None, "py", "px", None),
        P(None, "py", "px", None),
        P(),
        P(None, None, None, None, "px", "py"),
        P(),
        P(),
        P(None, None, None, None, "px", "py"),
        P(),
    )
    return jax.shard_map(
        body,
        mesh=mesh,
        in_specs=placed,
        out_specs=(
            P(None, "py", "px", None),
            P(None, "py", "px", None),
            P(None, None, None, None, "px", "py"),
        ),
        check_vma=False,
    )
```

```python
import functools
import math

import jax
import jax.numpy as jnp
import numpy as np
from jax import lax
from jax.experimental import pallas as pl
from jax.experimental.pallas import tpu as pltpu
from jax.sharding import PartitionSpec as P

M = 16
F32 = jnp.float32
BF16 = jnp.bfloat16
MESH = pl.DeviceIdType.MESH
NPX, NPY = 32, 8
PAIRS = 320
ROOT = math.sqrt(2.0 / math.pi)


def single(table):
    return np.asarray(table, np.float64).astype(np.float32)


def signed(index):
    return np.where(index < M, index, index - 2 * M)


def turn(freq, cell, count):
    return (np.asarray(freq) * np.asarray(cell) % count) * (2.0 * np.pi / count)


@functools.cache
def tables():
    out = {}
    x = np.arange(256)
    rows = np.zeros((40, 256))
    for j in range(17):
        angle = turn(j, x, 256)
        if j == 0:
            rows[0] = rows[1] = 1.0
        else:
            rows[2 * j] = np.cos(angle)
            rows[2 * j + 1] = -np.sin(angle) if j < 16 else np.sin(angle)
    out["tx"] = single(rows)
    inv = rows.copy()
    inv[1] = 0.0
    out["ix"] = single(inv)

    ky = np.arange(32)
    theta = turn(signed(ky)[:, None], np.arange(256)[None, :], 256)
    cos, sin = np.cos(theta), np.sin(theta)
    zero = np.zeros_like(cos)
    plus = (((cos, sin), (-sin, cos)))
    minus = (((cos, -sin), (-sin, -cos)))
    from0 = (((cos, zero), (-sin, zero)))
    from1 = (((zero, cos), (zero, -sin)))
    none = (((zero, zero), (zero, zero)))
    kinds = [(plus, minus), (minus, plus), (from0, from1), (plus, none), (none, plus)]
    ty = np.zeros((5, 2, 2, 8, 2, 4, 32, 2, 8))
    for k, pair in enumerate(kinds):
        for q in range(2):
            for r1 in range(2):
                for r in range(2):
                    block = pair[q][r1][r].reshape(8, 4, 32, 8)
                    for dup in range(2):
                        ty[k, r1, q, :, dup, :, :, r, :] = block
    ty = ty.reshape(5, 256, 512)
    out["ty"] = single(ty)

    ti = np.zeros((5, 32, 2, 8, 2, 2, 8, 2, 4))

    def add(k, rout, q, part, sign):
        c = cos.T.reshape(32, 8, 8, 4)
        s = sin.T.reshape(32, 8, 8, 4)
        if part == 0:
            coef = {(0, 0): c, (1, 1): -c, (0, 1): -s, (1, 0): -s}
        else:
            coef = {(0, 0): s, (1, 1): -s, (0, 1): c, (1, 0): c}
        for (cs, r), value in coef.items():
            ti[k, :, rout, :, cs, q, :, r, :] += sign * value

    for k, first in ((0, 1.0), (1, -1.0)):
        add(k, 0, 0, 0, 1.0)
        add(k, 0, 1, 0, 1.0)
        add(k, 1, 0, 1, first)
        add(k, 1, 1, 1, -first)
    add(2, 0, 0, 0, 1.0)
    add(2, 1, 1, 0, 1.0)
    for k, q in ((3, 0), (4, 1)):
        add(k, 0, q, 0, 1.0)
        add(k, 1, q, 1, 1.0)
    out["ti"] = single(ti.reshape(5, 512, 256))

    kz = np.arange(16)
    zf = np.zeros((8, 2, 8, 16, 2, 8, 16))
    zi = np.zeros((8, 8, 16, 2, 8, 16))
    for b in range(8):
        phi = turn(kz[None, :], (b * 16 + np.arange(16))[:, None], 128)
        for c in range(8):
            zf[b, 0, c, :, 0, c, :] = np.cos(phi)
            zf[b, 1, c, :, 0, c, :] = np.sin(phi)
            zf[b, 0, c, :, 1, c, :] = -np.sin(phi)
            zf[b, 1, c, :, 1, c, :] = np.cos(phi)
            zi[b, c, :, 0, c, :] = np.cos(phi).T
            zi[b, c, :, 1, c, :] = np.sin(phi).T
    out["zf"] = single(zf.reshape(8, 256, 256))
    out["zi"] = single(zi.reshape(8, 128, 256))

    kx = np.arange(32)
    alpha = turn(signed(kx)[:, None], (x // 4)[None, :], 64)
    txc = np.stack([np.cos(alpha), -np.sin(alpha)], axis=1).reshape(64, 256)
    out["txc"] = single(txc)
    theta = turn(signed(ky)[:, None], np.arange(64)[None, :], 64)
    cos, sin = np.cos(theta), np.sin(theta)
    tyc = np.zeros((2, 8, 2, 4, 32, 2, 4))
    plus = ((cos, sin), (-sin, cos))
    for r1 in range(2):
        for r in range(2):
            for dup in range(2):
                tyc[r1, :, dup, :, :, r, :2] = plus[r1][r].reshape(8, 4, 32, 2)
    out["tyc"] = single(tyc.reshape(128, 256))
    tic = np.zeros((32, 2, 2, 2, 8, 2, 4))
    c = cos.T.reshape(32, 2, 8, 4)
    s = sin.T.reshape(32, 2, 8, 4)
    for (rout, cs, r), value in {
        (0, 0, 0): c, (0, 1, 1): -c, (0, 0, 1): -s, (0, 1, 0): -s,
        (1, 0, 0): s, (1, 1, 1): -s, (1, 0, 1): c, (1, 1, 0): c,
    }.items():
        tic[:, rout, :, cs, :, r, :] = value
    out["tic"] = single(tic.reshape(128, 128))
    zfc = np.zeros((8, 2, 2, 4, 2, 32, 16))
    zic = np.zeros((8, 16, 2, 64, 4))
    for b in range(8):
        phi = turn(kz[None, :], (b * 4 + np.arange(4))[:, None], 32)
        zfc[b, 0, :, :, 0] = np.cos(phi)[None, :, None, :]
        zfc[b, 1, :, :, 0] = np.sin(phi)[None, :, None, :]
        zfc[b, 0, :, :, 1] = -np.sin(phi)[None, :, None, :]
        zfc[b, 1, :, :, 1] = np.cos(phi)[None, :, None, :]
        zic[b, :, 0] = np.cos(phi).T[:, None, :]
        zic[b, :, 1] = np.sin(phi).T[:, None, :]
    out["zfc"] = single(zfc.reshape(8, 2, 8, 1024))
    out["zic"] = single(zic.reshape(8, 16, 512))
    alpha = turn(signed(kx)[:, None], np.arange(64)[None, :], 64)
    ixc = np.zeros((32, 2, 2, 2, 64))
    for big in range(2):
        ixc[:, 0, big, big] = np.cos(alpha)
        ixc[:, 1, big, big] = -np.sin(alpha)
    out["ixc"] = single(ixc.reshape(128, 128))
    return out


def split(value):
    high = value.astype(BF16)
    return high, (value - high.astype(F32)).astype(BF16)


def dot(left, right, dims=((1,), (0,))):
    return lax.dot_general(left, right, (dims, ((), ())), preferred_element_type=F32)


def dot3(left_high, left_low, right_high, right_low, dims=((1,), (0,))):
    return (
        dot(left_high, right_high, dims)
        + dot(left_high, right_low, dims)
        + dot(left_low, right_high, dims)
    )


def iota(shape, dim):
    return lax.broadcasted_iota(jnp.int32, shape, dim)


def ones_where(condition):
    return jnp.where(condition, 1.0, 0.0).astype(BF16)


def kron_eye(first, shift):
    rows, m = first.shape
    spread = ones_where(iota((m, m << shift), 0) == (iota((m, m << shift), 1) >> shift))
    full = dot(first.astype(BF16), spread)
    low = (1 << shift) - 1
    shape = (rows, m << shift)
    return jnp.where((iota(shape, 0) & low) == (iota(shape, 1) & low), full, 0.0).astype(BF16)


def rows_of(weight, n, shift, axis):
    pick = ones_where((iota((n << shift, n), 0) >> shift) == iota((n << shift, n), 1))
    return dot(pick, weight, ((1,), (axis,)))


def to_modes(packed, count):
    lanes = count * 16
    real = jnp.concatenate([packed[0:4]] * 16, axis=0)
    imag = jnp.concatenate([packed[4:8]] * 16, axis=0)
    mask = (iota((64, lanes), 0) >> 2) == (iota((64, lanes), 1) & 15)
    wide = jnp.concatenate([jnp.where(mask, real, 0.0), jnp.where(mask, imag, 0.0)], axis=0)
    pick = ones_where((iota((lanes, count), 0) >> 4) == iota((lanes, count), 1))
    high, low = split(wide)
    modes = dot(high, pick) + dot(low, pick)
    return modes[:64], modes[64:]


def from_modes(real, imag, count):
    lanes = count * 16
    high, low = split(jnp.concatenate([real, imag], axis=0))
    spread = ones_where(iota((count, lanes), 0) == (iota((count, lanes), 1) >> 4))
    wide = dot(high, spread) + dot(low, spread)
    mask = ((iota((128, lanes), 0) & 63) >> 2) == (iota((128, lanes), 1) & 15)
    high, low = split(jnp.where(mask, wide, 0.0))
    shape = (8, 128)
    total = ones_where(
        ((iota(shape, 1) >> 6) == (iota(shape, 0) >> 2)) & ((iota(shape, 1) & 3) == (iota(shape, 0) & 3))
    )
    return dot(total, high) + dot(total, low)


def column(values, index):
    return values[:, index : index + 1]


def mix_modes(weight_ref, real, imag, count):
    out_real = jnp.zeros((64, count), F32)
    out_imag = jnp.zeros((64, count), F32)
    for i in range(count):
        w0, w1 = weight_ref[0, i], weight_ref[1, i]
        a, b = column(real, i), column(imag, i)
        out_real = out_real + (w0 * a - w1 * b)
        out_imag = out_imag + (w0 * b + w1 * a)
    return out_real, out_imag


def mode_factor(cells):
    return jnp.where(iota((64, 1), 0) < 4, 1.0 / cells, 2.0 / cells).astype(F32)


def stacked_table(table):
    high, low = split(table)
    high, low = high.astype(F32), low.astype(F32)
    return jnp.concatenate([high, high, low, jnp.zeros((8, 256), F32)], axis=0).astype(BF16)


def synthesise_x(value, table):
    high = value.astype(BF16).astype(F32)
    pad = jnp.zeros((8, value.shape[1]), F32)
    stacked = jnp.concatenate([high, value - high, high, pad], axis=0)
    return dot(stacked.T.astype(BF16), table)


def tanh_gelu(value):
    return 0.5 * value * (1.0 + jnp.tanh(ROOT * (value + 0.044715 * value * value * value)))


def kernel(
    feat_hbm, cot_hbm, w_fine_hbm, spec_hbm, lift_hbm, w_coarse_hbm, spec_c_hbm, project_hbm,
    tx_hbm, ix_hbm, ty_hbm, zf_hbm, zi_hbm, ti_hbm, txc_hbm, tyc_hbm, zfc_hbm, zic_hbm, tic_hbm, ixc_hbm,
    layer_hbm, dir_hbm, gspec_hbm, g_hbm,
    w_fine, lift, w_coarse, project, tx_in, ix_in, txc_in, tyc_in, tic_in, ixc_in,
    b0, b1, b2, fy, gph, gpl, feat, cot, spec, spec_c, layer_out, gspec,
    ty, tye, zf, zi, ti, tie, zfc, zic, zfull_h, zfull_l, zifull_h, zifull_l,
    tx, ix, ty_s, tye_s, zf_s, zi_s, ti_s, tie_s,
    wk, wkt, yc, rst, rst2, modes,
    s_buf, rx, rxe, ex, re_buf, hq, ri, sv, g_buf,
    sc, rc, exc, rec, hc, ric, svc, gc,
    load_sem, out_sem, px_send, px_recv, pxe_send, pxe_recv, py_send, py_recv, pye_send,
    c_send, c_recv, here,
):
    me = lax.axis_index("px")
    mine = lax.axis_index("py")
    partner = lax.rem(NPX - me, NPX)
    upper = lax.div(me + 15, 32)
    is0 = 1 - lax.div(me + 31, 32)
    is16 = lax.div(me, 16) * (1 - upper)
    kind = upper + 2 * is0 + 3 * is16
    regular = 1 - is0 - is16

    loads = [
        (feat_hbm, feat), (tx_hbm, tx_in), (ix_hbm, ix_in), (txc_hbm, txc_in), (w_fine_hbm, w_fine),
        (lift_hbm, lift), (w_coarse_hbm, w_coarse), (project_hbm, project), (tyc_hbm, tyc_in),
        (tic_hbm, tic_in), (ixc_hbm, ixc_in),
        (cot_hbm, cot), (spec_hbm, spec), (spec_c_hbm, spec_c),
        (ty_hbm.at[kind], ty), (ty_hbm.at[4], tye), (zf_hbm.at[mine], zf), (zi_hbm.at[mine], zi),
        (ti_hbm.at[kind], ti), (ti_hbm.at[4], tie), (zfc_hbm.at[mine], zfc), (zic_hbm.at[mine], zic),
    ]
    loads = [pltpu.make_async_copy(a, b, load_sem.at[n]) for n, (a, b) in enumerate(loads)]
    for load in loads[:4]:
        load.start()

    barrier = pltpu.get_barrier_semaphore()
    row = 8 * lax.div(me, 8)

    def tell(semaphore, px, py):
        pl.semaphore_signal(semaphore, inc=1, device_id={"px": px, "py": py}, device_id_type=MESH)

    for t in range(1, 8):
        tell(barrier, row + lax.rem(me + t, 8), mine)
    for t in range(1, 4):
        tell(barrier, lax.rem(me + 8 * t, NPX), mine)
    for t in range(1, 4):
        tell(barrier, me, lax.rem(mine + 2 * t, NPY))
    other = 2 * lax.div(mine, 2) + 1 - lax.rem(mine, 2)
    tell(barrier, me, other)
    for load in loads[4:]:
        load.start()
    pl.semaphore_wait(barrier, 14)
    for t in range(1, 4):
        tell(here.at[0], lax.rem(me + 8 * t, NPX), mine)

    def pair_row(d):
        h = lax.div(d + 15, 32)
        return h, pl.multiple_of(16 * (d * (1 - 2 * h) + 32 * h), 16)

    pending = []

    def left(semaphore, ref, condition=None):
        def wait():
            pltpu.make_async_copy(ref, ref, semaphore).wait()

        pending.append(wait if condition is None else lambda: pl.when(condition)(wait))

    slab, side = lax.div(mine, 2), lax.rem(mine, 2)

    def each_px(send):
        def step(t, carry):
            send(lax.rem(me + t, NPX))
            return carry

        lax.fori_loop(1, NPX, step, 0)

    def each_py(send):
        for far, ahead in ((1, 2), (1, 1), (1, 3), (1, 0), (0, 2), (0, 1), (0, 3)):
            send(2 * lax.rem(slab + ahead, 4) + (1 - side if far else side))

    def at16(d):
        return pl.ds(pl.multiple_of(16 * d, 16), 16)

    def px_forward(n, t):
        k = 4 * n + t
        left(px_send.at[k], rx.at[0, 0, pl.ds(0, 496)])
        left(pxe_send.at[k], rx.at[0, 0, pl.ds(0, 16)], is16 == 0)

        def send(d):
            h, row = pair_row(d)
            pltpu.make_async_remote_copy(
                s_buf.at[n, t, h, pl.ds(row, 16)], rx.at[n, t, at16(me)],
                px_send.at[k], px_recv.at[k], device_id={"px": d, "py": mine}, device_id_type=MESH,
            ).start()

        each_px(send)
        h, row = pair_row(me)
        pltpu.make_async_copy(s_buf.at[n, t, h, pl.ds(row, 16)], rx.at[n, t, at16(me)], px_recv.at[k]).start()

        @pl.when(is16 == 0)
        def _():
            pltpu.make_async_remote_copy(
                s_buf.at[n, t, 1, pl.ds(256, 16)], rxe.at[n, t, at16(me)],
                pxe_send.at[k], pxe_recv.at[k], device_id={"px": 16, "py": mine}, device_id_type=MESH,
            ).start()

        @pl.when(is16 == 1)
        def _():
            pltpu.make_async_copy(
                s_buf.at[n, t, 1, pl.ds(256, 16)], rxe.at[n, t, at16(me)], pxe_recv.at[k]
            ).start()

    def px_forward_wait(n, t):
        k = 4 * n + t
        pltpu.make_async_copy(rx.at[n, t], rx.at[n, t], px_recv.at[k]).wait()

        @pl.when(is16 == 1)
        def _():
            pltpu.make_async_copy(rxe.at[n, t], rxe.at[n, t], pxe_recv.at[k]).wait()

    def px_inverse(n, t, target):
        k = 4 * n + 2 + t
        left(px_send.at[k], rx.at[0, 0, pl.ds(0, 496)], is16 == 0)
        left(px_send.at[k], rx.at[0, :, pl.ds(0, 496)], is16 == 1)
        h, row = pair_row(me)

        @pl.when(is16 == 0)
        def _():
            def send(d):
                pltpu.make_async_remote_copy(
                    sv.at[n, t, 0, at16(d)], target.at[t, h, pl.ds(row, 16)],
                    px_send.at[k], px_recv.at[k], device_id={"px": d, "py": mine}, device_id_type=MESH,
                ).start()

            each_px(send)
            pltpu.make_async_copy(
                sv.at[n, t, 0, at16(me)], target.at[t, h, pl.ds(row, 16)], px_recv.at[k]
            ).start()

        @pl.when(is16 == 1)
        def _():
            def send(d):
                pltpu.make_async_remote_copy(
                    sv.at[n, t, :, at16(d)], target.at[t, :, pl.ds(256, 16)],
                    px_send.at[k], px_recv.at[k], device_id={"px": d, "py": mine}, device_id_type=MESH,
                ).start()

            each_px(send)
            pltpu.make_async_copy(
                sv.at[n, t, :, at16(me)], target.at[t, :, pl.ds(256, 16)], px_recv.at[k]
            ).start()

    def px_inverse_wait(n, t):
        some = rx.at[n, :, pl.ds(0, 264)]
        pltpu.make_async_copy(some, some, px_recv.at[4 * n + 2 + t]).wait()

    def py_exchange(slot, source, target):
        left(py_send.at[slot], ex.at[0, 0, pl.ds(0, 14)])
        left(pye_send.at[slot], ex.at[0, 0, 0], regular == 1)

        def send(p):
            for q, to in ((1, partner), (0, me)):
                pltpu.make_async_remote_copy(
                    source(q, p), target.at[8 * q + mine], py_send.at[slot], py_recv.at[slot],
                    device_id={"px": to, "py": p}, device_id_type=MESH,
                ).start()

        each_py(send)
        pltpu.make_async_copy(source(0, mine), target.at[mine], py_recv.at[slot]).start()

        @pl.when(regular == 1)
        def _():
            pltpu.make_async_remote_copy(
                source(1, mine), target.at[8 + mine], pye_send.at[slot], py_recv.at[slot],
                device_id={"px": partner, "py": mine}, device_id_type=MESH,
            ).start()

        @pl.when(regular == 0)
        def _():
            pltpu.make_async_copy(source(1, mine), target.at[8 + mine], py_recv.at[slot]).start()

    def py_wait(slot, target):
        pltpu.make_async_copy(target, target, py_recv.at[slot]).wait()

    def coarse_px(slot, source, target):
        left(c_send.at[slot], target.at[pl.ds(0, 248)])
        there = target.at[pl.ds(pl.multiple_of(8 * me, 8), 8)]

        def send(d):
            pltpu.make_async_remote_copy(
                source.at[pl.ds(pl.multiple_of(8 * d, 8), 8)], there, c_send.at[slot], c_recv.at[slot],
                device_id={"px": d, "py": mine}, device_id_type=MESH,
            ).start()

        each_px(send)
        pltpu.make_async_copy(source.at[pl.ds(pl.multiple_of(8 * me, 8), 8)], there, c_recv.at[slot]).start()

    def coarse_py(slot, source, target):
        left(c_send.at[slot], target.at[pl.ds(0, 7)])

        def send(p):
            pltpu.make_async_remote_copy(
                source(p), target.at[mine], c_send.at[slot], c_recv.at[slot],
                device_id={"px": me, "py": p}, device_id_type=MESH,
            ).start()

        each_py(send)
        pltpu.make_async_copy(source(mine), target.at[mine], c_recv.at[slot]).start()

    def coarse_wait(slot, target):
        pltpu.make_async_copy(target, target, c_recv.at[slot]).wait()

    def fix_zero(n, t):
        s_buf[n, t, 0, pl.ds(8, 8), :] = s_buf[n, t, 1, pl.ds(0, 8), :]

    def forward_yz(n, t):
        high, low = split(rx[n, t])
        yc[...] = dot3(ty_s[0], ty_s[1], high, low)

        @pl.when(is16 == 1)
        def _():
            high, low = split(rxe[n, t])
            yc[...] += dot3(tye_s[0], tye_s[1], high, low)

        dup = ((iota((128, 128), 0) >> 2) & 1) == 0
        both = jnp.concatenate([yc[pl.ds(0, 128), :], yc[pl.ds(128, 128), :]], axis=1)
        high, low = split(both)
        full = dot3(high, low, zf_s[0], zf_s[1])
        ex[n, t] = jnp.where(dup, full[:, :128], full[:, 128:]).reshape(16, 8, 128)
        py_exchange(4 * n + t, lambda q, p: ex.at[n, t, 8 * q + p], re_buf.at[n, t])

    def gather_modes(n):
        slots = []
        for q in range(2):
            parts = []
            for t in range(2):
                if q == 0:
                    py_wait(4 * n + t, re_buf.at[n, t])
                parts.append(jnp.sum(re_buf[n, t, 8 * q : 8 * q + 8], axis=0))
            slots.append(jnp.concatenate(parts, axis=1))
        swap = upper == 1
        first = jnp.where(swap, slots[1], slots[0])
        second = jnp.where(swap, slots[0], slots[1])
        return to_modes(jnp.concatenate([first, second], axis=1), 32)

    def spread_modes(n, real, imag):
        packed = from_modes(real, imag, 32)
        swap = upper == 1
        for t in range(2):
            first, second = packed[:, 128 * t : 128 * t + 128], packed[:, 256 + 128 * t : 384 + 128 * t]
            hq[n, t, 0] = jnp.where(swap, second, first)
            hq[n, t, 1] = jnp.where(swap, first, second)
            py_exchange(4 * n + 2 + t, lambda q, p: hq.at[n, t, q], ri.at[n, t])

    def inverse_zy(n, t, target):
        py_wait(4 * n + 2 + t, ri.at[n, t])
        high, low = split(ri[n, t].reshape(128, 128))
        full = dot3(high, low, zi_s[0], zi_s[1])
        high, low = split(jnp.concatenate([full[:, :128], full[:, 128:]], axis=0))
        sv[n, t, 0] = dot3(ti_s[0], ti_s[1], high, low)

        @pl.when(is16 == 1)
        def _():
            sv[n, t, 1] = dot3(tie_s[0], tie_s[1], high, low)

        px_inverse(n, t, target)

    def rows_at(h, t):
        return 256 * h + 128 * t

    def take(ref, t, y):
        return jnp.concatenate(
            [
                jnp.concatenate(
                    [ref[lane, pl.ds(8 * rows_at(h, t) + y, 128, stride=8), :] for lane in range(2)], axis=1
                )
                for h in range(2)
            ],
            axis=0,
        )

    def put(ref, y, value):
        for lane in range(2):
            ref[lane, pl.ds(y, 512, stride=8), :] = value[:, 128 * lane : 128 * lane + 128]

    def block(ref, y):
        rows = pl.ds(pl.multiple_of(512 * y, 512), 512)
        return jnp.concatenate([ref[0, rows, :], ref[1, rows, :]], axis=1)

    def put_block(ref, y, value):
        rows = pl.ds(pl.multiple_of(512 * y, 512), 512)
        ref[0, rows, :] = value[:, :128]
        ref[1, rows, :] = value[:, 128:]

    def part_rows(h, t, y):
        return pl.ds(pl.multiple_of(512 * y + rows_at(h, t), 128), 128)

    def some_rows(ref, t, y):
        return jnp.concatenate(
            [
                jnp.concatenate([ref[lane, part_rows(h, t, y), :] for lane in range(2)], axis=1)
                for h in range(2)
            ],
            axis=0,
        )

    def put_part(ref, t, y, value):
        for h in range(2):
            for lane in range(2):
                ref[lane, part_rows(h, t, y), :] = value[128 * h : 128 * h + 128, 128 * lane : 128 * lane + 128]

    def put_rows(ref, t, y, value):
        for h in range(2):
            ref[y, pl.ds(rows_at(h, t), 128), :] = value[128 * h : 128 * h + 128]

    def unpack(ref, field, t):
        for h in range(2):
            for lane in range(2):
                some = field[pl.ds(rows_at(h, t), 128), :, pl.ds(128 * lane, 128)]
                ref[lane, pl.ds(8 * rows_at(h, t), 1024), :] = some.astype(F32).reshape(1024, 128)

    def pack(field, ref):
        for lane in range(2):
            field[:, :, pl.ds(128 * lane, 128)] = ref[lane].reshape(512, 8, 128).astype(BF16)

    def store_pairs(n, t, y, both):
        for h in range(2):
            s_buf[n, t, h, pl.ds(y, 40, stride=8), :] = both[:, 128 * h : 128 * h + 128]

    for n in range(4):
        loads[n].wait()
    high, low = split(tx_in[...])
    tx[pl.ds(0, 40), :] = high
    tx[pl.ds(40, 40), :] = low
    ix[...] = stacked_table(ix_in[...])
    for t in range(2):
        unpack(b0, feat, t)

        def analyse_x(y, carry):
            field = take(b0, t, y).astype(BF16)
            put_rows(fy, t, y, field)
            both = dot(tx[...], field, ((1,), (1,)))
            store_pairs(0, t, y, both[:40] + both[40:])
            return carry

        lax.fori_loop(0, 8, analyse_x, 0, unroll=2)
        fix_zero(0, t)
        if t == 0:
            pl.semaphore_wait(here.at[0], 3)
        px_forward(0, t)
    for t in range(1, 4):
        tell(here.at[1], me, lax.rem(mine + 2 * t, NPY))
    g_buf[:, :, pl.ds(272, 48), :] = jnp.zeros((2, 2, 48, 128), F32)
    g_buf[:, 1, pl.ds(0, 16), :] = jnp.zeros((2, 16, 128), F32)
    sc[...] = jnp.zeros((256, 128), F32)

    for n in range(4, 11):
        loads[n].wait()

    txc_high, txc_low = split(txc_in[...])
    pool = ones_where(iota((128, 512), 0) == (iota((128, 512), 1) >> 2))
    for big in range(2):
        total = dot(pool, fy[4 * big])
        for y in range(1, 4):
            total = total + dot(pool, fy[4 * big + y])
        total = total * (1.0 / 64.0)
        rst[big] = total
        high, low = split(total)
        part = dot3(txc_high, txc_low, high, low, ((1,), (1,)))
        sc[pl.ds(big, 64, stride=4), :] = part
    pl.semaphore_wait(here.at[1], 3)
    tell(here.at[2], me, other)

    wk[...] = kron_eye(rows_of(w_fine[...], 32, 4, 1), 4)
    wkt[...] = kron_eye(rows_of(w_fine[...], 32, 4, 0), 4)

    def local(y, carry):
        put_block(b2, y, dot(wk[...], fy[y]))
        return carry

    lax.fori_loop(0, 8, local, 0)
    loads[11].wait()
    for t in range(2):
        unpack(b1, cot, t)
    low_total = jnp.zeros((128, 128), F32)
    for big in range(2):
        gather = ones_where(iota((256, 128), 1) == 64 * big + (iota((256, 128), 0) >> 2))
        high, low = split(rst[big])
        low_total = low_total + dot(high, gather) + dot(low, gather)
    rst2[...] = low_total
    for n in range(12, 22):
        loads[n].wait()
    for whole, parts in ((ty, ty_s), (tye, tye_s), (zf, zf_s), (zi, zi_s), (ti, ti_s), (tie, tie_s)):
        high, low = split(whole[...])
        parts[0] = high
        parts[1] = low
    base_mask = (iota((128, 1024), 0) >> 2) == ((iota((128, 1024), 1) & 511) >> 4)
    for r in range(2):
        full = jnp.where(base_mask, jnp.concatenate([zfc[r]] * 16, axis=0), 0.0)
        high, low = split(full)
        zfull_h[pl.ds(128 * r, 128), :] = high
        zfull_l[pl.ds(128 * r, 128), :] = low

    def build(step, carry):
        rows = 128 * step + iota((128, 512), 0)
        keep = (rows >> 4) == ((iota((128, 512), 1) & 255) >> 2)
        high, low = split(jnp.where(keep, jnp.concatenate([zic[...]] * 8, axis=0), 0.0))
        at = pl.ds(pl.multiple_of(128 * step, 128), 128)
        zifull_h[at, :] = high
        zifull_l[at, :] = low
        return carry

    lax.fori_loop(0, 8, build, 0)

    pl.semaphore_wait(here.at[2], 1)
    for t in range(2):
        px_forward_wait(0, t)
        forward_yz(0, t)

    coarse_px(0, sc, rc)

    real, imag = gather_modes(0)
    modes[0] = real
    modes[1] = imag
    out_real, out_imag = mix_modes(spec, real, imag, 32)
    fine_factor = mode_factor(256.0 * 256.0 * 128.0)
    spread_modes(0, out_real * fine_factor, out_imag * fine_factor)

    coarse_wait(0, rc)
    high, low = split(rc[...])
    along_y = dot3(*split(tyc_in[...]), high, low)
    high, low = split(jnp.concatenate([along_y[:64], along_y[64:]], axis=1))
    full = dot3(high, low, zfull_h[...], zfull_l[...])
    dup = ((iota((64, 512), 0) >> 2) & 1) == 0
    exc[...] = jnp.where(dup, full[:, :512], full[:, 512:]).reshape(8, 8, 512)
    coarse_py(1, lambda p: exc.at[p], rec)

    for t in range(2):
        inverse_zy(0, t, g_buf)

    for t in range(2):
        px_inverse_wait(0, t)
        g_buf[t, 1, pl.ds(0, 8), :] = g_buf[t, 0, pl.ds(8, 8), :]

        def middle(y, carry):
            value = jnp.concatenate([g_buf[t, h, pl.ds(y, 40, stride=8), :] for h in range(2)], axis=1)
            pre = some_rows(b2, t, y) + synthesise_x(value, ix[...])
            square = pre * pre
            half = 0.5 + 0.5 * jnp.tanh(pre * (ROOT + (0.044715 * ROOT) * square))
            act = pre * half
            put_part(b0, t, y, act)
            slope = half + act * (1.0 - half) * (2.0 * ROOT + (6.0 * 0.044715 * ROOT) * square)
            high, low = split(take(b1, t, y) * slope)
            put_rows(gph, t, y, high)
            put_rows(gpl, t, y, low)
            both = dot(tx[...], high, ((1,), (1,)))
            store_pairs(1, t, y, both[:40] + both[40:] + dot(tx[pl.ds(0, 40), :], low, ((1,), (1,))))
            return carry

        lax.fori_loop(0, 8, middle, 0, unroll=2)
        fix_zero(1, t)
        px_forward(1, t)

    def direct(y, carry):
        put_block(b1, y, dot(wkt[...], gph[y]) + dot(wkt[...], gpl[y]))
        return carry

    lax.fori_loop(0, 8, direct, 0)
    writes = [pltpu.make_async_copy(b1, dir_hbm, out_sem.at[0])]
    writes[0].start()

    coarse_wait(1, rec)
    real, imag = to_modes(jnp.sum(rec[...], axis=0), 32)
    high, low = split(jnp.concatenate([real, imag], axis=0))
    lifted = dot(high, lift[...]) + dot(low, lift[...])
    out_real, out_imag = mix_modes(spec_c, lifted[:64], lifted[64:], 64)
    coarse_factor = mode_factor(64.0 * 64.0 * 32.0)
    hc[...] = from_modes(out_real * coarse_factor, out_imag * coarse_factor, 64)
    for t in range(2):
        px_forward_wait(1, t)
        forward_yz(1, t)
    coarse_py(2, lambda p: hc, ric)

    real, imag = gather_modes(1)
    real, imag = real * fine_factor, imag * fine_factor
    lane = iota((64, 32), 1)
    pull_real = jnp.zeros((64, 32), F32)
    pull_imag = jnp.zeros((64, 32), F32)
    for i in range(32):
        w0, w1 = spec[0, i], spec[1, i]
        a = jnp.sum(w0 * real + w1 * imag, axis=1, keepdims=True)
        b = jnp.sum(w0 * imag - w1 * real, axis=1, keepdims=True)
        pull_real = jnp.where(lane == i, a, pull_real)
        pull_imag = jnp.where(lane == i, b, pull_imag)
    spread_modes(1, pull_real, pull_imag)
    coarse_wait(2, ric)
    high, low = split(ric[...].reshape(64, 1024))
    along_z = dot3(high, low, zifull_h[...], zifull_l[...])
    high, low = split(jnp.concatenate([along_z[:, :256], along_z[:, 256:]], axis=0))
    along_y = dot3(*split(tic_in[...]), high, low)
    for hh in range(2):
        svc[pl.ds(hh, 128, stride=2), :] = along_y[:, 128 * hh : 128 * hh + 128]
    coarse_px(3, svc, gc)

    x_real, x_imag = modes[0], modes[1]
    for i in range(32):
        a, b = column(x_real, i), column(x_imag, i)
        gspec[0, i] = real * a + imag * b
        gspec[1, i] = imag * a - real * b
    writes.append(pltpu.make_async_copy(gspec, gspec_hbm, out_sem.at[2]))
    writes[1].start()
    for t in range(2):
        inverse_zy(1, t, g_hbm)
    coarse_wait(3, gc)
    halves_out = []
    for hh in range(2):
        high, low = split(gc[pl.ds(hh, 128, stride=2), :].T)
        halves_out.append(dot3(high, low, *split(ixc_in[...])))
    spectral_part = jnp.concatenate(halves_out, axis=0)
    lift_wide = kron_eye(rows_of(lift[...], 64, 2, 1), 2)
    coarse_wide = kron_eye(rows_of(w_coarse[...], 64, 2, 1), 2)
    project_wide = kron_eye(rows_of(project[...], 32, 2, 0), 2)
    high, low = split(rst2[...])
    lifted = dot(lift_wide, high) + dot(lift_wide, low)
    high, low = split(lifted)
    coarse_pre = spectral_part + dot(coarse_wide, high) + dot(coarse_wide, low)
    high, low = split(tanh_gelu(coarse_pre))
    coarse_out = dot(project_wide, high) + dot(project_wide, low)
    out_high, out_low = split(coarse_out)
    widen = ones_where((iota((512, 128), 0) >> 2) == iota((512, 128), 1))
    for big in range(2):
        stretch = ones_where(iota((128, 256), 0) == 64 * big + (iota((128, 256), 1) >> 2))
        high, low = split(dot(out_high, stretch) + dot(out_low, stretch))
        prolonged = dot(widen, high) + dot(widen, low)
        for small in range(4):
            y = 4 * big + small
            put(b2, y, block(b0, y) + prolonged)
    pack(layer_out, b2)
    writes.append(pltpu.make_async_copy(layer_out, layer_hbm, out_sem.at[1]))
    writes[2].start()

    for t in range(2):
        px_inverse_wait(1, t)

    for write in writes:
        write.wait()
    for wait in pending:
        wait()


def finish(g_ref, zero_ref, dir_ref, layer_ref, gspec_ref, ix_in, layer_out, grad_out, gspec_out, kept, mixed):
    second = pl.program_id(0) >= 2
    rows = iota((PAIRS, 128), 0)
    value = jnp.where(rows < 272, g_ref[0, 0], 0.0)
    zero = jnp.concatenate([zero_ref[0, 0], jnp.zeros((PAIRS - 8, 128), F32)], axis=0)
    kept[...] = jnp.where(jnp.logical_and(second, rows < 16), zero, value)
    table = stacked_table(ix_in[...])

    for y in range(8):
        some = synthesise_x(kept[pl.ds(y, 40, stride=8), :], table)
        for lane in range(2):
            at = slice(128 * lane, 128 * lane + 128)
            mixed[lane, pl.ds(y, 128, stride=8), :] = some[:, at] + dir_ref[lane, y]
    for lane in range(2):
        grad_out[:, :, pl.ds(128 * lane, 128)] = mixed[lane].reshape(128, 8, 128).astype(BF16)
    layer_out[...] = layer_ref[...]
    gspec_out[...] = gspec_ref[...]


def body(
    features, cotangent, pointwise_fine, spectral_fine, lift_weight, pointwise_coarse,
    spectral_coarse, project_weight,
):
    table = tables()
    fine = spectral_fine.transpose(0, 1, 3, 4, 5, 2).reshape(2, 32, 64, 32)
    coarse = spectral_coarse.transpose(0, 1, 3, 4, 5, 2).reshape(2, 64, 64, 64)
    hbm = pl.BlockSpec(memory_space=pl.ANY)

    def f32(*shape):
        return pltpu.VMEM(shape, F32)

    def bf16(*shape):
        return pltpu.VMEM(shape, BF16)

    dma = pltpu.SemaphoreType.DMA
    layer, direct, gspec, spectrum = pl.pallas_call(
        kernel,
        out_shape=[
            jax.ShapeDtypeStruct((512, 8, 256), BF16),
            jax.ShapeDtypeStruct((2, 4096, 128), F32),
            jax.ShapeDtypeStruct((2, 32, 64, 32), F32),
            jax.ShapeDtypeStruct((2, 2, PAIRS, 128), F32),
        ],
        in_specs=[hbm] * 20,
        out_specs=[hbm] * 4,
        scratch_shapes=[
            bf16(32, 32), bf16(32, 64), bf16(64, 64), bf16(32, 64), f32(40, 256), f32(40, 256), f32(64, 256),
            f32(128, 256), f32(128, 128), f32(128, 128),
            f32(2, 4096, 128), f32(2, 4096, 128), f32(2, 4096, 128),
            bf16(8, 512, 256), bf16(8, 512, 256), bf16(8, 512, 256),
            bf16(512, 8, 256), bf16(512, 8, 256), f32(2, 32, 64, 32), f32(2, 64, 64, 64),
            bf16(512, 8, 256), f32(2, 32, 64, 32),
            f32(256, 512), f32(256, 512), f32(256, 256), f32(128, 256),
            f32(512, 256), f32(512, 256), f32(2, 8, 1024), f32(16, 512),
            bf16(256, 1024), bf16(256, 1024), bf16(1024, 512), bf16(1024, 512),
            bf16(80, 256), bf16(128, 256), bf16(2, 256, 512), bf16(2, 256, 512), bf16(2, 256, 256), bf16(2, 128, 256),
            bf16(2, 512, 256), bf16(2, 512, 256),
            bf16(512, 512), bf16(512, 512), f32(256, 128), f32(2, 128, 256), f32(128, 128), f32(2, 64, 32),
            f32(2, 2, 2, PAIRS, 128), f32(2, 2, 512, 128), f32(2, 2, 512, 128), f32(2, 2, 16, 8, 128), f32(2, 2, 16, 8, 128),
            f32(2, 2, 2, 8, 128), f32(2, 2, 16, 8, 128), f32(2, 2, 2, 512, 128), f32(2, 2, PAIRS, 128),
            f32(256, 128), f32(256, 128), f32(8, 8, 512), f32(8, 8, 512), f32(8, 1024), f32(8, 8, 1024),
            f32(256, 128), f32(256, 128),
            dma((22,)), dma((3,)), dma((8,)), dma((8,)), dma((8,)), dma((8,)), dma((8,)), dma((8,)), dma((8,)),
            dma((4,)), dma((4,)), pltpu.SemaphoreType.REGULAR((3,)),
        ],
        compiler_params=pltpu.CompilerParams(
            collective_id=0, has_side_effects=True, vmem_limit_bytes=60 * 1024 * 1024
        ),
        name="fno_layer",
    )(
        features.reshape(512, 8, 256), cotangent.reshape(512, 8, 256), pointwise_fine, fine, lift_weight,
        pointwise_coarse, coarse, project_weight.T,
        table["tx"], table["ix"], table["ty"], table["zf"], table["zi"], table["ti"], table["txc"], table["tyc"],
        table["zfc"], table["zic"], table["tic"], table["ixc"],
    )
    layer_out, grad_out, gspec = pl.pallas_call(
        finish,
        grid=(4,),
        out_shape=[
            jax.ShapeDtypeStruct((512, 8, 256), BF16),
            jax.ShapeDtypeStruct((512, 8, 256), BF16),
            jax.ShapeDtypeStruct((2, 32, 64, 32), F32),
        ],
        in_specs=[
            pl.BlockSpec((1, 1, PAIRS, 128), lambda i: (i % 2, i // 2, 0, 0)),
            pl.BlockSpec((1, 1, 8, 128), lambda i: (i % 2, 0, 1, 0)),
            pl.BlockSpec((2, 8, 128, 128), lambda i: (0, 0, i, 0)),
            pl.BlockSpec((128, 8, 256), lambda i: (i, 0, 0)),
            pl.BlockSpec((2, 8, 64, 32), lambda i: (0, i, 0, 0)),
            pl.BlockSpec((40, 256), lambda i: (0, 0)),
        ],
        out_specs=[
            pl.BlockSpec((128, 8, 256), lambda i: (i, 0, 0)),
            pl.BlockSpec((128, 8, 256), lambda i: (i, 0, 0)),
            pl.BlockSpec((2, 8, 64, 32), lambda i: (0, i, 0, 0)),
        ],
        scratch_shapes=[f32(PAIRS, 128), f32(2, 1024, 128)],
        compiler_params=pltpu.CompilerParams(vmem_limit_bytes=60 * 1024 * 1024),
        name="finish",
    )(spectrum, spectrum, direct.reshape(2, 8, 512, 128), layer, gspec, table["ix"])
    shape = (32, 16, 8, 256)
    gspec = gspec.reshape(2, 32, 16, 1, 4, 32).transpose(0, 1, 5, 2, 3, 4)
    return layer_out.reshape(shape), grad_out.reshape(shape), gspec


def solution(mesh):
    placed = (
        P(None, "py", "px", None),
        P(None, "py", "px", None),
        P(),
        P(None, None, None, None, "px", "py"),
        P(),
        P(),
        P(None, None, None, None, "px", "py"),
        P(),
    )
    return jax.shard_map(
        body,
        mesh=mesh,
        in_specs=placed,
        out_specs=(
            P(None, "py", "px", None),
            P(None, "py", "px", None),
            P(None, None, None, None, "px", "py"),
        ),
        check_vma=False,
    )
```

```python
import functools
import math

import jax
import jax.numpy as jnp
import numpy as np
from jax import lax
from jax.experimental import pallas as pl
from jax.experimental.pallas import tpu as pltpu
from jax.sharding import PartitionSpec as P

M = 16
F32 = jnp.float32
BF16 = jnp.bfloat16
MESH = pl.DeviceIdType.MESH
NPX, NPY = 32, 8
PAIRS = 320
ROOT = math.sqrt(2.0 / math.pi)


def single(table):
    return np.asarray(table, np.float64).astype(np.float32)


def signed(index):
    return np.where(index < M, index, index - 2 * M)


def turn(freq, cell, count):
    return (np.asarray(freq) * np.asarray(cell) % count) * (2.0 * np.pi / count)


@functools.cache
def tables():
    out = {}
    x = np.arange(256)
    rows = np.zeros((40, 256))
    for j in range(17):
        angle = turn(j, x, 256)
        if j == 0:
            rows[0] = rows[1] = 1.0
        else:
            rows[2 * j] = np.cos(angle)
            rows[2 * j + 1] = -np.sin(angle) if j < 16 else np.sin(angle)
    out["tx"] = single(rows)
    inv = rows.copy()
    inv[1] = 0.0
    out["ix"] = single(inv)

    ky = np.arange(32)
    theta = turn(signed(ky)[:, None], np.arange(256)[None, :], 256)
    cos, sin = np.cos(theta), np.sin(theta)
    zero = np.zeros_like(cos)
    plus = (((cos, sin), (-sin, cos)))
    minus = (((cos, -sin), (-sin, -cos)))
    from0 = (((cos, zero), (-sin, zero)))
    from1 = (((zero, cos), (zero, -sin)))
    none = (((zero, zero), (zero, zero)))
    kinds = [(plus, minus), (minus, plus), (from0, from1), (plus, none), (none, plus)]
    ty = np.zeros((5, 2, 2, 8, 2, 4, 32, 2, 8))
    for k, pair in enumerate(kinds):
        for q in range(2):
            for r1 in range(2):
                for r in range(2):
                    block = pair[q][r1][r].reshape(8, 4, 32, 8)
                    for dup in range(2):
                        ty[k, r1, q, :, dup, :, :, r, :] = block
    ty = ty.reshape(5, 256, 512)
    out["ty"] = single(ty)

    ti = np.zeros((5, 32, 2, 8, 2, 2, 8, 2, 4))

    def add(k, rout, q, part, sign):
        c = cos.T.reshape(32, 8, 8, 4)
        s = sin.T.reshape(32, 8, 8, 4)
        if part == 0:
            coef = {(0, 0): c, (1, 1): -c, (0, 1): -s, (1, 0): -s}
        else:
            coef = {(0, 0): s, (1, 1): -s, (0, 1): c, (1, 0): c}
        for (cs, r), value in coef.items():
            ti[k, :, rout, :, cs, q, :, r, :] += sign * value

    for k, first in ((0, 1.0), (1, -1.0)):
        add(k, 0, 0, 0, 1.0)
        add(k, 0, 1, 0, 1.0)
        add(k, 1, 0, 1, first)
        add(k, 1, 1, 1, -first)
    add(2, 0, 0, 0, 1.0)
    add(2, 1, 1, 0, 1.0)
    for k, q in ((3, 0), (4, 1)):
        add(k, 0, q, 0, 1.0)
        add(k, 1, q, 1, 1.0)
    out["ti"] = single(ti.reshape(5, 512, 256))

    kz = np.arange(16)
    zf = np.zeros((8, 2, 8, 16, 2, 8, 16))
    zi = np.zeros((8, 8, 16, 2, 8, 16))
    for b in range(8):
        phi = turn(kz[None, :], (b * 16 + np.arange(16))[:, None], 128)
        for c in range(8):
            zf[b, 0, c, :, 0, c, :] = np.cos(phi)
            zf[b, 1, c, :, 0, c, :] = np.sin(phi)
            zf[b, 0, c, :, 1, c, :] = -np.sin(phi)
            zf[b, 1, c, :, 1, c, :] = np.cos(phi)
            zi[b, c, :, 0, c, :] = np.cos(phi).T
            zi[b, c, :, 1, c, :] = np.sin(phi).T
    out["zf"] = single(zf.reshape(8, 256, 256))
    out["zi"] = single(zi.reshape(8, 128, 256))

    kx = np.arange(32)
    alpha = turn(signed(kx)[:, None], (x // 4)[None, :], 64)
    txc = np.stack([np.cos(alpha), -np.sin(alpha)], axis=1).reshape(64, 256)
    out["txc"] = single(txc)
    theta = turn(signed(ky)[:, None], np.arange(64)[None, :], 64)
    cos, sin = np.cos(theta), np.sin(theta)
    tyc = np.zeros((2, 8, 2, 4, 32, 2, 4))
    plus = ((cos, sin), (-sin, cos))
    for r1 in range(2):
        for r in range(2):
            for dup in range(2):
                tyc[r1, :, dup, :, :, r, :2] = plus[r1][r].reshape(8, 4, 32, 2)
    out["tyc"] = single(tyc.reshape(128, 256))
    tic = np.zeros((32, 2, 2, 2, 8, 2, 4))
    c = cos.T.reshape(32, 2, 8, 4)
    s = sin.T.reshape(32, 2, 8, 4)
    for (rout, cs, r), value in {
        (0, 0, 0): c, (0, 1, 1): -c, (0, 0, 1): -s, (0, 1, 0): -s,
        (1, 0, 0): s, (1, 1, 1): -s, (1, 0, 1): c, (1, 1, 0): c,
    }.items():
        tic[:, rout, :, cs, :, r, :] = value
    out["tic"] = single(tic.reshape(128, 128))
    zfc = np.zeros((8, 2, 2, 4, 2, 32, 16))
    zic = np.zeros((8, 16, 2, 64, 4))
    for b in range(8):
        phi = turn(kz[None, :], (b * 4 + np.arange(4))[:, None], 32)
        zfc[b, 0, :, :, 0] = np.cos(phi)[None, :, None, :]
        zfc[b, 1, :, :, 0] = np.sin(phi)[None, :, None, :]
        zfc[b, 0, :, :, 1] = -np.sin(phi)[None, :, None, :]
        zfc[b, 1, :, :, 1] = np.cos(phi)[None, :, None, :]
        zic[b, :, 0] = np.cos(phi).T[:, None, :]
        zic[b, :, 1] = np.sin(phi).T[:, None, :]
    out["zfc"] = single(zfc.reshape(8, 2, 8, 1024))
    out["zic"] = single(zic.reshape(8, 16, 512))
    alpha = turn(signed(kx)[:, None], np.arange(64)[None, :], 64)
    ixc = np.zeros((32, 2, 2, 2, 64))
    for big in range(2):
        ixc[:, 0, big, big] = np.cos(alpha)
        ixc[:, 1, big, big] = -np.sin(alpha)
    out["ixc"] = single(ixc.reshape(128, 128))
    return out


def split(value):
    high = value.astype(BF16)
    return high, (value - high.astype(F32)).astype(BF16)


def dot(left, right, dims=((1,), (0,))):
    return lax.dot_general(left, right, (dims, ((), ())), preferred_element_type=F32)


def dot3(left_high, left_low, right_high, right_low, dims=((1,), (0,))):
    return (
        dot(left_high, right_high, dims)
        + dot(left_high, right_low, dims)
        + dot(left_low, right_high, dims)
    )


def iota(shape, dim):
    return lax.broadcasted_iota(jnp.int32, shape, dim)


def ones_where(condition):
    return jnp.where(condition, 1.0, 0.0).astype(BF16)


def kron_eye(first, shift):
    rows, m = first.shape
    spread = ones_where(iota((m, m << shift), 0) == (iota((m, m << shift), 1) >> shift))
    full = dot(first.astype(BF16), spread)
    low = (1 << shift) - 1
    shape = (rows, m << shift)
    return jnp.where((iota(shape, 0) & low) == (iota(shape, 1) & low), full, 0.0).astype(BF16)


def rows_of(weight, n, shift, axis):
    pick = ones_where((iota((n << shift, n), 0) >> shift) == iota((n << shift, n), 1))
    return dot(pick, weight, ((1,), (axis,)))


def to_modes(packed, count):
    lanes = count * 16
    real = jnp.concatenate([packed[0:4]] * 16, axis=0)
    imag = jnp.concatenate([packed[4:8]] * 16, axis=0)
    mask = (iota((64, lanes), 0) >> 2) == (iota((64, lanes), 1) & 15)
    wide = jnp.concatenate([jnp.where(mask, real, 0.0), jnp.where(mask, imag, 0.0)], axis=0)
    pick = ones_where((iota((lanes, count), 0) >> 4) == iota((lanes, count), 1))
    high, low = split(wide)
    modes = dot(high, pick) + dot(low, pick)
    return modes[:64], modes[64:]


def from_modes(real, imag, count):
    lanes = count * 16
    high, low = split(jnp.concatenate([real, imag], axis=0))
    spread = ones_where(iota((count, lanes), 0) == (iota((count, lanes), 1) >> 4))
    wide = dot(high, spread) + dot(low, spread)
    mask = ((iota((128, lanes), 0) & 63) >> 2) == (iota((128, lanes), 1) & 15)
    high, low = split(jnp.where(mask, wide, 0.0))
    shape = (8, 128)
    total = ones_where(
        ((iota(shape, 1) >> 6) == (iota(shape, 0) >> 2)) & ((iota(shape, 1) & 3) == (iota(shape, 0) & 3))
    )
    return dot(total, high) + dot(total, low)


def column(values, index):
    return values[:, index : index + 1]


def mix_modes(weight_ref, real, imag, count):
    out_real = jnp.zeros((64, count), F32)
    out_imag = jnp.zeros((64, count), F32)
    for i in range(count):
        w0, w1 = weight_ref[0, i], weight_ref[1, i]
        a, b = column(real, i), column(imag, i)
        out_real = out_real + (w0 * a - w1 * b)
        out_imag = out_imag + (w0 * b + w1 * a)
    return out_real, out_imag


def mode_factor(cells):
    return jnp.where(iota((64, 1), 0) < 4, 1.0 / cells, 2.0 / cells).astype(F32)


def stacked_table(table):
    high, low = split(table)
    high, low = high.astype(F32), low.astype(F32)
    return jnp.concatenate([high, high, low, jnp.zeros((8, 256), F32)], axis=0).astype(BF16)


def synthesise_x(value, table):
    high = value.astype(BF16).astype(F32)
    pad = jnp.zeros((8, value.shape[1]), F32)
    stacked = jnp.concatenate([high, value - high, high, pad], axis=0)
    return dot(stacked.T.astype(BF16), table)


def tanh_gelu(value):
    return 0.5 * value * (1.0 + jnp.tanh(ROOT * (value + 0.044715 * value * value * value)))


def kernel(
    feat_hbm, cot_hbm, w_fine_hbm, spec_hbm, lift_hbm, w_coarse_hbm, spec_c_hbm, project_hbm,
    tx_hbm, ix_hbm, ty_hbm, zf_hbm, zi_hbm, ti_hbm, txc_hbm, tyc_hbm, zfc_hbm, zic_hbm, tic_hbm, ixc_hbm,
    layer_hbm, dir_hbm, gspec_hbm, g_hbm,
    w_fine, lift, w_coarse, project, tx_in, ix_in, txc_in, tyc_in, tic_in, ixc_in,
    b0, b1, b2, fy, gph, gpl, feat, cot, spec, spec_c, layer_out, gspec,
    ty, tye, zf, zi, ti, tie, zfc, zic, zfull_h, zfull_l, zifull_h, zifull_l,
    tx, ix, ty_s, tye_s, zf_s, zi_s, ti_s, tie_s,
    wk, wkt, yc, rst, rst2, modes,
    s_buf, rx, rxe, ex, re_buf, hq, ri, sv, g_buf,
    sc, rc, exc, rec, hc, ric, svc, gc,
    load_sem, out_sem, px_send, px_recv, pxe_send, pxe_recv, py_send, py_recv, pye_send,
    c_send, c_recv, here,
):
    me = lax.axis_index("px")
    mine = lax.axis_index("py")
    partner = lax.rem(NPX - me, NPX)
    upper = lax.div(me + 15, 32)
    is0 = 1 - lax.div(me + 31, 32)
    is16 = lax.div(me, 16) * (1 - upper)
    kind = upper + 2 * is0 + 3 * is16
    regular = 1 - is0 - is16

    loads = [
        (feat_hbm, feat), (tx_hbm, tx_in), (ix_hbm, ix_in), (txc_hbm, txc_in), (w_fine_hbm, w_fine),
        (lift_hbm, lift), (w_coarse_hbm, w_coarse), (project_hbm, project), (tyc_hbm, tyc_in),
        (tic_hbm, tic_in), (ixc_hbm, ixc_in),
        (cot_hbm, cot), (spec_hbm, spec), (spec_c_hbm, spec_c),
        (ty_hbm.at[kind], ty), (ty_hbm.at[4], tye), (zf_hbm.at[mine], zf), (zi_hbm.at[mine], zi),
        (ti_hbm.at[kind], ti), (ti_hbm.at[4], tie), (zfc_hbm.at[mine], zfc), (zic_hbm.at[mine], zic),
    ]
    loads = [pltpu.make_async_copy(a, b, load_sem.at[n]) for n, (a, b) in enumerate(loads)]
    for load in loads[:4]:
        load.start()

    barrier = pltpu.get_barrier_semaphore()
    row = 8 * lax.div(me, 8)

    def tell(semaphore, px, py):
        pl.semaphore_signal(semaphore, inc=1, device_id={"px": px, "py": py}, device_id_type=MESH)

    for t in range(1, 8):
        tell(barrier, row + lax.rem(me + t, 8), mine)
    for t in range(1, 4):
        tell(barrier, lax.rem(me + 8 * t, NPX), mine)
    for t in range(1, 4):
        tell(barrier, me, lax.rem(mine + 2 * t, NPY))
    other = 2 * lax.div(mine, 2) + 1 - lax.rem(mine, 2)
    tell(barrier, me, other)
    for load in loads[4:]:
        load.start()
    pl.semaphore_wait(barrier, 14)
    for t in range(1, 4):
        tell(here.at[0], lax.rem(me + 8 * t, NPX), mine)

    def pair_row(d):
        h = lax.div(d + 15, 32)
        return h, pl.multiple_of(16 * (d * (1 - 2 * h) + 32 * h), 16)

    pending = []

    def left(semaphore, ref, condition=None):
        def wait():
            pltpu.make_async_copy(ref, ref, semaphore).wait()

        pending.append(wait if condition is None else lambda: pl.when(condition)(wait))

    slab, side = lax.div(mine, 2), lax.rem(mine, 2)

    def each_px(send):
        def step(t, carry):
            send(lax.rem(me + t, NPX))
            return carry

        lax.fori_loop(1, NPX, step, 0)

    def each_py(send):
        for far, ahead in ((1, 2), (1, 1), (1, 3), (1, 0), (0, 2), (0, 1), (0, 3)):
            send(2 * lax.rem(slab + ahead, 4) + (1 - side if far else side))

    def at16(d):
        return pl.ds(pl.multiple_of(16 * d, 16), 16)

    def px_forward(n, t):
        k = 4 * n + t
        left(px_send.at[k], rx.at[0, 0, pl.ds(0, 496)])
        left(pxe_send.at[k], rx.at[0, 0, pl.ds(0, 16)], is16 == 0)

        def send(d):
            h, row = pair_row(d)
            pltpu.make_async_remote_copy(
                s_buf.at[n, t, h, pl.ds(row, 16)], rx.at[n, t, at16(me)],
                px_send.at[k], px_recv.at[k], device_id={"px": d, "py": mine}, device_id_type=MESH,
            ).start()

        each_px(send)
        h, row = pair_row(me)
        pltpu.make_async_copy(s_buf.at[n, t, h, pl.ds(row, 16)], rx.at[n, t, at16(me)], px_recv.at[k]).start()

        @pl.when(is16 == 0)
        def _():
            pltpu.make_async_remote_copy(
                s_buf.at[n, t, 1, pl.ds(256, 16)], rxe.at[n, t, at16(me)],
                pxe_send.at[k], pxe_recv.at[k], device_id={"px": 16, "py": mine}, device_id_type=MESH,
            ).start()

        @pl.when(is16 == 1)
        def _():
            pltpu.make_async_copy(
                s_buf.at[n, t, 1, pl.ds(256, 16)], rxe.at[n, t, at16(me)], pxe_recv.at[k]
            ).start()

    def px_forward_wait(n, t):
        k = 4 * n + t
        pltpu.make_async_copy(rx.at[n, t], rx.at[n, t], px_recv.at[k]).wait()

        @pl.when(is16 == 1)
        def _():
            pltpu.make_async_copy(rxe.at[n, t], rxe.at[n, t], pxe_recv.at[k]).wait()

    def px_inverse(n, t, target):
        k = 4 * n + 2 + t
        left(px_send.at[k], rx.at[0, 0, pl.ds(0, 496)], is16 == 0)
        left(px_send.at[k], rx.at[0, :, pl.ds(0, 496)], is16 == 1)
        h, row = pair_row(me)

        @pl.when(is16 == 0)
        def _():
            def send(d):
                pltpu.make_async_remote_copy(
                    sv.at[n, t, 0, at16(d)], target.at[t, h, pl.ds(row, 16)],
                    px_send.at[k], px_recv.at[k], device_id={"px": d, "py": mine}, device_id_type=MESH,
                ).start()

            each_px(send)
            pltpu.make_async_copy(
                sv.at[n, t, 0, at16(me)], target.at[t, h, pl.ds(row, 16)], px_recv.at[k]
            ).start()

        @pl.when(is16 == 1)
        def _():
            def send(d):
                pltpu.make_async_remote_copy(
                    sv.at[n, t, :, at16(d)], target.at[t, :, pl.ds(256, 16)],
                    px_send.at[k], px_recv.at[k], device_id={"px": d, "py": mine}, device_id_type=MESH,
                ).start()

            each_px(send)
            pltpu.make_async_copy(
                sv.at[n, t, :, at16(me)], target.at[t, :, pl.ds(256, 16)], px_recv.at[k]
            ).start()

    def px_inverse_wait(n, t):
        some = rx.at[n, :, pl.ds(0, 264)]
        pltpu.make_async_copy(some, some, px_recv.at[4 * n + 2 + t]).wait()

    def py_exchange(slot, source, target):
        left(py_send.at[slot], ex.at[0, 0, pl.ds(0, 14)])
        left(pye_send.at[slot], ex.at[0, 0, 0], regular == 1)

        def send(p):
            for q, to in ((1, partner), (0, me)):
                pltpu.make_async_remote_copy(
                    source(q, p), target.at[8 * q + mine], py_send.at[slot], py_recv.at[slot],
                    device_id={"px": to, "py": p}, device_id_type=MESH,
                ).start()

        each_py(send)
        pltpu.make_async_copy(source(0, mine), target.at[mine], py_recv.at[slot]).start()

        @pl.when(regular == 1)
        def _():
            pltpu.make_async_remote_copy(
                source(1, mine), target.at[8 + mine], pye_send.at[slot], py_recv.at[slot],
                device_id={"px": partner, "py": mine}, device_id_type=MESH,
            ).start()

        @pl.when(regular == 0)
        def _():
            pltpu.make_async_copy(source(1, mine), target.at[8 + mine], py_recv.at[slot]).start()

    def py_wait(slot, target):
        pltpu.make_async_copy(target, target, py_recv.at[slot]).wait()

    def coarse_px(slot, source, target):
        left(c_send.at[slot], target.at[pl.ds(0, 248)])
        there = target.at[pl.ds(pl.multiple_of(8 * me, 8), 8)]

        def send(d):
            pltpu.make_async_remote_copy(
                source.at[pl.ds(pl.multiple_of(8 * d, 8), 8)], there, c_send.at[slot], c_recv.at[slot],
                device_id={"px": d, "py": mine}, device_id_type=MESH,
            ).start()

        each_px(send)
        pltpu.make_async_copy(source.at[pl.ds(pl.multiple_of(8 * me, 8), 8)], there, c_recv.at[slot]).start()

    def coarse_py(slot, source, target):
        left(c_send.at[slot], target.at[pl.ds(0, 7)])

        def send(p):
            pltpu.make_async_remote_copy(
                source(p), target.at[mine], c_send.at[slot], c_recv.at[slot],
                device_id={"px": me, "py": p}, device_id_type=MESH,
            ).start()

        each_py(send)
        pltpu.make_async_copy(source(mine), target.at[mine], c_recv.at[slot]).start()

    def coarse_wait(slot, target):
        pltpu.make_async_copy(target, target, c_recv.at[slot]).wait()

    def fix_zero(n, t):
        s_buf[n, t, 0, pl.ds(8, 8), :] = s_buf[n, t, 1, pl.ds(0, 8), :]

    def forward_yz(n, t):
        high, low = split(rx[n, t])
        yc[...] = dot3(ty_s[0], ty_s[1], high, low)

        @pl.when(is16 == 1)
        def _():
            high, low = split(rxe[n, t])
            yc[...] += dot3(tye_s[0], tye_s[1], high, low)

        dup = ((iota((128, 128), 0) >> 2) & 1) == 0
        both = jnp.concatenate([yc[pl.ds(0, 128), :], yc[pl.ds(128, 128), :]], axis=1)
        high, low = split(both)
        full = dot3(high, low, zf_s[0], zf_s[1])
        ex[n, t] = jnp.where(dup, full[:, :128], full[:, 128:]).reshape(16, 8, 128)
        py_exchange(4 * n + t, lambda q, p: ex.at[n, t, 8 * q + p], re_buf.at[n, t])

    def gather_modes(n):
        slots = []
        for q in range(2):
            parts = []
            for t in range(2):
                if q == 0:
                    py_wait(4 * n + t, re_buf.at[n, t])
                parts.append(jnp.sum(re_buf[n, t, 8 * q : 8 * q + 8], axis=0))
            slots.append(jnp.concatenate(parts, axis=1))
        swap = upper == 1
        first = jnp.where(swap, slots[1], slots[0])
        second = jnp.where(swap, slots[0], slots[1])
        return to_modes(jnp.concatenate([first, second], axis=1), 32)

    def spread_modes(n, real, imag):
        packed = from_modes(real, imag, 32)
        swap = upper == 1
        for t in range(2):
            first, second = packed[:, 128 * t : 128 * t + 128], packed[:, 256 + 128 * t : 384 + 128 * t]
            hq[n, t, 0] = jnp.where(swap, second, first)
            hq[n, t, 1] = jnp.where(swap, first, second)
            py_exchange(4 * n + 2 + t, lambda q, p: hq.at[n, t, q], ri.at[n, t])

    def inverse_zy(n, t, target):
        py_wait(4 * n + 2 + t, ri.at[n, t])
        high, low = split(ri[n, t].reshape(128, 128))
        full = dot3(high, low, zi_s[0], zi_s[1])
        high, low = split(jnp.concatenate([full[:, :128], full[:, 128:]], axis=0))
        sv[n, t, 0] = dot3(ti_s[0], ti_s[1], high, low)

        @pl.when(is16 == 1)
        def _():
            sv[n, t, 1] = dot3(tie_s[0], tie_s[1], high, low)

        px_inverse(n, t, target)

    def rows_at(h, t):
        return 256 * h + 128 * t

    def take(ref, t, y):
        return jnp.concatenate(
            [
                jnp.concatenate(
                    [ref[lane, pl.ds(8 * rows_at(h, t) + y, 128, stride=8), :] for lane in range(2)], axis=1
                )
                for h in range(2)
            ],
            axis=0,
        )

    def put(ref, y, value):
        for lane in range(2):
            ref[lane, pl.ds(y, 512, stride=8), :] = value[:, 128 * lane : 128 * lane + 128]

    def block(ref, y):
        rows = pl.ds(pl.multiple_of(512 * y, 512), 512)
        return jnp.concatenate([ref[0, rows, :], ref[1, rows, :]], axis=1)

    def put_block(ref, y, value):
        rows = pl.ds(pl.multiple_of(512 * y, 512), 512)
        ref[0, rows, :] = value[:, :128]
        ref[1, rows, :] = value[:, 128:]

    def part_rows(h, t, y):
        return pl.ds(pl.multiple_of(512 * y + rows_at(h, t), 128), 128)

    def some_rows(ref, t, y):
        return jnp.concatenate(
            [
                jnp.concatenate([ref[lane, part_rows(h, t, y), :] for lane in range(2)], axis=1)
                for h in range(2)
            ],
            axis=0,
        )

    def put_part(ref, t, y, value):
        for h in range(2):
            for lane in range(2):
                ref[lane, part_rows(h, t, y), :] = value[128 * h : 128 * h + 128, 128 * lane : 128 * lane + 128]

    def put_rows(ref, t, y, value):
        for h in range(2):
            ref[y, pl.ds(rows_at(h, t), 128), :] = value[128 * h : 128 * h + 128]

    def unpack(ref, field, t):
        for h in range(2):
            for lane in range(2):
                some = field[pl.ds(rows_at(h, t), 128), :, pl.ds(128 * lane, 128)]
                ref[lane, pl.ds(8 * rows_at(h, t), 1024), :] = some.astype(F32).reshape(1024, 128)

    def pack(field, ref):
        for lane in range(2):
            field[:, :, pl.ds(128 * lane, 128)] = ref[lane].reshape(512, 8, 128).astype(BF16)

    def store_pairs(n, t, y, both):
        for h in range(2):
            s_buf[n, t, h, pl.ds(y, 40, stride=8), :] = both[:, 128 * h : 128 * h + 128]

    for n in range(4):
        loads[n].wait()
    high, low = split(tx_in[...])
    tx[pl.ds(0, 40), :] = high
    tx[pl.ds(40, 40), :] = low
    ix[...] = stacked_table(ix_in[...])
    for t in range(2):
        unpack(b0, feat, t)

        def analyse_x(y, carry):
            field = take(b0, t, y).astype(BF16)
            put_rows(fy, t, y, field)
            both = dot(tx[...], field, ((1,), (1,)))
            store_pairs(0, t, y, both[:40] + both[40:])
            return carry

        lax.fori_loop(0, 8, analyse_x, 0, unroll=2)
        fix_zero(0, t)
        if t == 0:
            pl.semaphore_wait(here.at[0], 3)
        px_forward(0, t)
    for t in range(1, 4):
        tell(here.at[1], me, lax.rem(mine + 2 * t, NPY))
    g_buf[:, :, pl.ds(272, 48), :] = jnp.zeros((2, 2, 48, 128), F32)
    g_buf[:, 1, pl.ds(0, 16), :] = jnp.zeros((2, 16, 128), F32)
    sc[...] = jnp.zeros((256, 128), F32)

    for n in range(4, 11):
        loads[n].wait()

    txc_high, txc_low = split(txc_in[...])
    pool = ones_where(iota((128, 512), 0) == (iota((128, 512), 1) >> 2))
    for big in range(2):
        total = dot(pool, fy[4 * big])
        for y in range(1, 4):
            total = total + dot(pool, fy[4 * big + y])
        total = total * (1.0 / 64.0)
        rst[big] = total
        high, low = split(total)
        part = dot3(txc_high, txc_low, high, low, ((1,), (1,)))
        sc[pl.ds(big, 64, stride=4), :] = part
    pl.semaphore_wait(here.at[1], 3)
    tell(here.at[2], me, other)

    wk[...] = kron_eye(rows_of(w_fine[...], 32, 4, 1), 4)
    wkt[...] = kron_eye(rows_of(w_fine[...], 32, 4, 0), 4)

    def local(y, carry):
        put_block(b2, y, dot(wk[...], fy[y]))
        return carry

    lax.fori_loop(0, 8, local, 0)
    loads[11].wait()
    for t in range(2):
        unpack(b1, cot, t)
    low_total = jnp.zeros((128, 128), F32)
    for big in range(2):
        gather = ones_where(iota((256, 128), 1) == 64 * big + (iota((256, 128), 0) >> 2))
        high, low = split(rst[big])
        low_total = low_total + dot(high, gather) + dot(low, gather)
    rst2[...] = low_total
    for n in range(12, 22):
        loads[n].wait()
    for whole, parts in ((ty, ty_s), (tye, tye_s), (zf, zf_s), (zi, zi_s), (ti, ti_s), (tie, tie_s)):
        high, low = split(whole[...])
        parts[0] = high
        parts[1] = low
    base_mask = (iota((128, 1024), 0) >> 2) == ((iota((128, 1024), 1) & 511) >> 4)
    for r in range(2):
        full = jnp.where(base_mask, jnp.concatenate([zfc[r]] * 16, axis=0), 0.0)
        high, low = split(full)
        zfull_h[pl.ds(128 * r, 128), :] = high
        zfull_l[pl.ds(128 * r, 128), :] = low

    def build(step, carry):
        rows = 128 * step + iota((128, 512), 0)
        keep = (rows >> 4) == ((iota((128, 512), 1) & 255) >> 2)
        high, low = split(jnp.where(keep, jnp.concatenate([zic[...]] * 8, axis=0), 0.0))
        at = pl.ds(pl.multiple_of(128 * step, 128), 128)
        zifull_h[at, :] = high
        zifull_l[at, :] = low
        return carry

    lax.fori_loop(0, 8, build, 0)

    pl.semaphore_wait(here.at[2], 1)
    for t in range(2):
        px_forward_wait(0, t)
        forward_yz(0, t)

    coarse_px(0, sc, rc)

    real, imag = gather_modes(0)
    modes[0] = real
    modes[1] = imag
    out_real, out_imag = mix_modes(spec, real, imag, 32)
    fine_factor = mode_factor(256.0 * 256.0 * 128.0)
    spread_modes(0, out_real * fine_factor, out_imag * fine_factor)

    coarse_wait(0, rc)
    high, low = split(rc[...])
    along_y = dot3(*split(tyc_in[...]), high, low)
    high, low = split(jnp.concatenate([along_y[:64], along_y[64:]], axis=1))
    full = dot3(high, low, zfull_h[...], zfull_l[...])
    dup = ((iota((64, 512), 0) >> 2) & 1) == 0
    exc[...] = jnp.where(dup, full[:, :512], full[:, 512:]).reshape(8, 8, 512)
    coarse_py(1, lambda p: exc.at[p], rec)

    for t in range(2):
        inverse_zy(0, t, g_buf)

    for t in range(2):
        px_inverse_wait(0, t)
        g_buf[t, 1, pl.ds(0, 8), :] = g_buf[t, 0, pl.ds(8, 8), :]

        def middle(y, carry):
            value = jnp.concatenate([g_buf[t, h, pl.ds(y, 40, stride=8), :] for h in range(2)], axis=1)
            pre = some_rows(b2, t, y) + synthesise_x(value, ix[...])
            square = pre * pre
            half = 0.5 + 0.5 * jnp.tanh(pre * (ROOT + (0.044715 * ROOT) * square))
            act = pre * half
            put_part(b0, t, y, act)
            slope = half + act * (1.0 - half) * (2.0 * ROOT + (6.0 * 0.044715 * ROOT) * square)
            high, low = split(take(b1, t, y) * slope)
            put_rows(gph, t, y, high)
            put_rows(gpl, t, y, low)
            both = dot(tx[...], high, ((1,), (1,)))
            store_pairs(1, t, y, both[:40] + both[40:] + dot(tx[pl.ds(0, 40), :], low, ((1,), (1,))))
            return carry

        lax.fori_loop(0, 8, middle, 0, unroll=2)
        fix_zero(1, t)
        px_forward(1, t)

    def direct(y, carry):
        put_block(b1, y, dot(wkt[...], gph[y]) + dot(wkt[...], gpl[y]))
        return carry

    lax.fori_loop(0, 8, direct, 0)
    writes = [pltpu.make_async_copy(b1, dir_hbm, out_sem.at[0])]
    writes[0].start()

    coarse_wait(1, rec)
    real, imag = to_modes(jnp.sum(rec[...], axis=0), 32)
    high, low = split(jnp.concatenate([real, imag], axis=0))
    lifted = dot(high, lift[...]) + dot(low, lift[...])
    out_real, out_imag = mix_modes(spec_c, lifted[:64], lifted[64:], 64)
    coarse_factor = mode_factor(64.0 * 64.0 * 32.0)
    hc[...] = from_modes(out_real * coarse_factor, out_imag * coarse_factor, 64)
    for t in range(2):
        px_forward_wait(1, t)
        forward_yz(1, t)
    coarse_py(2, lambda p: hc, ric)

    real, imag = gather_modes(1)
    real, imag = real * fine_factor, imag * fine_factor
    lane = iota((64, 32), 1)
    pull_real = jnp.zeros((64, 32), F32)
    pull_imag = jnp.zeros((64, 32), F32)
    for i in range(32):
        w0, w1 = spec[0, i], spec[1, i]
        a = jnp.sum(w0 * real + w1 * imag, axis=1, keepdims=True)
        b = jnp.sum(w0 * imag - w1 * real, axis=1, keepdims=True)
        pull_real = jnp.where(lane == i, a, pull_real)
        pull_imag = jnp.where(lane == i, b, pull_imag)
    spread_modes(1, pull_real, pull_imag)
    coarse_wait(2, ric)
    high, low = split(ric[...].reshape(64, 1024))
    along_z = dot3(high, low, zifull_h[...], zifull_l[...])
    high, low = split(jnp.concatenate([along_z[:, :256], along_z[:, 256:]], axis=0))
    along_y = dot3(*split(tic_in[...]), high, low)
    for hh in range(2):
        svc[pl.ds(hh, 128, stride=2), :] = along_y[:, 128 * hh : 128 * hh + 128]
    coarse_px(3, svc, gc)

    x_real, x_imag = modes[0], modes[1]
    for i in range(32):
        a, b = column(x_real, i), column(x_imag, i)
        lanes = pl.ds(32 * (i % 4), 32)
        gspec[0, i // 4, :, lanes] = real * a + imag * b
        gspec[1, i // 4, :, lanes] = imag * a - real * b
    writes.append(pltpu.make_async_copy(gspec, gspec_hbm, out_sem.at[2]))
    writes[1].start()
    for t in range(2):
        inverse_zy(1, t, g_hbm)
    coarse_wait(3, gc)
    halves_out = []
    for hh in range(2):
        high, low = split(gc[pl.ds(hh, 128, stride=2), :].T)
        halves_out.append(dot3(high, low, *split(ixc_in[...])))
    spectral_part = jnp.concatenate(halves_out, axis=0)
    lift_wide = kron_eye(rows_of(lift[...], 64, 2, 1), 2)
    coarse_wide = kron_eye(rows_of(w_coarse[...], 64, 2, 1), 2)
    project_wide = kron_eye(rows_of(project[...], 32, 2, 0), 2)
    high, low = split(rst2[...])
    lifted = dot(lift_wide, high) + dot(lift_wide, low)
    high, low = split(lifted)
    coarse_pre = spectral_part + dot(coarse_wide, high) + dot(coarse_wide, low)
    high, low = split(tanh_gelu(coarse_pre))
    coarse_out = dot(project_wide, high) + dot(project_wide, low)
    out_high, out_low = split(coarse_out)
    widen = ones_where((iota((512, 128), 0) >> 2) == iota((512, 128), 1))
    for big in range(2):
        stretch = ones_where(iota((128, 256), 0) == 64 * big + (iota((128, 256), 1) >> 2))
        high, low = split(dot(out_high, stretch) + dot(out_low, stretch))
        prolonged = dot(widen, high) + dot(widen, low)
        for small in range(4):
            y = 4 * big + small
            put(b2, y, block(b0, y) + prolonged)
    pack(layer_out, b2)
    writes.append(pltpu.make_async_copy(layer_out, layer_hbm, out_sem.at[1]))
    writes[2].start()

    for t in range(2):
        px_inverse_wait(1, t)

    for write in writes:
        write.wait()
    for wait in pending:
        wait()


def finish(g_ref, zero_ref, dir_ref, layer_ref, gspec_ref, ix_in, layer_out, grad_out, gspec_out, kept, mixed):
    second = pl.program_id(0) >= 2
    rows = iota((PAIRS, 128), 0)
    value = jnp.where(rows < 272, g_ref[0, 0], 0.0)
    zero = jnp.concatenate([zero_ref[0, 0], jnp.zeros((PAIRS - 8, 128), F32)], axis=0)
    kept[...] = jnp.where(jnp.logical_and(second, rows < 16), zero, value)
    table = stacked_table(ix_in[...])

    for y in range(8):
        some = synthesise_x(kept[pl.ds(y, 40, stride=8), :], table)
        for lane in range(2):
            at = slice(128 * lane, 128 * lane + 128)
            mixed[lane, pl.ds(y, 128, stride=8), :] = some[:, at] + dir_ref[lane, y]
    for lane in range(2):
        grad_out[:, :, pl.ds(128 * lane, 128)] = mixed[lane].reshape(128, 8, 128).astype(BF16)
    layer_out[...] = layer_ref[...]
    for c in range(8):
        gspec_out[:, c] = gspec_ref[:, c // 4, :, 32 * (c % 4) : 32 * (c % 4) + 32]


def body(
    features, cotangent, pointwise_fine, spectral_fine, lift_weight, pointwise_coarse,
    spectral_coarse, project_weight,
):
    table = tables()
    fine = spectral_fine.transpose(0, 1, 3, 4, 5, 2).reshape(2, 32, 64, 32)
    coarse = spectral_coarse.transpose(0, 1, 3, 4, 5, 2).reshape(2, 64, 64, 64)
    hbm = pl.BlockSpec(memory_space=pl.ANY)

    def f32(*shape):
        return pltpu.VMEM(shape, F32)

    def bf16(*shape):
        return pltpu.VMEM(shape, BF16)

    dma = pltpu.SemaphoreType.DMA
    layer, direct, gspec, spectrum = pl.pallas_call(
        kernel,
        out_shape=[
            jax.ShapeDtypeStruct((512, 8, 256), BF16),
            jax.ShapeDtypeStruct((2, 4096, 128), F32),
            jax.ShapeDtypeStruct((2, 8, 64, 128), F32),
            jax.ShapeDtypeStruct((2, 2, PAIRS, 128), F32),
        ],
        in_specs=[hbm] * 20,
        out_specs=[hbm] * 4,
        scratch_shapes=[
            bf16(32, 32), bf16(32, 64), bf16(64, 64), bf16(32, 64), f32(40, 256), f32(40, 256), f32(64, 256),
            f32(128, 256), f32(128, 128), f32(128, 128),
            f32(2, 4096, 128), f32(2, 4096, 128), f32(2, 4096, 128),
            bf16(8, 512, 256), bf16(8, 512, 256), bf16(8, 512, 256),
            bf16(512, 8, 256), bf16(512, 8, 256), f32(2, 32, 64, 32), f32(2, 64, 64, 64),
            bf16(512, 8, 256), f32(2, 8, 64, 128),
            f32(256, 512), f32(256, 512), f32(256, 256), f32(128, 256),
            f32(512, 256), f32(512, 256), f32(2, 8, 1024), f32(16, 512),
            bf16(256, 1024), bf16(256, 1024), bf16(1024, 512), bf16(1024, 512),
            bf16(80, 256), bf16(128, 256), bf16(2, 256, 512), bf16(2, 256, 512), bf16(2, 256, 256), bf16(2, 128, 256),
            bf16(2, 512, 256), bf16(2, 512, 256),
            bf16(512, 512), bf16(512, 512), f32(256, 128), f32(2, 128, 256), f32(128, 128), f32(2, 64, 32),
            f32(2, 2, 2, PAIRS, 128), f32(2, 2, 512, 128), f32(2, 2, 512, 128), f32(2, 2, 16, 8, 128), f32(2, 2, 16, 8, 128),
            f32(2, 2, 2, 8, 128), f32(2, 2, 16, 8, 128), f32(2, 2, 2, 512, 128), f32(2, 2, PAIRS, 128),
            f32(256, 128), f32(256, 128), f32(8, 8, 512), f32(8, 8, 512), f32(8, 1024), f32(8, 8, 1024),
            f32(256, 128), f32(256, 128),
            dma((22,)), dma((3,)), dma((8,)), dma((8,)), dma((8,)), dma((8,)), dma((8,)), dma((8,)), dma((8,)),
            dma((4,)), dma((4,)), pltpu.SemaphoreType.REGULAR((3,)),
        ],
        compiler_params=pltpu.CompilerParams(
            collective_id=0, has_side_effects=True, vmem_limit_bytes=60 * 1024 * 1024
        ),
        name="fno_layer",
    )(
        features.reshape(512, 8, 256), cotangent.reshape(512, 8, 256), pointwise_fine, fine, lift_weight,
        pointwise_coarse, coarse, project_weight.T,
        table["tx"], table["ix"], table["ty"], table["zf"], table["zi"], table["ti"], table["txc"], table["tyc"],
        table["zfc"], table["zic"], table["tic"], table["ixc"],
    )
    layer_out, grad_out, gspec = pl.pallas_call(
        finish,
        grid=(4,),
        out_shape=[
            jax.ShapeDtypeStruct((512, 8, 256), BF16),
            jax.ShapeDtypeStruct((512, 8, 256), BF16),
            jax.ShapeDtypeStruct((2, 32, 64, 32), F32),
        ],
        in_specs=[
            pl.BlockSpec((1, 1, PAIRS, 128), lambda i: (i % 2, i // 2, 0, 0)),
            pl.BlockSpec((1, 1, 8, 128), lambda i: (i % 2, 0, 1, 0)),
            pl.BlockSpec((2, 8, 128, 128), lambda i: (0, 0, i, 0)),
            pl.BlockSpec((128, 8, 256), lambda i: (i, 0, 0)),
            pl.BlockSpec((2, 2, 64, 128), lambda i: (0, i, 0, 0)),
            pl.BlockSpec((40, 256), lambda i: (0, 0)),
        ],
        out_specs=[
            pl.BlockSpec((128, 8, 256), lambda i: (i, 0, 0)),
            pl.BlockSpec((128, 8, 256), lambda i: (i, 0, 0)),
            pl.BlockSpec((2, 8, 64, 32), lambda i: (0, i, 0, 0)),
        ],
        scratch_shapes=[f32(PAIRS, 128), f32(2, 1024, 128)],
        compiler_params=pltpu.CompilerParams(vmem_limit_bytes=60 * 1024 * 1024),
        name="finish",
    )(spectrum, spectrum, direct.reshape(2, 8, 512, 128), layer, gspec, table["ix"])
    shape = (32, 16, 8, 256)
    gspec = gspec.reshape(2, 32, 16, 1, 4, 32).transpose(0, 1, 5, 2, 3, 4)
    return layer_out.reshape(shape), grad_out.reshape(shape), gspec


def solution(mesh):
    placed = (
        P(None, "py", "px", None),
        P(None, "py", "px", None),
        P(),
        P(None, None, None, None, "px", "py"),
        P(),
        P(),
        P(None, None, None, None, "px", "py"),
        P(),
    )
    return jax.shard_map(
        body,
        mesh=mesh,
        in_specs=placed,
        out_specs=(
            P(None, "py", "px", None),
            P(None, "py", "px", None),
            P(None, None, None, None, "px", "py"),
        ),
        check_vma=False,
    )
```
